32 devices in a mesh: section: 2 (over x), dp: 4 (over z), mp: 4 (over y, core).
Axes of the slice: x: 2, y: 2, z: 4, core: 2. Of those that a mesh axis runs over, the one named last changes fastest.
Arguments:
- embeddings: bfloat16 [2, 12, 1024, 512], P('section', 'dp', 'mp'), may hold values from -6 to 6
- src_len: int32 [12, 4], P('dp'), may hold values from 1 to 512, 896 in all within a row
- tgt_len: int32 [12, 4], P('dp'), may hold values from 1 to 512, 896 in all within a row
- attn_in: bfloat16 [2, 3, 512, 512], P('section', None, None, 'mp'), may hold values from -0.25 to 0.25
- attn_out: bfloat16 [2, 512, 512], P('section', 'mp'), may hold values from -1 to 1
- ffn_in: bfloat16 [2, 512, 2048], P('section', None, 'mp'), may hold values from -0.25 to 0.25
- ffn_out: bfloat16 [2, 2048, 512], P('section', 'mp'), may hold values from -0.125 to 0.125
- cross_a: bfloat16 [2, 512, 512], P('section', None, 'mp'), may hold values from -0.25 to 0.25
- cross_b: bfloat16 [2, 512, 512], P('section', None, 'mp'), may hold values from -1 to 1
- norm_gain: float32 [2, 2, 512], P('section'), may hold values from 0.5 to 1.5
- norm_bias: float32 [2, 2, 512], P('section'), may hold values from -1.8 to 1.8
- cross_gain: float32 [512], replicated, may hold values from 0.5 to 1.5
- cross_bias: float32 [512], replicated, may hold values from -1.8 to 1.8
- cotangent: bfloat16 [12, 1024, 512], P('dp', 'mp'), may hold values from -6 to 6
Outputs:
- layer_out: bfloat16 [2, 12, 1024, 512], P('section', 'dp', 'mp')
- input_grad: float32 [2, 12, 1024, 512], P('section', 'dp', 'mp')
- grad_attn_in: float32 [2, 3, 512, 512], P('section', None, None, 'mp')
- grad_attn_out: float32 [2, 512, 512], P('section', 'mp')
- grad_ffn_in: float32 [2, 512, 2048], P('section', None, 'mp')
- grad_ffn_out: float32 [2, 2048, 512], P('section', 'mp')
- grad_cross_a: float32 [2, 512, 512], P('section', None, 'mp')
- grad_cross_b: float32 [2, 512, 512], P('section', None, 'mp')
- grad_norm_gain: float32 [2, 2, 512], P('section')
- grad_norm_bias: float32 [2, 2, 512], P('section')
- grad_cross_gain: float32 [512], replicated
- grad_cross_bias: float32 [512], replicated
The draws below stay inside these ranges and needn't reach their ends.
Inputs may be any that keep to these rules, and one draw needn't show every extreme that they name: `src_len`: each row lists the sentences packed into one pack in order; a row sums to 896 and its largest entry is 512; the remaining slots are padding. `tgt_len`: each row lists the sentences packed into one pack in order; a row sums to 896 and its largest entry is 512; target sentence j translates source sentence j of the same pack.
All inputs are finite; a program needn't handle non-finite values.
Results may differ from the reference program's by a relative error of at most 0.035.
Values may be sent and summed in bfloat16 or wider, within the bound.
No kernel may reach another device: no remote copies, remote signals or barrier semaphores. Data moves between devices by JAX's collectives and lax.ppermute only.
A program may use at most 256 MiB of HBM per device.

```python
import math
import jax
import jax.numpy as jnp
import numpy as np
from jax import lax

D = 512
H = 8
FF = 2048
HD = 64
TOK_MB = 1024
SENT_MAX = 512
SENT = 4
PACKS = 12


def block_levels(own_key, extent, cuts, low, high):
    def one(dim, parts):
        draws = jax.random.uniform(jax.random.fold_in(jax.random.fold_in(own_key, 6), dim), (parts,), jnp.float32, low / len(cuts), high / len(cuts))
        return jnp.repeat(jnp.exp(draws), extent[dim] // parts).reshape((-1,) + (1,) * (len(extent) - dim - 1))

    level = one(*cuts[0])
    for cut in cuts[1:]:
        level = level * one(*cut)
    return level


def split_up(amount, total, reach, skew):
    loads = [(1 << 20) // math.isqrt(grade ** skew) + 1 for grade in range(2, amount + 1)]
    surplus, holding = total - reach - (amount - 1), [1] * (amount - 1)
    while surplus > 0:
        candidates = [i for i in range(amount - 1) if holding[i] < reach]
        whole, remaining = sum([loads[i] for i in candidates]), surplus
        for i in candidates:
            extra = min(reach - holding[i], max(1, remaining * loads[i] // whole), surplus)
            holding[i] = holding[i] + extra
            surplus = surplus - extra
    return np.array([reach] + holding)


def ragged_sizes(own_key, number_of, total, reach, skew):
    if number_of == 2:
        one = jax.random.randint(own_key, (), max(1, total - reach), min(reach, total - 1) + 1)
        return jnp.stack([one, total - one])
    sizes = jnp.asarray(split_up(number_of, total, reach, skew), jnp.int32)
    pairs = (number_of - 1) // 2
    donor, sink = sizes[1:1 + 2 * pairs:2], sizes[2:2 + 2 * pairs:2]
    margin = jnp.minimum(donor - 1, reach - sink)
    passed = jax.random.randint(jax.random.fold_in(own_key, 1), (pairs,), 0, 1 << 20) % (margin + 1)
    sizes = sizes.at[1:1 + 2 * pairs:2].set(donor - passed).at[2:2 + 2 * pairs:2].set(sink + passed)
    return sizes[jax.random.permutation(jax.random.fold_in(own_key, 2), number_of)]


def normal_values(rng, shape, spread, reach, cuts=(), kind=jnp.bfloat16):
    result = spread * jax.random.normal(rng, shape, jnp.float32)
    if cuts:
        result = result * block_levels(rng, shape, cuts, -0.22, 0.18)
    return jnp.clip(result, -reach, reach).astype(kind)


def setup_inputs(seed: int = 0) -> dict:
    streams_of = jax.random.split(jax.random.key(seed), 15)
    return {
        "embeddings": normal_values(streams_of[0], (2, PACKS, TOK_MB, D), 1.0, 6.0, ((0, 2), (1, 4), (2, 4))),
        "src_len": jax.vmap(lambda own: ragged_sizes(own, SENT, TOK_MB - TOK_MB // 8, SENT_MAX, 2))(jax.random.split(streams_of[1], PACKS)).reshape((PACKS, SENT)).astype(jnp.int32),
        "tgt_len": jax.vmap(lambda own: ragged_sizes(own, SENT, TOK_MB - TOK_MB // 8, SENT_MAX, 2))(jax.random.split(streams_of[2], PACKS)).reshape((PACKS, SENT)).astype(jnp.int32),
        "attn_in": normal_values(streams_of[3], (2, 3, D, D), D ** -0.5, 0.25, ((0, 2), (3, 4))),
        "attn_out": normal_values(streams_of[4], (2, D, D), (D // 16) ** -0.5, 1.0, ((0, 2), (1, 4))),
        "ffn_in": normal_values(streams_of[5], (2, D, FF), D ** -0.5, 0.25, ((0, 2), (2, 4))),
        "ffn_out": normal_values(streams_of[6], (2, FF, D), FF ** -0.5, 0.125, ((0, 2), (1, 4))),
        "cross_a": normal_values(streams_of[7], (2, D, D), D ** -0.5, 0.25, ((0, 2), (2, 4))),
        "cross_b": normal_values(streams_of[8], (2, D, D), (D // 16) ** -0.5, 1.0, ((0, 2), (2, 4))),
        "norm_gain": jnp.clip(1.0 + 0.1 * jax.random.normal(streams_of[9], (2, 2, D), jnp.float32), 0.5, 1.5),
        "norm_bias": normal_values(streams_of[10], (2, 2, D), 0.3, 1.8, ((0, 2),), jnp.float32),
        "cross_gain": jnp.clip(1.0 + 0.1 * jax.random.normal(streams_of[11], (D,), jnp.float32), 0.5, 1.5),
        "cross_bias": normal_values(streams_of[12], (D,), 0.3, 1.8, (), jnp.float32),
        "cotangent": normal_values(streams_of[13], (PACKS, TOK_MB, D), 1.0, 6.0, ((0, 4), (1, 4))),
    }


EPS = 1e-05
NEG = -1000000000.0

@jax.custom_vjp
def low(v):
    return lax.optimization_barrier(v.astype(jnp.bfloat16)).astype(jnp.float32)

@jax.custom_vjp
def low_back(v):
    return v

def low_keep(v):
    return (low(v), None)

def low_pass(kept, grad):
    return (grad,)

def back_keep(v):
    return (v, None)

def back_low(kept, grad):
    return (low(grad),)
low.defvjp(low_keep, low_pass)
low_back.defvjp(back_keep, back_low)

def segment_ids(lengths, count):
    ends = jnp.cumsum(lengths)
    position = jnp.arange(count, dtype=jnp.int32)
    return lax.optimization_barrier(jnp.sum((position[:, None] >= ends[None, :]).astype(jnp.int32), axis=1))

def matmul_high(left, right):
    return jnp.dot(left, right, precision=lax.Precision.HIGHEST)

def layer_norm(total, gain, shift_bias):
    center = lax.optimization_barrier(jnp.mean(total, axis=-1, keepdims=True))
    centred = total - center
    inverse = lax.rsqrt(lax.optimization_barrier(jnp.mean(centred * centred, axis=-1, keepdims=True)) + EPS)
    scaled = centred * inverse
    return scaled * gain + shift_bias

def attention(query, keys, values, query_seg, key_seg, causal):
    count = query.shape[0]
    query_heads = query.reshape(count, H, HD)
    key_heads = keys.reshape(keys.shape[0], H, HD)
    value_heads = values.reshape(values.shape[0], H, HD)
    scores = low_back(jnp.einsum('qhd,khd->hqk', query_heads, key_heads, precision=lax.Precision.HIGHEST) * HD ** (-0.5))
    position = jnp.arange(count, dtype=jnp.int32)
    allowed = query_seg[:, None] == key_seg[None, :]
    if causal:
        allowed = allowed & (position[None, :] <= position[:, None])
    scores = jnp.where(allowed[None], scores, NEG)
    top_score = lax.optimization_barrier(jnp.max(scores, axis=-1, keepdims=True))
    raised = jnp.exp(scores - top_score)
    weights = low(raised / lax.optimization_barrier(jnp.sum(raised, axis=-1, keepdims=True)))
    mixed = jnp.einsum('hqk,khd->qhd', weights, value_heads, precision=lax.Precision.HIGHEST)
    return low(low_back(mixed.reshape(count, H * HD)))

def self_part(rows, projections, out_proj, seg_ids, causal):
    query = low(low_back(matmul_high(rows, projections[0])))
    keys = low(low_back(matmul_high(rows, projections[1])))
    values = low(low_back(matmul_high(rows, projections[2])))
    return low_back(matmul_high(attention(query, keys, values, seg_ids, seg_ids, causal), out_proj))

def ffn_part(normed, up_proj, down_proj):
    hidden_pre = low_back(matmul_high(low(normed), up_proj))
    return low_back(matmul_high(low(jax.nn.silu(hidden_pre)), down_proj))

def reference(embeddings, src_len, tgt_len, attn_in, attn_out, ffn_in, ffn_out, cross_a, cross_b, norm_gain, norm_bias, cross_gain, cross_bias, cotangent):
    source_seg = jax.vmap(lambda lengths: segment_ids(lengths, TOK_MB))(src_len)
    target_seg = jax.vmap(lambda lengths: segment_ids(lengths, TOK_MB))(tgt_len)
    live = (target_seg < SENT).astype(jnp.float32)
    floats = tuple((item.astype(jnp.float32) for item in (embeddings, attn_in, attn_out, ffn_in, ffn_out, cross_a, cross_b, norm_gain, norm_bias, cross_gain, cross_bias)))

    def forward(embed_all, attn_all, out_all, up_all, down_all, first_all, second_all, gain_all, bias_all, cross_scale, cross_shift):

        def pair(items):
            source_rows, target_rows, source_ids, target_ids = items
            enc_first = layer_norm(source_rows + self_part(source_rows, attn_all[0], out_all[0], source_ids, False), gain_all[0, 0], bias_all[0, 0])
            encoded = layer_norm(enc_first + ffn_part(enc_first, up_all[0], down_all[0]), gain_all[0, 1], bias_all[0, 1])
            memory = low(encoded)
            mem_keys = low(low_back(matmul_high(memory, first_all[0])))
            mem_values = low(low_back(matmul_high(memory, second_all[0])))
            dec_first = layer_norm(target_rows + self_part(target_rows, attn_all[1], out_all[1], target_ids, True), gain_all[1, 0], bias_all[1, 0])
            cross_query = low(low_back(matmul_high(low(dec_first), first_all[1])))
            cross_mix = attention(cross_query, mem_keys, mem_values, target_ids, source_ids, False)
            dec_second = layer_norm(dec_first + low_back(matmul_high(cross_mix, second_all[1].T)), cross_scale, cross_shift)
            decoded = layer_norm(dec_second + ffn_part(dec_second, up_all[1], down_all[1]), gain_all[1, 1], bias_all[1, 1])
            return (encoded, decoded)
        return lax.map(jax.checkpoint(pair), (embed_all[0], embed_all[1], source_seg, target_seg))
    (encoded, decoded), pull = jax.vjp(forward, *floats)
    grads = pull((jnp.zeros_like(encoded), cotangent.astype(jnp.float32) * live[:, :, None]))
    layer_out = jnp.stack([encoded, decoded]).astype(jnp.bfloat16)
    return (layer_out, grads[0], grads[1], grads[2], grads[3], grads[4], grads[5], grads[6], grads[7], grads[8], grads[9], grads[10])
```

```python
import functools

import jax
import jax.numpy as jnp
from jax import lax
from jax.experimental import pallas as pl
from jax.experimental.pallas import tpu as pltpu
from jax.sharding import PartitionSpec as P

HD = 64
EPS = 1e-05
NEG = -1000000000.0
F32 = jnp.float32
BF16 = jnp.bfloat16
QC = 256


def nn(left, right):
    return lax.dot_general(left, right, (((1,), (0,)), ((), ())), preferred_element_type=F32)


def nt(left, right):
    return lax.dot_general(left, right, (((1,), (1,)), ((), ())), preferred_element_type=F32)


def tn(left, right):
    return lax.dot_general(left, right, (((0,), (0,)), ((), ())), preferred_element_type=F32)


def hop(value, distance):
    count = lax.axis_size("mp")
    return lax.ppermute(value, "mp", [(i, i ^ distance) for i in range(count)])


def gather(own):
    far = hop(own, 2)
    return own, hop(own, 1), far, hop(far, 1)


def exchange(blocks):
    return [blocks[0]] + [hop(blocks[r], r) for r in range(1, 4)]


def reduce_rows(even, odd):
    near = hop(odd, 1)
    far = hop((even[1].astype(F32) + near[1].astype(F32)).astype(BF16), 2)
    return even[0].astype(F32) + near[0].astype(F32) + far.astype(F32)


def section_send(value, source):
    return lax.ppermute(value, "section", [(source, 1 - source)])


def chain_sum(values):
    count = lax.axis_size("dp")
    if count == 1:
        return values
    if count % 2:
        return lax.psum(values, "dp")
    index = lax.axis_index("dp")
    for i in range(count // 2 - 1):
        moved = lax.ppermute(values, "dp", [(i, i + 1), (count - 1 - i, count - 2 - i)])
        values = (values.astype(F32) + moved.astype(F32)).astype(BF16)
    middle = count // 2
    moved = lax.ppermute(values, "dp", [(middle - 1, middle), (middle, middle - 1)])
    values = (values.astype(F32) + moved.astype(F32)).astype(BF16)
    for i in reversed(range(count // 2 - 1)):
        moved = lax.ppermute(values, "dp", [(i + 1, i), (count - 2 - i, count - 1 - i)])
        values = jnp.where((index == i) | (index == count - 1 - i), moved, values)
    return values


def tree_sum(value):
    value = value + hop(value, 1)
    value = value + hop(value, 2)
    count = lax.axis_size("dp")
    if count & (count - 1):
        return lax.psum(value, "dp")
    step = 1
    while step < count:
        value = value + lax.ppermute(value, "dp", [(i, i ^ step) for i in range(count)])
        step *= 2
    return value


def pack_layout(lengths, pack, sentences):
    ends, start, largest, top, end = [], 0, 0, 0, 0
    for j in range(sentences):
        size = lengths[pack, j]
        better = size > top
        start = jnp.where(better, end, start)
        largest = jnp.where(better, j, largest)
        top = jnp.where(better, size, top)
        end = end + size
        ends.append(end)
    return ends, start, largest


def segment_ids(ends, shift, first, shape, dim, total):
    at = lax.broadcasted_iota(jnp.int32, shape, dim) + (first + shift)
    at = jnp.where(at >= total, at - total, at)
    return sum(jnp.where(at >= end, 1, 0) for end in ends)


def center_rows(total):
    center = jnp.mean(total, axis=-1, keepdims=True)
    centred = total - center
    inverse = lax.rsqrt(jnp.mean(centred * centred, axis=-1, keepdims=True) + EPS)
    return centred * inverse, inverse


def norm_back(grad, scaled, inverse, gain):
    inner = grad * gain
    first = jnp.mean(inner, axis=-1, keepdims=True)
    second = jnp.mean(inner * scaled, axis=-1, keepdims=True)
    return (
        inverse * (inner - first - scaled * second),
        jnp.sum(grad * scaled, axis=0, keepdims=True),
        jnp.sum(grad, axis=0, keepdims=True),
    )


def place(roll, slot, me, block, rows, value):
    count = roll.shape[1] // 2
    start = pl.multiple_of((me ^ block) * rows, rows)
    roll[slot, pl.ds(start, rows), :] = value
    roll[slot, pl.ds(start + count, rows), :] = value


def rolled(roll, slot, shift, half, size):
    return roll[slot, pl.ds(shift + half * size, size), :]


def unroll_into(roll, slot, shift, source, half):
    roll[slot, pl.ds(shift + half, half), :] = source[0:half, :]
    roll[slot, pl.ds(shift + 2 * half, half), :] = source[half : 2 * half, :]
    roll[slot, pl.ds(shift, half), :] = source[half : 2 * half, :]


def unrolled(roll, slot, me, block, rows, half):
    return roll[slot, pl.ds(pl.multiple_of(half + (me ^ block) * rows, rows), rows), :]


def head_masks(width):
    lane = lax.broadcasted_iota(jnp.int32, (1, width), 1)
    return [
        jnp.where((lane >= h * HD) & (lane < (h + 1) * HD), 1.0, 0.0).astype(BF16)
        for h in range(width // HD)
    ]


def attend_chunk(keys, values, query, bias, masks):
    tops, sums, outs = [], [], []
    for h, mask in enumerate(masks):
        scores = nt(keys, query * mask) + bias
        top = jnp.max(scores, axis=0, keepdims=True)
        raised = jnp.exp(scores - top)
        total = jnp.sum(raised, axis=0, keepdims=True)
        mixed = tn(values, raised.astype(BF16))
        outs.append(mixed[h * HD : (h + 1) * HD, :] / total)
        sums.append(top + jnp.log(total))
    return jnp.concatenate(outs, axis=0).T, sums


def attend_back_chunk(keys, values, query, grad, out, lse, bias, masks):
    folded = (grad.astype(F32) * out).T
    grad_query = []
    probs, grads = [], []
    for h, mask in enumerate(masks):
        scores = nt(keys, query * mask) + bias
        prob = jnp.exp(scores - lse[h])
        grad_prob = nt(values, grad * mask)
        inner = jnp.sum(folded[h * HD : (h + 1) * HD, :], axis=0, keepdims=True)
        grad_score = (prob * (grad_prob - inner)).astype(BF16)
        probs.append(prob.astype(BF16))
        grads.append(grad_score)
        grad_query.append(tn(keys, grad_score)[h * HD : (h + 1) * HD, :])
    grad_keys = sum(nn(g, query * m) for g, m in zip(grads, masks))
    grad_values = sum(nn(p, grad * m) for p, m in zip(probs, masks))
    return jnp.concatenate(grad_query, axis=0).T * (HD ** (-0.5)), grad_keys, grad_values


def self_bias(is_dec, ends, shift, bias, half):
    key = lax.broadcasted_iota(jnp.int32, (half, QC), 0)
    key_ids = segment_ids(ends, shift, half, (half, 1), 0, 2 * half)
    for c in range(half // QC):
        cols = slice(c * QC, (c + 1) * QC)
        query = lax.broadcasted_iota(jnp.int32, (half, QC), 1) + c * QC
        query_ids = segment_ids(ends, shift, half + c * QC, (1, QC), 1, 2 * half)
        allowed = (key <= query) | (is_dec == 0)
        bias[0, :, cols] = jnp.where(allowed, 0.0, NEG)
        bias[1, :, cols] = jnp.where(allowed & (key_ids == query_ids), 0.0, NEG)


def cross_bias(source, target, own_keys, bias, half):
    for kind in range(2):
        query_ids = segment_ids(target[0], target[1], kind * half, (1, half), 1, 2 * half)
        for part in range(kind + 1):
            first = part * half if kind else own_keys
            key_ids = segment_ids(source[0], source[1], first, (half, 1), 0, 2 * half)
            rows = slice(part * half, (part + 1) * half)
            bias[kind, rows, :] = jnp.where(key_ids == query_ids, 0.0, NEG)


def place_of():
    return lax.axis_index("section"), lax.axis_index("mp")


def own_layout(source, target, is_dec, pack):
    sentences = source.shape[1]
    first, second = pack_layout(source, pack, sentences), pack_layout(target, pack, sentences)
    return [jnp.where(is_dec == 1, b, a) for a, b in zip(first[0], second[0])], jnp.where(
        is_dec == 1, second[1], first[1]
    )


def self_forward(
    pack, source, target, x0, x1, x2, x3, weights,
    o0, o1, o2, o3, query, keys, values, lse, outs, roll, bias,
):
    is_dec, me = place_of()
    ends, shift = own_layout(source, target, is_dec, pack)
    rows = x0.shape[1]
    half = 2 * rows
    for block, x in enumerate((x0, x1, x2, x3)):
        for slot in range(3):
            value = nn(x[pack], weights[slot])
            if slot == 0:
                value = value.astype(BF16).astype(F32) * (HD ** (-0.5))
            place(roll, slot, me, block, rows, value)
    for h in range(2):
        part = slice(h * half, (h + 1) * half)
        query[part, :] = rolled(roll, 0, shift, h, half).astype(BF16)
        keys[part, :] = rolled(roll, 1, shift, h, half).astype(BF16)
        values[part, :] = rolled(roll, 2, shift, h, half).astype(BF16)
    self_bias(is_dec, ends, shift, bias, half)
    masks = head_masks(query.shape[1])
    chunks = half // QC

    def step(i, carry):
        h, c = i // chunks, i % chunks
        at = pl.multiple_of(i * QC, QC)
        part = pl.ds(pl.multiple_of(h * half, half), half)
        out, sums = attend_chunk(
            keys[part, :],
            values[part, :],
            query[pl.ds(at, QC), :],
            bias[h, :, pl.ds(pl.multiple_of(c * QC, QC), QC)],
            masks,
        )
        outs[pl.ds(at, QC), :] = out
        for k, row in enumerate(sums):
            lse[k : k + 1, pl.ds(at, QC)] = row
        return carry

    lax.fori_loop(0, 2 * chunks, step, 0)
    unroll_into(roll, 0, shift, outs, half)
    for block, o in enumerate((o0, o1, o2, o3)):
        o[...] = unrolled(roll, 0, me, block, rows, half).astype(BF16)


def self_backward(
    pack, source, target, g0, g1, g2, g3, query, keys, values, lse, outs, x0, x1, x2, x3, weights, *rest,
):
    total = rest[0] if pack else None
    even, odd, new_total, roll, bias, grads, grad_out = rest[1:] if pack else rest
    is_dec, me = place_of()
    ends, shift = own_layout(source, target, is_dec, pack)
    rows = x0.shape[1]
    half = 2 * rows
    for block, g in enumerate((g0, g1, g2, g3)):
        place(roll, 0, me, block, rows, g[...].astype(F32))
    for h in range(2):
        grad_out[h * half : (h + 1) * half, :] = rolled(roll, 0, shift, h, half).astype(BF16)
    self_bias(is_dec, ends, shift, bias, half)
    masks = head_masks(query.shape[1])
    chunks = half // QC
    grads[1] = jnp.zeros(grads.shape[1:], F32)
    grads[2] = jnp.zeros(grads.shape[1:], F32)

    def step(i, carry):
        h, c = i // chunks, i % chunks
        at = pl.ds(pl.multiple_of(i * QC, QC), QC)
        part = pl.ds(pl.multiple_of(h * half, half), half)
        dq, dk, dv = attend_back_chunk(
            keys[part, :],
            values[part, :],
            query[at, :],
            grad_out[at, :],
            outs[at, :],
            [lse[k : k + 1, at] for k in range(len(masks))],
            bias[h, :, pl.ds(pl.multiple_of(c * QC, QC), QC)],
            masks,
        )
        grads[0, at, :] = dq
        grads[1, part, :] += dk
        grads[2, part, :] += dv
        return carry

    lax.fori_loop(0, 2 * chunks, step, 0)
    for slot in range(3):
        unroll_into(roll, slot, shift, grads.at[slot], half)
    for block, x in enumerate((x0, x1, x2, x3)):
        parts = [
            unrolled(roll, slot, me, block, rows, half).astype(BF16) for slot in range(3)
        ]
        sums = odd if block & 1 else even
        sums[block >> 1] = sum(nt(parts[slot], weights[slot]) for slot in range(3)).astype(BF16)
        for slot in range(3):
            grad = tn(x[pack], parts[slot])
            base = total if block == 0 else new_total
            new_total[slot] = grad if base is None else base[slot] + grad


def cross_forward(
    pack, source, target, q0, q1, q2, q3, e0, e1, e2, e3, weights,
    o0, o1, o2, o3, query, keys, values, lse, outs, roll, bias,
):
    is_dec, me = place_of()

    @pl.when(is_dec == 1)
    def _():
        sentences = source.shape[1]
        source_ends, source_shift, source_big = pack_layout(source, pack, sentences)
        ends, shift, big = pack_layout(target, pack, sentences)
        rows = q0.shape[0]
        half = 2 * rows
        own_keys = pl.multiple_of(jnp.where(source_big == big, 0, half), half)
        for block, (q, e) in enumerate(zip((q0, q1, q2, q3), (e0, e1, e2, e3))):
            place(roll, 0, me, block, rows, q[...].astype(F32) * (HD ** (-0.5)))
            place(roll, 1, me, block, rows, nn(e[...], weights[0]))
            place(roll, 2, me, block, rows, nn(e[...], weights[1]))
        for h in range(2):
            part = slice(h * half, (h + 1) * half)
            query[part, :] = rolled(roll, 0, shift, h, half).astype(BF16)
            keys[part, :] = rolled(roll, 1, source_shift, h, half).astype(BF16)
            values[part, :] = rolled(roll, 2, source_shift, h, half).astype(BF16)
        cross_bias((source_ends, source_shift), (ends, shift), own_keys, bias, half)
        masks = head_masks(query.shape[1])

        def run(i, kind, key_rows):
            at = pl.multiple_of(kind * half + i * QC, QC)
            out, sums = attend_chunk(
                keys[key_rows, :],
                values[key_rows, :],
                query[pl.ds(at, QC), :],
                bias[kind, 0 : key_rows.size, pl.ds(pl.multiple_of(i * QC, QC), QC)],
                masks,
            )
            outs[pl.ds(at, QC), :] = out
            for k, row in enumerate(sums):
                lse[k : k + 1, pl.ds(at, QC)] = row

        def step(i, carry):
            run(i, 0, pl.ds(own_keys, half))
            run(i, 1, pl.ds(0, 2 * half))
            return carry

        lax.fori_loop(0, half // QC, step, 0)
        unroll_into(roll, 0, shift, outs, half)
        for block, o in enumerate((o0, o1, o2, o3)):
            o[...] = unrolled(roll, 0, me, block, rows, half).astype(BF16)


def cross_backward(
    pack, source, target, g0, g1, g2, g3, query, keys, values, lse, outs, e0, e1, e2, e3, weights, *rest,
):
    total = rest[0] if pack else None
    c0, c1, c2, c3, even, odd, new_total, roll, bias, grads, grad_out = rest[1:] if pack else rest
    is_dec, me = place_of()

    @pl.when(is_dec == 1)
    def _():
        sentences = source.shape[1]
        source_ends, source_shift, source_big = pack_layout(source, pack, sentences)
        ends, shift, big = pack_layout(target, pack, sentences)
        rows = g0.shape[0]
        half = 2 * rows
        own_keys = pl.multiple_of(jnp.where(source_big == big, 0, half), half)
        for block, g in enumerate((g0, g1, g2, g3)):
            place(roll, 0, me, block, rows, g[...].astype(F32))
        for h in range(2):
            grad_out[h * half : (h + 1) * half, :] = rolled(roll, 0, shift, h, half).astype(BF16)
        cross_bias((source_ends, source_shift), (ends, shift), own_keys, bias, half)
        masks = head_masks(query.shape[1])
        grads[1] = jnp.zeros(grads.shape[1:], F32)
        grads[2] = jnp.zeros(grads.shape[1:], F32)

        def run(i, kind, key_rows):
            at = pl.ds(pl.multiple_of(kind * half + i * QC, QC), QC)
            dq, dk, dv = attend_back_chunk(
                keys[key_rows, :],
                values[key_rows, :],
                query[at, :],
                grad_out[at, :],
                outs[at, :],
                [lse[k : k + 1, at] for k in range(len(masks))],
                bias[kind, 0 : key_rows.size, pl.ds(pl.multiple_of(i * QC, QC), QC)],
                masks,
            )
            grads[0, at, :] = dq
            grads[1, key_rows, :] += dk
            grads[2, key_rows, :] += dv

        def step(i, carry):
            run(i, 0, pl.ds(own_keys, half))
            run(i, 1, pl.ds(0, 2 * half))
            return carry

        lax.fori_loop(0, half // QC, step, 0)
        unroll_into(roll, 0, shift, grads.at[0], half)
        unroll_into(roll, 1, source_shift, grads.at[1], half)
        unroll_into(roll, 2, source_shift, grads.at[2], half)
        for block, (c, e) in enumerate(zip((c0, c1, c2, c3), (e0, e1, e2, e3))):
            parts = [
                unrolled(roll, slot, me, block, rows, half).astype(BF16) for slot in range(3)
            ]
            c[...] = parts[0]
            sums = odd if block & 1 else even
            sums[block >> 1] = (nt(parts[1], weights[0]) + nt(parts[2], weights[1])).astype(BF16)
            for slot in range(2):
                grad = tn(e[...], parts[slot + 1])
                base = total if block == 0 else new_total
                new_total[slot] = grad if base is None else base[slot] + grad


def silu_parts(hidden):
    gate = 1.0 / (1.0 + jnp.exp(-hidden))
    return hidden * gate, gate


def split_weights(stacked):
    width = stacked.shape[0] - 2 * stacked.shape[1]
    inner = (stacked.shape[0] - width) // 2
    return pl.ds(0, width), pl.ds(width, inner), pl.ds(width + inner, inner)


def ffn_forward(normed, shares, out):
    _, up, down = split_weights(shares[0])
    for k, share in enumerate(shares):
        hidden = nn(normed, share[up, :])
        part = nn(silu_parts(hidden)[0].astype(BF16), share[down, :])
        out[...] = part if k == 0 else out[...] + part


def ffn_backward(normed, grad, shares, kept, grad_kept, out):
    _, up, down = split_weights(shares[0])
    for k, share in enumerate(shares):
        hidden = nn(normed, share[up, :])
        value, gate = silu_parts(hidden)
        kept[k] = value.astype(BF16)
        slope = gate * (1.0 + hidden * (1.0 - gate))
        grad_pre = (nt(grad, share[down, :]) * slope).astype(BF16)
        grad_kept[k] = grad_pre
        part = nt(grad_pre, share[up, :])
        out[...] = part if k == 0 else out[...] + part


def after_self(
    pack, m0, m1, m2, m3, x, w0, w1, w2, w3, k0, k1, k2, k3, gains, biases,
    scaled, inverse, low, encoded, scaled_two, inverse_two, c0, c1, c2, c3, work,
):
    is_dec, _ = place_of()
    shares = (w0, w1, w2, w3)
    rows = split_weights(w0)[0]
    total = x[pack].astype(F32)
    for mixed, share in zip((m0, m1, m2, m3), shares):
        total = total + nn(mixed[...], share[rows, :])
    first_scaled, first_inverse = center_rows(total)
    scaled[...] = first_scaled
    inverse[...] = first_inverse
    first = first_scaled * gains[0:1, :] + biases[0:1, :]
    low[...] = first.astype(BF16)

    @pl.when(is_dec == 1)
    def _():
        for c, share in zip((c0, c1, c2, c3), (k0, k1, k2, k3)):
            c[...] = nn(low[...], share[0]).astype(BF16)

    @pl.when(is_dec == 0)
    def _():
        ffn_forward(low[...], shares, work)
        again = scaled[...] * gains[0:1, :] + biases[0:1, :]
        second_scaled, second_inverse = center_rows(again + work[...])
        scaled_two[...] = second_scaled
        inverse_two[...] = second_inverse
        encoded[...] = (second_scaled * gains[1:2, :] + biases[1:2, :]).astype(BF16)


def after_cross(
    pack, target, m0, m1, m2, m3, scaled, w0, w1, w2, w3, k0, k1, k2, k3,
    gains, biases, cross_gain, cross_shift, cotangent,
    decoded, low, grad_low, hidden, grad_hidden, out_low, g0, g1, g2, g3, grad_two, norms, work, kept,
):
    is_dec, me = place_of()

    @pl.when(is_dec == 1)
    def _():
        shares = (w0, w1, w2, w3)
        rows = scaled.shape[0]
        total = scaled[...] * gains[0:1, :] + biases[0:1, :]
        for mixed, share in zip((m0, m1, m2, m3), (k0, k1, k2, k3)):
            total = total + nt(mixed[...], share[1])
        second_scaled, second_inverse = center_rows(total)
        kept[...] = second_scaled
        low[...] = (second_scaled * cross_gain[...] + cross_shift[...]).astype(BF16)
        ffn_forward(low[...], shares, work)
        second = kept[...] * cross_gain[...] + cross_shift[...]
        third_scaled, third_inverse = center_rows(second + work[...])
        decoded[...] = (third_scaled * gains[1:2, :] + biases[1:2, :]).astype(BF16)
        at = lax.broadcasted_iota(jnp.int32, (rows, 1), 0) + me * rows
        end = pack_layout(target, pack, target.shape[1])[0][-1]
        grad = jnp.where(at < end, cotangent[pack].astype(F32), 0.0)
        grad_third, gain_two, bias_two = norm_back(grad, third_scaled, third_inverse, gains[1:2, :])
        grad_low[...] = grad_third.astype(BF16)
        grad_two[...] = grad_third
        ffn_backward(low[...], grad_low[...], shares, hidden, grad_hidden, work)
        grad_second, cross_gain_grad, cross_bias_grad = norm_back(
            grad_two[...] + work[...], kept[...], second_inverse, cross_gain[...]
        )
        grad_two[...] = grad_second
        out_low[...] = grad_second.astype(BF16)
        for g, share in zip((g0, g1, g2, g3), (k0, k1, k2, k3)):
            g[...] = nn(out_low[...], share[1]).astype(BF16)
        norms[...] = jnp.zeros(norms.shape, F32)
        norms[1:2, :] = gain_two
        norms[3:4, :] = bias_two
        norms[4:5, :] = cross_gain_grad
        norms[5:6, :] = cross_bias_grad


def before_self(
    pack, scaled, inverse, low, gains, w0, w1, w2, w3, k0, k1, k2, k3, grad_encoded, scaled_two, inverse_two,
    c0, c1, c2, c3, grad_two, norms_in,
    grad_rows, out_low, g0, g1, g2, g3, grad_low, hidden, grad_hidden, norms, work,
):
    is_dec, _ = place_of()
    shares = (w0, w1, w2, w3)
    rows = split_weights(w0)[0]

    @pl.when(is_dec == 0)
    def _():
        grad_sum, gain_two, bias_two = norm_back(
            grad_encoded[...].astype(F32), scaled_two[...], inverse_two[...], gains[1:2, :]
        )
        grad_low[...] = grad_sum.astype(BF16)
        grad_rows[...] = grad_sum
        ffn_backward(low[...], grad_low[...], shares, hidden, grad_hidden, work)
        work[...] += grad_rows[...]
        norms[...] = jnp.zeros(norms.shape, F32)
        norms[1:2, :] = gain_two
        norms[3:4, :] = bias_two

    @pl.when(is_dec == 1)
    def _():
        total = grad_two[...]
        for grad, share in zip((c0, c1, c2, c3), (k0, k1, k2, k3)):
            total = total + nt(grad[...], share[0])
        work[...] = total
        norms[...] = norms_in[...]

    grad_first, gain_one, bias_one = norm_back(work[...], scaled[...], inverse[...], gains[0:1, :])
    norms[0:1, :] = gain_one
    norms[2:3, :] = bias_one
    grad_rows[...] = grad_first
    out_low[...] = grad_first.astype(BF16)
    for g, share in zip((g0, g1, g2, g3), shares):
        g[...] = nt(out_low[...], share[rows, :]).astype(BF16)


def ffn_grads(packs, *refs):
    is_dec, _ = place_of()
    groups = [refs[i * packs : (i + 1) * packs] for i in range(8)]
    up_even, up_odd, down_even, down_odd = refs[8 * packs :]

    def run(inputs, hiddens, grads, grad_hiddens):
        for k in range(4):
            up, down = (up_odd, down_odd) if k & 1 else (up_even, down_even)
            down[k >> 1] = sum(tn(h[k], g[...]) for h, g in zip(hiddens, grads)).astype(BF16)
            up[k >> 1] = sum(tn(x[...], h[k]) for x, h in zip(inputs, grad_hiddens)).astype(BF16)

    @pl.when(is_dec == 1)
    def _():
        run(*groups[:4])

    @pl.when(is_dec == 0)
    def _():
        run(*groups[4:])


def projection_grads(packs, *refs):
    is_dec, _ = place_of()
    take = lambda n, at: [refs[at + i * n : at + (i + 1) * n] for i in range(packs)]
    mixes, outs = take(4, 0), refs[4 * packs : 5 * packs]
    queries, lows = take(4, 5 * packs), refs[9 * packs : 10 * packs]
    crosses, cross_outs = take(4, 10 * packs), refs[14 * packs : 15 * packs]
    out_even, out_odd, cross_even, cross_odd = refs[15 * packs :]
    for k in range(4):
        target = out_odd if k & 1 else out_even
        target[k >> 1] = sum(tn(m[k][...], g[...]) for m, g in zip(mixes, outs)).astype(BF16)

    @pl.when(is_dec == 1)
    def _():
        for k in range(4):
            target = cross_odd if k & 1 else cross_even
            target[k >> 1, 0] = sum(tn(x[...], q[k][...]) for x, q in zip(lows, queries)).astype(BF16)
            target[k >> 1, 1] = sum(tn(g[...], c[k][...]) for g, c in zip(cross_outs, crosses)).astype(BF16)


def call(kernel, scalars, outs, scratch, micros, *operands):
    space = pl.BlockSpec(memory_space=pltpu.VMEM)
    operands = [pltpu.with_memory_space_constraint(x, pltpu.VMEM) for x in operands]
    return pl.pallas_call(
        kernel,
        out_shape=[pltpu.VMEM(shape, kind) for shape, kind in outs],
        in_specs=[pl.BlockSpec(memory_space=pltpu.SMEM)] * len(scalars) + [space] * len(operands),
        out_specs=[space] * len(outs),
        scratch_shapes=[pltpu.VMEM(shape, kind) for shape, kind in scratch],
        compiler_params=pltpu.CompilerParams(vmem_limit_bytes=24 * 1024 * 1024),
        cost_estimate=pl.CostEstimate(
            flops=int(micros * 1e9), bytes_accessed=1 << 16, transcendentals=0
        ),
    )(*scalars, *operands)


def body(
    embeddings, src_len, tgt_len, attn_in, attn_out, ffn_in, ffn_out, cross_a, cross_b,
    norm_gain, norm_bias, cross_gain, cross_bias_vec, cotangent,
):
    is_dec = lax.axis_index("section") == 1
    x_all = embeddings[0]
    packs, rows, features = x_all.shape
    total_rows = rows * lax.axis_size("mp")
    half = total_rows // 2
    width = attn_in.shape[3]
    hidden = ffn_in.shape[2]
    share_rows = width + 2 * hidden
    gains, biases = norm_gain[0], norm_bias[0]
    cgain, cbias = cross_gain[None, :], cross_bias_vec[None, :]
    lens = (src_len, tgt_len)
    every = range(packs)

    xs = gather(x_all)
    w_self = attn_in[0]
    share = jnp.concatenate([attn_out[0], ffn_in[0], ffn_out[0]], axis=0)
    cross_share = jnp.stack([cross_a[0], cross_b[0]])
    xs, share, cross_share = lax.optimization_barrier((xs, share, cross_share))
    shares = gather(share)
    cross_shares = gather(cross_share)
    memory_weights = section_send(cross_share, 0)

    blocks = [((rows, width), BF16)] * 4
    saved_spec = [((total_rows, width), BF16)] * 3 + [((8, total_rows), F32), ((total_rows, width), F32)]
    roll_spec = ((3, 2 * total_rows, width), F32)
    back_spec = [((3, total_rows, width), F32), ((total_rows, width), BF16)]
    full = (rows, features)
    column = ((rows, 1), F32)
    hid_spec = ((4, rows, hidden), BF16)
    self_scratch = [roll_spec, ((2, half, half), F32)]
    cross_scratch = [roll_spec, ((2, total_rows, half), F32)]
    part = functools.partial

    saved, mixes = [], []
    for p in every:
        out = call(
            part(self_forward, p), lens, blocks + saved_spec, self_scratch, 5.0, *xs, w_self,
        )
        mixes.append(exchange(out[:4]))
        saved.append(out[4:])

    firsts, queries, memories = [], [], []
    for p in every:
        out = call(
            part(after_self, p), (),
            [(full, F32), column, (full, BF16), (full, BF16), (full, F32), column] + blocks,
            [(full, F32)], 4.0,
            *mixes[p], x_all, *shares, *cross_shares, gains, biases,
        )
        firsts.append(out[:6])
        queries.append(exchange(out[6:]))
        memories.append(gather(section_send(out[3], 0)))

    cross_saved, cross_mixes = [], []
    for p in every:
        out = call(
            part(cross_forward, p), lens, blocks + saved_spec, cross_scratch, 6.0,
            *queries[p], *memories[p], memory_weights,
        )
        cross_mixes.append(exchange(out[:4]))
        cross_saved.append(out[4:])

    decs, cross_grads = [], []
    for p in every:
        out = call(
            part(after_cross, p), (tgt_len,),
            [(full, BF16)] * 3 + [hid_spec] * 2 + [(full, BF16)] + blocks + [(full, F32), ((8, features), F32)],
            [(full, F32), (full, F32)], 7.0,
            *cross_mixes[p], firsts[p][0], *shares, *cross_shares, gains, biases, cgain, cbias, cotangent,
        )
        decs.append(out)
        cross_grads.append(exchange(out[6:10]))

    memory_total = ()
    query_grads, encoded_grads = [], []
    for p in every:
        out = call(
            part(cross_backward, p), lens,
            blocks + [((2,) + full, BF16)] * 2 + [((2, features, width), F32)],
            cross_scratch + back_spec, 8.0,
            *cross_grads[p], *cross_saved[p], *memories[p], memory_weights, *memory_total,
        )
        query_grads.append(exchange(out[:4]))
        encoded_grads.append(section_send(reduce_rows(out[4], out[5]).astype(BF16), 1))
        memory_total = (out[6],)
    memory_sent = section_send(memory_total[0].astype(BF16), 1)

    encs, self_grads = [], []
    for p in every:
        out = call(
            part(before_self, p), (),
            [(full, F32), (full, BF16)] + blocks + [(full, BF16), hid_spec, hid_spec, ((8, features), F32)],
            [(full, F32)], 6.0,
            firsts[p][0], firsts[p][1], firsts[p][2], gains, *shares, *cross_shares, encoded_grads[p],
            firsts[p][4], firsts[p][5], *query_grads[p], decs[p][10], decs[p][11],
        )
        encs.append(out)
        self_grads.append(exchange(out[2:6]))

    pair = lambda *tail: [((2,) + tail, BF16)] * 2
    up_even, up_odd, down_even, down_odd = call(
        part(ffn_grads, packs), (), pair(features, hidden) + pair(hidden, features), [], 5.0,
        *[d[1] for d in decs], *[d[3] for d in decs], *[d[2] for d in decs], *[d[4] for d in decs],
        *[f[2] for f in firsts], *[e[7] for e in encs], *[e[6] for e in encs], *[e[8] for e in encs],
    )
    out_even, out_odd, cross_even, cross_odd = call(
        part(projection_grads, packs), (), pair(width, features) + pair(2, features, width), [], 3.0,
        *sum(mixes, []), *[e[1] for e in encs],
        *sum(query_grads, []), *[f[2] for f in firsts],
        *sum(cross_mixes, []), *[d[5] for d in decs],
    )
    down_grad = chain_sum(reduce_rows(down_even, down_odd).astype(BF16))
    up_grad = chain_sum(reduce_rows(up_even, up_odd).astype(BF16))
    out_grad = chain_sum(reduce_rows(out_even, out_odd).astype(BF16))
    cross_own = reduce_rows(cross_even, cross_odd).astype(BF16)
    cross_grad = chain_sum(jnp.where(is_dec, cross_own, memory_sent))
    norms = tree_sum(sum(e[9] for e in encs))
    cross_norms = norms[4:6]
    cross_norms = jnp.where(is_dec, cross_norms, section_send(cross_norms, 1))

    qkv_total = ()
    input_grads = []
    for p in every:
        out = call(
            part(self_backward, p), lens,
            pair(rows, features) + [((3, features, width), F32)], self_scratch + back_spec, 8.0,
            *self_grads[p], *saved[p], *xs, w_self, *qkv_total,
        )
        input_grads.append(encs[p][0] + reduce_rows(out[0], out[1]))
        qkv_total = (out[2],)
    qkv_grad = chain_sum(qkv_total[0].astype(BF16))

    layer_rows = jnp.stack([jnp.where(is_dec, decs[p][0], firsts[p][3]) for p in every])
    wide = lambda value: value.astype(F32)[None]
    return (
        layer_rows[None],
        jnp.stack(input_grads)[None],
        wide(qkv_grad),
        wide(out_grad),
        wide(up_grad),
        wide(down_grad),
        wide(cross_grad[0]),
        wide(cross_grad[1]),
        norms[0:2][None],
        norms[2:4][None],
        cross_norms[0],
        cross_norms[1],
    )


def solution(mesh):
    return jax.shard_map(
        body,
        mesh=mesh,
        in_specs=(
            P("section", "dp", "mp", None),
            P("dp", None),
            P("dp", None),
            P("section", None, None, "mp"),
            P("section", "mp", None),
            P("section", None, "mp"),
            P("section", "mp", None),
            P("section", None, "mp"),
            P("section", None, "mp"),
            P("section", None, None),
            P("section", None, None),
            P(),
            P(),
            P("dp", "mp", None),
        ),
        out_specs=(
            P("section", "dp", "mp", None),
            P("section", "dp", "mp", None),
            P("section", None, None, "mp"),
            P("section", "mp", None),
            P("section", None, "mp"),
            P("section", "mp", None),
            P("section", None, "mp"),
            P("section", None, "mp"),
            P("section", None, None),
            P("section", None, None),
            P(),
            P(),
        ),
        check_vma=False,
    )
```

```python
import functools

import jax
import jax.numpy as jnp
from jax import lax
from jax.experimental import pallas as pl
from jax.experimental.pallas import tpu as pltpu
from jax.sharding import PartitionSpec as P

HD = 64
EPS = 1e-05
NEG = -1000000000.0
F32 = jnp.float32
BF16 = jnp.bfloat16
QC = 256
COST = 2e8
SCOPED = 12 * 1024 * 1024


def nn(left, right):
    return lax.dot_general(left, right, (((1,), (0,)), ((), ())), preferred_element_type=F32)


def nt(left, right):
    return lax.dot_general(left, right, (((1,), (1,)), ((), ())), preferred_element_type=F32)


def tn(left, right):
    return lax.dot_general(left, right, (((0,), (0,)), ((), ())), preferred_element_type=F32)


def hop(value, distance):
    count = lax.axis_size("mp")
    return lax.ppermute(value, "mp", [(i, i ^ distance) for i in range(count)])


def gather(own):
    even = jnp.stack([own, hop(own, 2)])
    return even, hop(even, 1)


def exchange(even, odd, axis=0):
    near = hop(odd, 1)
    pick = lambda pair, k: lax.index_in_dim(pair, k, axis, keepdims=False)
    far = hop(jnp.stack([pick(even, 1), pick(near, 1)], axis=axis), 2)
    return even, near, far


def after(value, *earlier):
    return lax.optimization_barrier((value, earlier))[0]


def reduce_rows(even, odd):
    near = hop(odd, 1)
    far = hop((even[1].astype(F32) + near[1].astype(F32)).astype(BF16), 2)
    return even[0].astype(F32) + near[0].astype(F32) + far.astype(F32)


def section_send(value, source):
    return lax.ppermute(value, "section", [(source, 1 - source)])


def chain_sum(values, earlier):
    count = lax.axis_size("dp")
    if count == 1:
        return values
    if count % 2:
        return lax.psum(values, "dp")
    index = lax.axis_index("dp")
    middle = count // 2
    pairs = [[(i, i + 1), (count - 1 - i, count - 2 - i)] for i in range(middle - 1)]
    for k, step in enumerate(pairs + [[(middle - 1, middle), (middle, middle - 1)]]):
        moved = lax.ppermute(after(values, *earlier) if k == 0 else values, "dp", step)
        if k == 0:
            earlier[:] = [moved]
        values = (values.astype(F32) + moved.astype(F32)).astype(BF16)
    for i in reversed(range(middle - 1)):
        moved = lax.ppermute(values, "dp", [(b, a) for a, b in pairs[i]])
        values = jnp.where((index == i) | (index == count - 1 - i), moved, values)
    return values


def tree_sum(value):
    value = value + hop(value, 1)
    value = value + hop(value, 2)
    count = lax.axis_size("dp")
    if count & (count - 1):
        return lax.psum(value, "dp")
    step = 1
    while step < count:
        value = value + lax.ppermute(value, "dp", [(i, i ^ step) for i in range(count)])
        step *= 2
    return value


def blocks_of(even, odd):
    return even.at[0], odd.at[0], even.at[1], odd.at[1]


def views(even, near, far):
    return even.at[0], near.at[0], far.at[0], far.at[1]


def pack_layout(lengths, pack, sentences):
    ends, start, largest, top, end = [], 0, 0, 0, 0
    for j in range(sentences):
        size = lengths[pack, j]
        better = size > top
        start = jnp.where(better, end, start)
        largest = jnp.where(better, j, largest)
        top = jnp.where(better, size, top)
        end = end + size
        ends.append(end)
    return ends, start, largest


def segment_ids(ends, shift, first, shape, dim, total):
    at = lax.broadcasted_iota(jnp.int32, shape, dim) + (first + shift)
    at = jnp.where(at >= total, at - total, at)
    return sum(jnp.where(at >= end, 1, 0) for end in ends)


def center_rows(total):
    center = jnp.mean(total, axis=-1, keepdims=True)
    centred = total - center
    inverse = lax.rsqrt(jnp.mean(centred * centred, axis=-1, keepdims=True) + EPS)
    return centred * inverse, inverse


def norm_back(grad, scaled, inverse, gain):
    inner = grad * gain
    first = jnp.mean(inner, axis=-1, keepdims=True)
    second = jnp.mean(inner * scaled, axis=-1, keepdims=True)
    return (
        inverse * (inner - first - scaled * second),
        jnp.sum(grad * scaled, axis=0, keepdims=True),
        jnp.sum(grad, axis=0, keepdims=True),
    )


def place(roll, slot, me, block, rows, value):
    count = roll.shape[1] // 2
    start = pl.multiple_of((me ^ block) * rows, rows)
    roll[slot, pl.ds(start, rows), :] = value
    roll[slot, pl.ds(start + count, rows), :] = value


def rolled(roll, slot, shift, half, size):
    return roll[slot, pl.ds(shift + half * size, size), :]


def unroll_into(roll, slot, shift, source, half):
    roll[slot, pl.ds(shift + half, half), :] = source[0:half, :]
    roll[slot, pl.ds(shift + 2 * half, half), :] = source[half : 2 * half, :]
    roll[slot, pl.ds(shift, half), :] = source[half : 2 * half, :]


def unrolled(roll, slot, me, block, rows, half):
    return roll[slot, pl.ds(pl.multiple_of(half + (me ^ block) * rows, rows), rows), :]


def head_masks(width):
    lane = lax.broadcasted_iota(jnp.int32, (1, width), 1)
    return [
        jnp.where((lane >= h * HD) & (lane < (h + 1) * HD), 1.0, 0.0).astype(BF16)
        for h in range(width // HD)
    ]


def attend_chunk(keys, values, query, bias, masks):
    tops, sums, outs = [], [], []
    for h, mask in enumerate(masks):
        scores = nt(keys, query * mask) + bias
        top = jnp.max(scores, axis=0, keepdims=True)
        raised = jnp.exp(scores - top)
        total = jnp.sum(raised, axis=0, keepdims=True)
        mixed = tn(values, raised.astype(BF16))
        outs.append(mixed[h * HD : (h + 1) * HD, :] / total)
        sums.append(top + jnp.log(total))
    return jnp.concatenate(outs, axis=0).T, sums


def attend_back_chunk(keys, values, query, grad, out, lse, bias, masks):
    folded = (grad.astype(F32) * out).T
    grad_query = []
    probs, grads = [], []
    for h, mask in enumerate(masks):
        scores = nt(keys, query * mask) + bias
        prob = jnp.exp(scores - lse[h])
        grad_prob = nt(values, grad * mask)
        inner = jnp.sum(folded[h * HD : (h + 1) * HD, :], axis=0, keepdims=True)
        grad_score = (prob * (grad_prob - inner)).astype(BF16)
        probs.append(prob.astype(BF16))
        grads.append(grad_score)
        grad_query.append(tn(keys, grad_score)[h * HD : (h + 1) * HD, :])
    grad_keys = sum(nn(g, query * m) for g, m in zip(grads, masks))
    grad_values = sum(nn(p, grad * m) for p, m in zip(probs, masks))
    return jnp.concatenate(grad_query, axis=0).T * (HD ** (-0.5)), grad_keys, grad_values


def self_bias(is_dec, ends, shift, bias, h, c, half):
    key = lax.broadcasted_iota(jnp.int32, (half, QC), 0)
    query = lax.broadcasted_iota(jnp.int32, (half, QC), 1) + c * QC
    key_ids = segment_ids(ends, shift, h * half, (half, 1), 0, 2 * half)
    query_ids = segment_ids(ends, shift, h * half + c * QC, (1, QC), 1, 2 * half)
    allowed = ((key <= query) | (is_dec == 0)) & (key_ids == query_ids)
    bias[...] = jnp.where(allowed, 0.0, NEG)


def cross_bias(source, target, first_key, first_query, size, bias, half):
    key_ids = segment_ids(source[0], source[1], first_key, (size, 1), 0, 2 * half)
    query_ids = segment_ids(target[0], target[1], first_query, (1, QC), 1, 2 * half)
    bias[0:size, :] = jnp.where(key_ids == query_ids, 0.0, NEG)


def place_of():
    return lax.axis_index("section"), lax.axis_index("mp")


def own_layout(source, target, is_dec, pack):
    sentences = source.shape[1]
    first, second = pack_layout(source, pack, sentences), pack_layout(target, pack, sentences)
    return [jnp.where(is_dec == 1, b, a) for a, b in zip(first[0], second[0])], jnp.where(
        is_dec == 1, second[1], first[1]
    )


def self_forward(
    pack, source, target, x0, x1, x2, x3, weights,
    out_even, out_odd, query, keys, values, lse, outs, roll, bias,
):
    is_dec, me = place_of()
    ends, shift = own_layout(source, target, is_dec, pack)
    rows = x0.shape[1]
    half = 2 * rows
    for block, x in enumerate((x0, x1, x2, x3)):
        for slot in range(3):
            value = nn(x[pack], weights[slot])
            if slot == 0:
                value = value.astype(BF16).astype(F32) * (HD ** (-0.5))
            place(roll, slot, me, block, rows, value)
    for h in range(2):
        part = slice(h * half, (h + 1) * half)
        query[part, :] = rolled(roll, 0, shift, h, half).astype(BF16)
        keys[part, :] = rolled(roll, 1, shift, h, half).astype(BF16)
        values[part, :] = rolled(roll, 2, shift, h, half).astype(BF16)
    masks = head_masks(query.shape[1])
    chunks = half // QC

    def step(i, carry):
        h, c = i // chunks, i % chunks
        at = pl.multiple_of(i * QC, QC)
        part = pl.ds(pl.multiple_of(h * half, half), half)
        self_bias(is_dec, ends, shift, bias, h, c, half)
        out, sums = attend_chunk(
            keys[part, :],
            values[part, :],
            query[pl.ds(at, QC), :],
            bias[...],
            masks,
        )
        outs[pl.ds(at, QC), :] = out
        for k, row in enumerate(sums):
            lse[k : k + 1, pl.ds(at, QC)] = row
        return carry

    lax.fori_loop(0, 2 * chunks, step, 0)
    unroll_into(roll, 0, shift, outs, half)
    for block, o in enumerate(blocks_of(out_even, out_odd)):
        o[...] = unrolled(roll, 0, me, block, rows, half).astype(BF16)


def self_backward(
    pack, source, target, g0, g1, g2, query, keys, values, lse, outs, x0, x1, x2, x3, weights, *rest,
):
    sum_even, sum_odd, total, roll, bias, grads, grad_out = rest[-7:]
    is_dec, me = place_of()
    ends, shift = own_layout(source, target, is_dec, pack)
    rows = x0.shape[1]
    half = 2 * rows
    for block, g in enumerate(views(g0, g1, g2)):
        place(roll, 0, me, block, rows, g[...].astype(F32))
    for h in range(2):
        grad_out[h * half : (h + 1) * half, :] = rolled(roll, 0, shift, h, half).astype(BF16)
    masks = head_masks(query.shape[1])
    chunks = half // QC
    grads[1] = jnp.zeros(grads.shape[1:], F32)
    grads[2] = jnp.zeros(grads.shape[1:], F32)

    def step(i, carry):
        h, c = i // chunks, i % chunks
        at = pl.ds(pl.multiple_of(i * QC, QC), QC)
        part = pl.ds(pl.multiple_of(h * half, half), half)
        self_bias(is_dec, ends, shift, bias, h, c, half)
        dq, dk, dv = attend_back_chunk(
            keys[part, :],
            values[part, :],
            query[at, :],
            grad_out[at, :],
            outs[at, :],
            [lse[k : k + 1, at] for k in range(len(masks))],
            bias[...],
            masks,
        )
        grads[0, at, :] = dq
        grads[1, part, :] += dk
        grads[2, part, :] += dv
        return carry

    lax.fori_loop(0, 2 * chunks, step, 0)
    for slot in range(3):
        unroll_into(roll, slot, shift, grads.at[slot], half)
    if pack:
        for old, new in zip(rest, (sum_even, sum_odd)):
            new[:, 0:pack] = old[:, 0:pack]
    sums = blocks_of(sum_even.at[:, pack], sum_odd.at[:, pack])
    for block, x in enumerate((x0, x1, x2, x3)):
        parts = [
            unrolled(roll, slot, me, block, rows, half).astype(BF16) for slot in range(3)
        ]
        sums[block][...] = sum(nt(parts[slot], weights[slot]) for slot in range(3)).astype(BF16)
        for slot in range(3):
            grad = tn(x[pack], parts[slot])
            before = rest[2] if block == 0 else total
            total[slot] = grad if pack == 0 and block == 0 else before[slot] + grad


def cross_forward(
    pack, source, target, q0, q1, q2, even, odd, weights,
    out_even, out_odd, query, keys, values, lse, outs, roll, bias,
):
    is_dec, me = place_of()

    @pl.when(is_dec == 1)
    def _():
        sentences = source.shape[1]
        source_ends, source_shift, source_big = pack_layout(source, pack, sentences)
        ends, shift, big = pack_layout(target, pack, sentences)
        rows = even.shape[1]
        half = 2 * rows
        own_keys = pl.multiple_of(jnp.where(source_big == big, 0, half), half)
        source_at, target_at = (source_ends, source_shift), (ends, shift)
        queries = views(q0.at[pack], q1.at[pack], q2.at[pack])
        for block, (q, e) in enumerate(zip(queries, blocks_of(even, odd))):
            place(roll, 0, me, block, rows, q[...].astype(F32) * (HD ** (-0.5)))
            place(roll, 1, me, block, rows, nn(e[...], weights[0]))
            place(roll, 2, me, block, rows, nn(e[...], weights[1]))
        for h in range(2):
            part = slice(h * half, (h + 1) * half)
            query[part, :] = rolled(roll, 0, shift, h, half).astype(BF16)
            keys[part, :] = rolled(roll, 1, source_shift, h, half).astype(BF16)
            values[part, :] = rolled(roll, 2, source_shift, h, half).astype(BF16)
        masks = head_masks(query.shape[1])

        def run(i, kind, key_rows):
            at = pl.multiple_of(kind * half + i * QC, QC)
            cross_bias(source_at, target_at, key_rows.start, at, key_rows.size, bias, half)
            out, sums = attend_chunk(
                keys[key_rows, :],
                values[key_rows, :],
                query[pl.ds(at, QC), :],
                bias[0 : key_rows.size, :],
                masks,
            )
            outs[pl.ds(at, QC), :] = out
            for k, row in enumerate(sums):
                lse[k : k + 1, pl.ds(at, QC)] = row

        def step(i, carry):
            run(i, 0, pl.ds(own_keys, half))
            run(i, 1, pl.ds(0, 2 * half))
            return carry

        lax.fori_loop(0, half // QC, step, 0)
        unroll_into(roll, 0, shift, outs, half)
        for block, o in enumerate(blocks_of(out_even, out_odd)):
            o[...] = unrolled(roll, 0, me, block, rows, half).astype(BF16)


def cross_backward(
    pack, source, target, g0, g1, g2, query, keys, values, lse, outs, even, odd, weights, *rest,
):
    query_even, query_odd, sum_even, sum_odd, total, roll, bias, grads, grad_out = rest[-9:]
    is_dec, me = place_of()

    @pl.when(is_dec == 1)
    def _():
        sentences = source.shape[1]
        source_ends, source_shift, source_big = pack_layout(source, pack, sentences)
        ends, shift, big = pack_layout(target, pack, sentences)
        rows = even.shape[1]
        half = 2 * rows
        own_keys = pl.multiple_of(jnp.where(source_big == big, 0, half), half)
        source_at, target_at = (source_ends, source_shift), (ends, shift)
        for block, g in enumerate(views(g0, g1, g2)):
            place(roll, 0, me, block, rows, g[...].astype(F32))
        for h in range(2):
            grad_out[h * half : (h + 1) * half, :] = rolled(roll, 0, shift, h, half).astype(BF16)
        masks = head_masks(query.shape[1])
        grads[1] = jnp.zeros(grads.shape[1:], F32)
        grads[2] = jnp.zeros(grads.shape[1:], F32)

        def run(i, kind, key_rows):
            at = pl.ds(pl.multiple_of(kind * half + i * QC, QC), QC)
            cross_bias(source_at, target_at, key_rows.start, at.start, key_rows.size, bias, half)
            dq, dk, dv = attend_back_chunk(
                keys[key_rows, :],
                values[key_rows, :],
                query[at, :],
                grad_out[at, :],
                outs[at, :],
                [lse[k : k + 1, at] for k in range(len(masks))],
                bias[0 : key_rows.size, :],
                masks,
            )
            grads[0, at, :] = dq
            grads[1, key_rows, :] += dk
            grads[2, key_rows, :] += dv

        def step(i, carry):
            run(i, 0, pl.ds(own_keys, half))
            run(i, 1, pl.ds(0, 2 * half))
            return carry

        lax.fori_loop(0, half // QC, step, 0)
        unroll_into(roll, 0, shift, grads.at[0], half)
        unroll_into(roll, 1, source_shift, grads.at[1], half)
        unroll_into(roll, 2, source_shift, grads.at[2], half)
        sums = blocks_of(sum_even, sum_odd)
        query_grads = blocks_of(query_even.at[pack], query_odd.at[pack])
        if pack:
            for old, new in zip(rest, (query_even, query_odd)):
                new[0:pack] = old[0:pack]
        for block, e in enumerate(blocks_of(even, odd)):
            parts = [
                unrolled(roll, slot, me, block, rows, half).astype(BF16) for slot in range(3)
            ]
            query_grads[block][...] = parts[0]
            sums[block][...] = (nt(parts[1], weights[0]) + nt(parts[2], weights[1])).astype(BF16)
            for slot in range(2):
                grad = tn(parts[slot + 1], e[...])
                before = rest[2] if block == 0 else total
                total[slot] = grad if pack == 0 and block == 0 else before[slot] + grad


def silu_parts(hidden):
    gate = 1.0 / (1.0 + jnp.exp(-hidden))
    return hidden * gate, gate


def split_weights(stacked):
    width = stacked.shape[0] - 2 * stacked.shape[1]
    inner = (stacked.shape[0] - width) // 2
    return pl.ds(0, width), pl.ds(width, inner), pl.ds(width + inner, inner)


def ffn_forward(normed, shares, out):
    _, up, down = split_weights(shares[0])
    for k, share in enumerate(shares):
        hidden = nn(normed, share[up, :])
        part = nn(silu_parts(hidden)[0].astype(BF16), share[down, :])
        out[...] = part if k == 0 else out[...] + part


def ffn_backward(normed, grad, shares, kept, grad_kept, out):
    _, up, down = split_weights(shares[0])
    for k, share in enumerate(shares):
        hidden = nn(normed, share[up, :])
        value, gate = silu_parts(hidden)
        kept[k] = value.astype(BF16)
        slope = gate * (1.0 + hidden * (1.0 - gate))
        grad_pre = (nt(grad, share[down, :]) * slope).astype(BF16)
        grad_kept[k] = grad_pre
        part = nt(grad_pre, share[up, :])
        out[...] = part if k == 0 else out[...] + part


def after_self(
    pack, m0, m1, m2, x, w0, w1, w2, w3, gains, biases,
    scaled, inverse, low, encoded, scaled_two, inverse_two, work,
):
    is_dec, _ = place_of()
    shares = (w0, w1, w2, w3)
    rows = split_weights(shares[0])[0]
    total = x[pack].astype(F32)
    for mixed, share in zip(views(m0, m1, m2), shares):
        total = total + nn(mixed[...], share[rows, :])
    first_scaled, first_inverse = center_rows(total)
    scaled[...] = first_scaled
    inverse[...] = first_inverse
    first = first_scaled * gains[0:1, :] + biases[0:1, :]
    low[...] = first.astype(BF16)

    @pl.when(is_dec == 0)
    def _():
        ffn_forward(low[...], shares, work)
        again = scaled[...] * gains[0:1, :] + biases[0:1, :]
        second_scaled, second_inverse = center_rows(again + work[...])
        scaled_two[...] = second_scaled
        inverse_two[...] = second_inverse
        encoded[...] = (second_scaled * gains[1:2, :] + biases[1:2, :]).astype(BF16)


def cross_queries(packs, *refs):
    lows, (ka, kb, even, odd) = refs[:packs], refs[packs:]

    @pl.when(place_of()[0] == 1)
    def _():
        for pack, low in enumerate(lows):
            for query, share in zip(blocks_of(even.at[pack], odd.at[pack]), blocks_of(ka, kb)):
                query[...] = nn(low[...], share[0]).astype(BF16)


def after_cross(
    pack, target, m0, m1, m2, scaled, w0, w1, w2, w3, ka, kb,
    gains, biases, cross_gain, cross_shift, cotangent,
    decoded, low, grad_low, hidden, grad_hidden, out_low, even, odd, grad_two, norms, work, kept,
):
    is_dec, me = place_of()

    @pl.when(is_dec == 1)
    def _():
        shares, crosses = (w0, w1, w2, w3), blocks_of(ka, kb)
        rows = scaled.shape[0]
        total = scaled[...] * gains[0:1, :] + biases[0:1, :]
        for mixed, share in zip(views(m0, m1, m2), crosses):
            total = total + nt(mixed[...], share[1])
        second_scaled, second_inverse = center_rows(total)
        kept[...] = second_scaled
        low[...] = (second_scaled * cross_gain[...] + cross_shift[...]).astype(BF16)
        ffn_forward(low[...], shares, work)
        second = kept[...] * cross_gain[...] + cross_shift[...]
        third_scaled, third_inverse = center_rows(second + work[...])
        decoded[...] = (third_scaled * gains[1:2, :] + biases[1:2, :]).astype(BF16)
        at = lax.broadcasted_iota(jnp.int32, (rows, 1), 0) + me * rows
        end = pack_layout(target, pack, target.shape[1])[0][-1]
        grad = jnp.where(at < end, cotangent[pack].astype(F32), 0.0)
        grad_third, gain_two, bias_two = norm_back(grad, third_scaled, third_inverse, gains[1:2, :])
        grad_low[...] = grad_third.astype(BF16)
        grad_two[...] = grad_third
        ffn_backward(low[...], grad_low[...], shares, hidden, grad_hidden, work)
        grad_second, cross_gain_grad, cross_bias_grad = norm_back(
            grad_two[...] + work[...], kept[...], second_inverse, cross_gain[...]
        )
        grad_two[...] = grad_second
        out_low[...] = grad_second.astype(BF16)
        for g, share in zip(blocks_of(even, odd), crosses):
            g[...] = nn(out_low[...], share[1]).astype(BF16)
        norms[...] = jnp.zeros(norms.shape, F32)
        norms[1:2, :] = gain_two
        norms[3:4, :] = bias_two
        norms[4:5, :] = cross_gain_grad
        norms[5:6, :] = cross_bias_grad


def before_self(
    pack, scaled, inverse, low, gains, w0, w1, w2, w3, ka, kb, grad_encoded, scaled_two, inverse_two,
    c0, c1, c2, grad_two, norms_in, in_low_old, grad_low_old, hidden_old, grad_hidden_old,
    grad_rows, out_low, even, odd, norms, in_low, grad_low, hidden, grad_hidden, work,
):
    is_dec, _ = place_of()
    shares = (w0, w1, w2, w3)
    rows = split_weights(shares[0])[0]

    @pl.when(is_dec == 0)
    def _():
        grad_sum, gain_two, bias_two = norm_back(
            grad_encoded[...].astype(F32), scaled_two[...], inverse_two[...], gains[1:2, :]
        )
        in_low[...] = low[...]
        grad_low[...] = grad_sum.astype(BF16)
        grad_rows[...] = grad_sum
        ffn_backward(low[...], grad_low[...], shares, hidden, grad_hidden, work)
        work[...] += grad_rows[...]
        norms[...] = jnp.zeros(norms.shape, F32)
        norms[1:2, :] = gain_two
        norms[3:4, :] = bias_two

    @pl.when(is_dec == 1)
    def _():
        total = grad_two[...]
        for grad, share in zip(views(c0.at[pack], c1.at[pack], c2.at[pack]), blocks_of(ka, kb)):
            total = total + nt(grad[...], share[0])
        work[...] = total
        norms[...] = norms_in[...]
        in_low[...] = in_low_old[...]
        grad_low[...] = grad_low_old[...]
        hidden[...] = hidden_old[...]
        grad_hidden[...] = grad_hidden_old[...]

    grad_first, gain_one, bias_one = norm_back(work[...], scaled[...], inverse[...], gains[0:1, :])
    norms[0:1, :] = gain_one
    norms[2:3, :] = bias_one
    grad_rows[...] = grad_first
    out_low[...] = grad_first.astype(BF16)
    for g, share in zip(blocks_of(even, odd), shares):
        g[...] = nt(out_low[...], share[rows, :]).astype(BF16)


def ffn_grads(packs, *refs):
    inputs, hiddens, grads, grad_hiddens = [refs[i * packs : (i + 1) * packs] for i in range(4)]
    up_even, up_odd, down_even, down_odd = refs[4 * packs :]
    ups, downs = blocks_of(up_even, up_odd), blocks_of(down_even, down_odd)
    for k in range(4):
        downs[k][...] = sum(tn(h[k], g[...]) for h, g in zip(hiddens, grads)).astype(BF16)
        ups[k][...] = sum(tn(x[...], h[k]) for x, h in zip(inputs, grad_hiddens)).astype(BF16)


def projection_grads(packs, *refs):
    is_dec, _ = place_of()
    mixes = [views(*refs[3 * i : 3 * i + 3]) for i in range(packs)]
    refs = refs[3 * packs :]
    crosses = [views(*refs[3 * i : 3 * i + 3]) for i in range(packs)]
    refs = refs[3 * packs :]
    queries = [views(*[c.at[i] for c in refs[:3]]) for i in range(packs)]
    outs, lows, cross_outs = [refs[3 + i * packs : 3 + (i + 1) * packs] for i in range(3)]
    targets = blocks_of(*refs[3 + 3 * packs :])
    for k in range(4):
        targets[k][0] = sum(tn(m[k][...], g[...]) for m, g in zip(mixes, outs)).astype(BF16)

    @pl.when(is_dec == 1)
    def _():
        for k in range(4):
            targets[k][1] = sum(tn(q[k][...], x[...]) for x, q in zip(lows, queries)).astype(BF16)
            targets[k][2] = sum(tn(c[k][...], g[...]) for g, c in zip(cross_outs, crosses)).astype(BF16)


def call(clock, kernel, scalars, outs, scratch, micros, *operands, aliases=()):
    space = pl.BlockSpec(memory_space=pltpu.VMEM)
    operands = after(operands, *clock)
    operands = [pltpu.with_memory_space_constraint(x, pltpu.VMEM) for x in operands]
    results = pl.pallas_call(
        kernel,
        out_shape=[pltpu.VMEM(shape, kind) for shape, kind in outs],
        in_specs=[pl.BlockSpec(memory_space=pltpu.SMEM)] * len(scalars) + [space] * len(operands),
        out_specs=[space] * len(outs),
        scratch_shapes=[pltpu.VMEM(shape, kind) for shape, kind in scratch],
        input_output_aliases={len(scalars) + len(operands) + a: b for a, b in aliases},
        compiler_params=pltpu.CompilerParams(vmem_limit_bytes=SCOPED),
        cost_estimate=pl.CostEstimate(
            flops=int(micros * COST), bytes_accessed=1, transcendentals=0
        ),
    )(*scalars, *operands)
    clock[:] = [results[0]]
    return results


def body(
    embeddings, src_len, tgt_len, attn_in, attn_out, ffn_in, ffn_out, cross_a, cross_b,
    norm_gain, norm_bias, cross_gain, cross_bias_vec, cotangent,
):
    is_dec = lax.axis_index("section") == 1
    x_all = embeddings[0]
    packs, rows, features = x_all.shape
    total_rows = rows * lax.axis_size("mp")
    half = total_rows // 2
    width = attn_in.shape[3]
    hidden = ffn_in.shape[2]
    gains, biases = norm_gain[0], norm_bias[0]
    cgain, cbias = cross_gain[None, :], cross_bias_vec[None, :]
    lens = (src_len, tgt_len)
    every = range(packs)
    w_self = attn_in[0]
    share = jnp.concatenate([attn_out[0], ffn_in[0], ffn_out[0]], axis=0)
    cross_share = jnp.stack([cross_a[0], cross_b[0]])

    clock = []
    x_far = hop(x_all, 2)
    xs = (x_all, hop(x_all, 1), x_far, hop(x_far, 1))
    share_far = hop(after(share, x_far), 2)
    share_near = hop(after(share, xs[3]), 1)

    pair = lambda *tail: [((2,) + tail, BF16)] * 2
    saved_spec = [((total_rows, width), BF16)] * 3 + [((8, total_rows), F32), ((total_rows, width), F32)]
    roll_spec = ((3, 2 * total_rows, width), F32)
    back_spec = [((3, total_rows, width), F32), ((total_rows, width), BF16)]
    full = (rows, features)
    column = ((rows, 1), F32)
    hid_spec = ((4, rows, hidden), BF16)
    self_scratch = [roll_spec, ((half, QC), F32)]
    cross_scratch = [roll_spec, ((total_rows, QC), F32)]
    part = functools.partial

    saved, mixes = [], []
    for p in every:
        if p == 2:
            clock += [mixes[0][2]]
        out = call(
            clock, part(self_forward, p), lens, pair(rows, width) + saved_spec, self_scratch, 5.0, *xs, w_self,
        )
        mixes.append(exchange(out[0], out[1]))
        saved.append(out[2:])
    share_far, cross_share = after((share_far, cross_share), saved[-1][0])
    shares = (share, share_near, share_far, hop(share_far, 1))
    cross_even = jnp.stack([cross_share, hop(cross_share, 2)])
    cross_shares = (cross_even, hop(cross_even, 1))
    memory_weights = section_send(cross_share, 0)

    firsts, arrived = [], []
    for p in every:
        out = call(
            clock, part(after_self, p), (),
            [(full, F32), column, (full, BF16), (full, BF16), (full, F32), column],
            [(full, F32)], 3.0,
            *mixes[p], x_all, *shares, gains, biases,
        )
        firsts.append(out)
        arrived.append(section_send(out[3], 0))
    clock += [arrived[0], memory_weights]
    out = call(
        clock, part(cross_queries, packs), (), [((packs, 2, rows, width), BF16)] * 2, [], 2.0,
        *[f[2] for f in firsts], *cross_shares,
    )
    queries = exchange(out[0], out[1], axis=1)
    memory_far = [hop(x, 2) for x in arrived]

    cross_saved, cross_mixes, memories = [], [], []
    for p in every:
        even = jnp.stack([arrived[p], after(memory_far[p], *clock) if p else memory_far[p]])
        memories.append((even, hop(even, 1)))
        out = call(
            clock, part(cross_forward, p), lens, pair(rows, width) + saved_spec, cross_scratch, 6.0,
            *queries, *memories[p], memory_weights,
        )
        cross_mixes.append(exchange(out[0], out[1]))
        cross_saved.append(out[2:])

    decs, cross_grads = [], []
    for p in every:
        out = call(
            clock, part(after_cross, p), (tgt_len,),
            [(full, BF16)] * 3 + [hid_spec] * 2 + [(full, BF16)] + pair(rows, width) + [(full, F32), ((8, features), F32)],
            [(full, F32), (full, F32)], 5.0,
            *cross_mixes[p], firsts[p][0], *shares, *cross_shares, gains, biases, cgain, cbias, cotangent,
        )
        decs.append(out)
        cross_grads.append(exchange(out[6], out[7]))

    add = lambda a, b: (a.astype(F32) + b.astype(F32)).astype(BF16)
    carried, aliases = (), ()
    encoded_grads, nears = [], []
    for p in every:
        if p == 2:
            clock += nears[:1]
        out = call(
            clock, part(cross_backward, p), lens,
            [((packs, 2, rows, width), BF16)] * 2 + pair(rows, features) + [((2, width, features), F32)],
            cross_scratch + back_spec, 7.0,
            *cross_grads[p], *cross_saved[p], *memories[p], memory_weights, *carried, aliases=aliases,
        )
        near = hop(out[3], 1)
        nears.append(near)
        far = hop(add(out[2][1], near[1]), 2)
        encoded_grads.append(section_send(add(add(out[2][0], near[0]), far), 1))
        carried, aliases = (out[0], out[1], out[4]), ((-3, 0), (-2, 1), (-1, 4))
    query_grads = exchange(carried[0], after(carried[1], far), axis=1)
    memory_sent = section_send(after(carried[2], encoded_grads[-1]).astype(BF16), 1)

    encs, self_grads = [], []
    for p in every:
        out = call(
            clock, part(before_self, p), (),
            [(full, F32), (full, BF16)] + pair(rows, width) + [((8, features), F32)]
            + [(full, BF16), (full, BF16), hid_spec, hid_spec],
            [(full, F32)], 4.0,
            firsts[p][0], firsts[p][1], firsts[p][2], gains, *shares, *cross_shares, encoded_grads[p],
            firsts[p][4], firsts[p][5], *query_grads, decs[p][8], decs[p][9],
            *decs[p][1:5], aliases=((-4, 5), (-3, 6), (-2, 7), (-1, 8)),
        )
        encs.append(out)
        self_grads.append(exchange(out[2], out[3]))
    up_even, up_odd, down_even, down_odd = call(
        clock, part(ffn_grads, packs), (), pair(features, hidden) + pair(hidden, features), [], 4.0,
        *[e[5] for e in encs], *[e[7] for e in encs], *[e[6] for e in encs], *[e[8] for e in encs],
    )
    down_near, up_near = hop(down_odd, 1), hop(up_odd, 1)
    down_far = hop(add(down_even[1], down_near[1]), 2)
    down_sum = add(add(down_even[0], down_near[0]), down_far)
    up_far = hop(after(add(up_even[1], up_near[1]), down_far), 2)
    up_sum = add(add(up_even[0], up_near[0]), up_far)
    chained = []
    down_grad = chain_sum(down_sum, chained)
    clock += [down_near, up_near]
    carried = ()
    for p in every:
        if p == packs - 1:
            clock += [down_far]
        carried = call(
            clock, part(self_backward, p), lens,
            [((2, packs, rows, features), BF16)] * 2 + [((3, features, width), F32)], self_scratch + back_spec,
            7.0,
            *self_grads[p], *saved[p], *xs, w_self, *carried, aliases=((-3, 0), (-2, 1), (-1, 2)) if p else (),
        )
    out_even, out_odd = call(
        clock, part(projection_grads, packs), (), pair(3, width, features), [], 2.0,
        *sum(mixes, ()), *sum(cross_mixes, ()), *query_grads,
        *[e[1] for e in encs], *[f[2] for f in firsts], *[d[5] for d in decs],
    )
    out_near = hop(out_odd, 1)
    out_far = hop(after(add(out_even[1], out_near[1]), up_far), 2)
    row_near = hop(carried[1], 1)
    row_far = hop(add(carried[0][1], row_near[1]), 2)
    input_grads = [
        encs[p][0] + carried[0][0, p].astype(F32) + row_near[0, p].astype(F32) + row_far[p].astype(F32)
        for p in every
    ]
    out_sum = add(add(out_even[0], out_near[0]), out_far)
    out_sum = jnp.concatenate([out_sum[:1], jnp.where(is_dec, out_sum[1:], memory_sent)])
    up_grad = chain_sum(up_sum, chained)
    norms = tree_sum(after(sum(e[4] for e in encs), *chained))
    out_grad = chain_sum(out_sum, chained)
    qkv_grad = chain_sum(carried[2].astype(BF16), chained)
    cross_norms = norms[4:6]
    cross_norms = jnp.where(is_dec, cross_norms, section_send(cross_norms, 1))

    layer_rows = jnp.stack([jnp.where(is_dec, decs[p][0], firsts[p][3]) for p in every])
    wide = lambda value: value.astype(F32)[None]
    return (
        layer_rows[None],
        jnp.stack(input_grads)[None],
        wide(qkv_grad),
        wide(out_grad[0]),
        wide(up_grad),
        wide(down_grad),
        wide(out_grad[1].T),
        wide(out_grad[2].T),
        norms[0:2][None],
        norms[2:4][None],
        cross_norms[0],
        cross_norms[1],
    )


def solution(mesh):
    return jax.shard_map(
        body,
        mesh=mesh,
        in_specs=(
            P("section", "dp", "mp", None),
            P("dp", None),
            P("dp", None),
            P("section", None, None, "mp"),
            P("section", "mp", None),
            P("section", None, "mp"),
            P("section", "mp", None),
            P("section", None, "mp"),
            P("section", None, "mp"),
            P("section", None, None),
            P("section", None, None),
            P(),
            P(),
            P("dp", "mp", None),
        ),
        out_specs=(
            P("section", "dp", "mp", None),
            P("section", "dp", "mp", None),
            P("section", None, None, "mp"),
            P("section", "mp", None),
            P("section", None, "mp"),
            P("section", "mp", None),
            P("section", None, "mp"),
            P("section", None, "mp"),
            P("section", None, None),
            P("section", None, None),
            P(),
            P(),
        ),
        check_vma=False,
    )
```

```python
import functools

import jax
import jax.numpy as jnp
from jax import lax
from jax.experimental import pallas as pl
from jax.experimental.pallas import tpu as pltpu
from jax.sharding import PartitionSpec as P

HD = 64
EPS = 1e-05
NEG = -1000000000.0
F32 = jnp.float32
BF16 = jnp.bfloat16
QC = 512
COST = 2e8
SCOPED = 12 * 1024 * 1024


def nn(left, right):
    return lax.dot_general(left, right, (((1,), (0,)), ((), ())), preferred_element_type=F32)


def nt(left, right):
    return lax.dot_general(left, right, (((1,), (1,)), ((), ())), preferred_element_type=F32)


def tn(left, right):
    return lax.dot_general(left, right, (((0,), (0,)), ((), ())), preferred_element_type=F32)


def hop(value, distance):
    count = lax.axis_size("mp")
    return lax.ppermute(value, "mp", [(i, i ^ distance) for i in range(count)])


def gather(own):
    even = jnp.stack([own, hop(own, 2)])
    return even, hop(even, 1)


def exchange(blocks):
    return [blocks[0]] + [hop(blocks[r], r) for r in range(1, 4)]


def after(value, *earlier):
    return lax.optimization_barrier((value, earlier))[0]


def reduce_rows(even, odd):
    near = hop(odd, 1)
    far = hop((even[1].astype(F32) + near[1].astype(F32)).astype(BF16), 2)
    return even[0].astype(F32) + near[0].astype(F32) + far.astype(F32)


def section_send(value, source):
    return lax.ppermute(value, "section", [(source, 1 - source)])


def chain_sum(values, earlier):
    count = lax.axis_size("dp")
    if count == 1:
        return values
    if count % 2:
        return lax.psum(values, "dp")
    index = lax.axis_index("dp")
    middle = count // 2
    pairs = [[(i, i + 1), (count - 1 - i, count - 2 - i)] for i in range(middle - 1)]
    for k, step in enumerate(pairs + [[(middle - 1, middle), (middle, middle - 1)]]):
        moved = lax.ppermute(after(values, *earlier) if k == 0 else values, "dp", step)
        if k == 0:
            earlier[:] = [moved]
        values = (values.astype(F32) + moved.astype(F32)).astype(BF16)
    for i in reversed(range(middle - 1)):
        moved = lax.ppermute(values, "dp", [(b, a) for a, b in pairs[i]])
        values = jnp.where((index == i) | (index == count - 1 - i), moved, values)
    return values


def blocks_of(even, odd):
    return even.at[0], odd.at[0], even.at[1], odd.at[1]


def pack_layout(lengths, pack, sentences):
    ends, start, largest, top, end = [], 0, 0, 0, 0
    for j in range(sentences):
        size = lengths[pack, j]
        better = size > top
        start = jnp.where(better, end, start)
        largest = jnp.where(better, j, largest)
        top = jnp.where(better, size, top)
        end = end + size
        ends.append(end)
    return ends, start, largest


def segment_ids(ends, shift, first, shape, dim, total):
    at = lax.broadcasted_iota(jnp.int32, shape, dim) + (first + shift)
    at = jnp.where(at >= total, at - total, at)
    return sum(jnp.where(at >= end, 1, 0) for end in ends)


def center_rows(total):
    center = jnp.mean(total, axis=-1, keepdims=True)
    centred = total - center
    inverse = lax.rsqrt(jnp.mean(centred * centred, axis=-1, keepdims=True) + EPS)
    return centred * inverse, inverse


def norm_back(grad, scaled, inverse, gain):
    inner = grad * gain
    first = jnp.mean(inner, axis=-1, keepdims=True)
    second = jnp.mean(inner * scaled, axis=-1, keepdims=True)
    return (
        inverse * (inner - first - scaled * second),
        jnp.sum(grad * scaled, axis=0, keepdims=True),
        jnp.sum(grad, axis=0, keepdims=True),
    )


def place(roll, slot, me, block, rows, value):
    count = roll.shape[1] // 2
    start = pl.multiple_of((me ^ block) * rows, rows)
    roll[slot, pl.ds(start, rows), :] = value
    roll[slot, pl.ds(start + count, rows), :] = value


def rolled(roll, slot, shift, half, size):
    return roll[slot, pl.ds(shift + half * size, size), :]


def unroll_into(roll, slot, shift, source, half):
    roll[slot, pl.ds(shift + half, half), :] = source[0:half, :]
    roll[slot, pl.ds(shift + 2 * half, half), :] = source[half : 2 * half, :]
    roll[slot, pl.ds(shift, half), :] = source[half : 2 * half, :]


def unrolled(roll, slot, me, block, rows, half):
    return roll[slot, pl.ds(pl.multiple_of(half + (me ^ block) * rows, rows), rows), :]


def head_masks(width):
    lane = lax.broadcasted_iota(jnp.int32, (1, width), 1)
    return [
        jnp.where((lane >= h * HD) & (lane < (h + 1) * HD), 1.0, 0.0).astype(BF16)
        for h in range(width // HD)
    ]


def attend_chunk(keys, values, query, bias, masks):
    tops, sums, outs = [], [], []
    for h, mask in enumerate(masks):
        scores = nt(keys, query * mask) + bias
        top = jnp.max(scores, axis=0, keepdims=True)
        raised = jnp.exp(scores - top)
        total = jnp.sum(raised, axis=0, keepdims=True)
        mixed = tn(values, raised.astype(BF16))
        outs.append(mixed[h * HD : (h + 1) * HD, :] / total)
        sums.append(top + jnp.log(total))
    return jnp.concatenate(outs, axis=0).T, sums


def attend_back_chunk(keys, values, query, grad, out, lse, bias, masks):
    folded = (grad.astype(F32) * out).T
    grad_query = []
    probs, grads = [], []
    for h, mask in enumerate(masks):
        scores = nt(keys, query * mask) + bias
        prob = jnp.exp(scores - lse[h])
        grad_prob = nt(values, grad * mask)
        inner = jnp.sum(folded[h * HD : (h + 1) * HD, :], axis=0, keepdims=True)
        grad_score = (prob * (grad_prob - inner)).astype(BF16)
        probs.append(prob.astype(BF16))
        grads.append(grad_score)
        grad_query.append(tn(keys, grad_score)[h * HD : (h + 1) * HD, :])
    grad_keys = sum(nn(g, query * m) for g, m in zip(grads, masks))
    grad_values = sum(nn(p, grad * m) for p, m in zip(probs, masks))
    return jnp.concatenate(grad_query, axis=0).T * (HD ** (-0.5)), grad_keys, grad_values


def self_bias(is_dec, ends, shift, bias, h, c, half):
    key = lax.broadcasted_iota(jnp.int32, (half, QC), 0)
    query = lax.broadcasted_iota(jnp.int32, (half, QC), 1) + c * QC
    key_ids = segment_ids(ends, shift, h * half, (half, 1), 0, 2 * half)
    query_ids = segment_ids(ends, shift, h * half + c * QC, (1, QC), 1, 2 * half)
    allowed = ((key <= query) | (is_dec == 0)) & (key_ids == query_ids)
    bias[...] = jnp.where(allowed, 0.0, NEG)


def cross_bias(source, target, first_key, first_query, size, bias, half):
    key_ids = segment_ids(source[0], source[1], first_key, (size, 1), 0, 2 * half)
    query_ids = segment_ids(target[0], target[1], first_query, (1, QC), 1, 2 * half)
    bias[0:size, :] = jnp.where(key_ids == query_ids, 0.0, NEG)


def place_of():
    return lax.axis_index("section"), lax.axis_index("mp")


def own_layout(source, target, is_dec, pack):
    sentences = source.shape[1]
    first, second = pack_layout(source, pack, sentences), pack_layout(target, pack, sentences)
    return [jnp.where(is_dec == 1, b, a) for a, b in zip(first[0], second[0])], jnp.where(
        is_dec == 1, second[1], first[1]
    )


def self_forward(
    pack, source, target, x0, x1, x2, x3, weights,
    o0, o1, o2, o3, query, keys, values, lse, outs, roll, bias,
):
    is_dec, me = place_of()
    ends, shift = own_layout(source, target, is_dec, pack)
    rows = x0.shape[1]
    half = 2 * rows
    for block, x in enumerate((x0, x1, x2, x3)):
        for slot in range(3):
            value = nn(x[pack], weights[slot])
            if slot == 0:
                value = value.astype(BF16).astype(F32) * (HD ** (-0.5))
            place(roll, slot, me, block, rows, value)
    for h in range(2):
        part = slice(h * half, (h + 1) * half)
        query[part, :] = rolled(roll, 0, shift, h, half).astype(BF16)
        keys[part, :] = rolled(roll, 1, shift, h, half).astype(BF16)
        values[part, :] = rolled(roll, 2, shift, h, half).astype(BF16)
    masks = head_masks(query.shape[1])
    chunks = half // QC

    def step(i, carry):
        h, c = i // chunks, i % chunks
        at = pl.multiple_of(i * QC, QC)
        part = pl.ds(pl.multiple_of(h * half, half), half)
        self_bias(is_dec, ends, shift, bias, h, c, half)
        out, sums = attend_chunk(
            keys[part, :],
            values[part, :],
            query[pl.ds(at, QC), :],
            bias[...],
            masks,
        )
        outs[pl.ds(at, QC), :] = out
        for k, row in enumerate(sums):
            lse[k : k + 1, pl.ds(at, QC)] = row
        return carry

    lax.fori_loop(0, 2 * chunks, step, 0)
    unroll_into(roll, 0, shift, outs, half)
    for block, o in enumerate((o0, o1, o2, o3)):
        o[...] = unrolled(roll, 0, me, block, rows, half).astype(BF16)


def self_backward(
    pack, source, target, g0, g1, g2, g3, query, keys, values, lse, outs, x0, x1, x2, x3, weights, *rest,
):
    sum_even, sum_odd, total, roll, bias, grads, grad_out = rest[-7:]
    is_dec, me = place_of()
    ends, shift = own_layout(source, target, is_dec, pack)
    rows = x0.shape[1]
    half = 2 * rows
    for block, g in enumerate((g0, g1, g2, g3)):
        place(roll, 0, me, block, rows, g[...].astype(F32))
    for h in range(2):
        grad_out[h * half : (h + 1) * half, :] = rolled(roll, 0, shift, h, half).astype(BF16)
    masks = head_masks(query.shape[1])
    chunks = half // QC
    grads[1] = jnp.zeros(grads.shape[1:], F32)
    grads[2] = jnp.zeros(grads.shape[1:], F32)

    def step(i, carry):
        h, c = i // chunks, i % chunks
        at = pl.ds(pl.multiple_of(i * QC, QC), QC)
        part = pl.ds(pl.multiple_of(h * half, half), half)
        self_bias(is_dec, ends, shift, bias, h, c, half)
        dq, dk, dv = attend_back_chunk(
            keys[part, :],
            values[part, :],
            query[at, :],
            grad_out[at, :],
            outs[at, :],
            [lse[k : k + 1, at] for k in range(len(masks))],
            bias[...],
            masks,
        )
        grads[0, at, :] = dq
        grads[1, part, :] += dk
        grads[2, part, :] += dv
        return carry

    lax.fori_loop(0, 2 * chunks, step, 0)
    for slot in range(3):
        unroll_into(roll, slot, shift, grads.at[slot], half)
    if pack:
        for old, new in zip(rest, (sum_even, sum_odd)):
            new[:, 0:pack] = old[:, 0:pack]
    sums = blocks_of(sum_even.at[:, pack], sum_odd.at[:, pack])
    for block, x in enumerate((x0, x1, x2, x3)):
        parts = [
            unrolled(roll, slot, me, block, rows, half).astype(BF16) for slot in range(3)
        ]
        sums[block][...] = sum(nt(parts[slot], weights[slot]) for slot in range(3)).astype(BF16)
        for slot in range(3):
            grad = tn(x[pack], parts[slot])
            before = rest[2] if block == 0 else total
            total[slot] = grad if pack == 0 and block == 0 else before[slot] + grad


def cross_forward(
    pack, source, target, q0, q1, q2, q3, even, odd, weights,
    o0, o1, o2, o3, query, keys, values, lse, outs, roll, bias,
):
    is_dec, me = place_of()

    @pl.when(is_dec == 1)
    def _():
        sentences = source.shape[1]
        source_ends, source_shift, source_big = pack_layout(source, pack, sentences)
        ends, shift, big = pack_layout(target, pack, sentences)
        rows = even.shape[1]
        half = 2 * rows
        own_keys = pl.multiple_of(jnp.where(source_big == big, 0, half), half)
        source_at, target_at = (source_ends, source_shift), (ends, shift)
        for block, (q, e) in enumerate(zip((q0, q1, q2, q3), blocks_of(even, odd))):
            place(roll, 0, me, block, rows, q[pack].astype(F32) * (HD ** (-0.5)))
            place(roll, 1, me, block, rows, nn(e[...], weights[0]))
            place(roll, 2, me, block, rows, nn(e[...], weights[1]))
        for h in range(2):
            part = slice(h * half, (h + 1) * half)
            query[part, :] = rolled(roll, 0, shift, h, half).astype(BF16)
            keys[part, :] = rolled(roll, 1, source_shift, h, half).astype(BF16)
            values[part, :] = rolled(roll, 2, source_shift, h, half).astype(BF16)
        masks = head_masks(query.shape[1])

        def run(i, kind, key_rows):
            at = pl.multiple_of(kind * half + i * QC, QC)
            cross_bias(source_at, target_at, key_rows.start, at, key_rows.size, bias, half)
            out, sums = attend_chunk(
                keys[key_rows, :],
                values[key_rows, :],
                query[pl.ds(at, QC), :],
                bias[0 : key_rows.size, :],
                masks,
            )
            outs[pl.ds(at, QC), :] = out
            for k, row in enumerate(sums):
                lse[k : k + 1, pl.ds(at, QC)] = row

        def step(i, carry):
            run(i, 0, pl.ds(own_keys, half))
            run(i, 1, pl.ds(0, 2 * half))
            return carry

        lax.fori_loop(0, half // QC, step, 0)
        unroll_into(roll, 0, shift, outs, half)
        for block, o in enumerate((o0, o1, o2, o3)):
            o[...] = unrolled(roll, 0, me, block, rows, half).astype(BF16)


def cross_backward(
    pack, source, target, g0, g1, g2, g3, query, keys, values, lse, outs, even, odd, weights, *rest,
):
    c0, c1, c2, c3, sum_even, sum_odd, total, roll, bias, grads, grad_out = rest[-11:]
    is_dec, me = place_of()

    @pl.when(is_dec == 1)
    def _():
        sentences = source.shape[1]
        source_ends, source_shift, source_big = pack_layout(source, pack, sentences)
        ends, shift, big = pack_layout(target, pack, sentences)
        rows = even.shape[1]
        half = 2 * rows
        own_keys = pl.multiple_of(jnp.where(source_big == big, 0, half), half)
        source_at, target_at = (source_ends, source_shift), (ends, shift)
        for block, g in enumerate((g0, g1, g2, g3)):
            place(roll, 0, me, block, rows, g[...].astype(F32))
        for h in range(2):
            grad_out[h * half : (h + 1) * half, :] = rolled(roll, 0, shift, h, half).astype(BF16)
        masks = head_masks(query.shape[1])
        grads[1] = jnp.zeros(grads.shape[1:], F32)
        grads[2] = jnp.zeros(grads.shape[1:], F32)

        def run(i, kind, key_rows):
            at = pl.ds(pl.multiple_of(kind * half + i * QC, QC), QC)
            cross_bias(source_at, target_at, key_rows.start, at.start, key_rows.size, bias, half)
            dq, dk, dv = attend_back_chunk(
                keys[key_rows, :],
                values[key_rows, :],
                query[at, :],
                grad_out[at, :],
                outs[at, :],
                [lse[k : k + 1, at] for k in range(len(masks))],
                bias[0 : key_rows.size, :],
                masks,
            )
            grads[0, at, :] = dq
            grads[1, key_rows, :] += dk
            grads[2, key_rows, :] += dv

        def step(i, carry):
            run(i, 0, pl.ds(own_keys, half))
            run(i, 1, pl.ds(0, 2 * half))
            return carry

        lax.fori_loop(0, half // QC, step, 0)
        unroll_into(roll, 0, shift, grads.at[0], half)
        unroll_into(roll, 1, source_shift, grads.at[1], half)
        unroll_into(roll, 2, source_shift, grads.at[2], half)
        sums = blocks_of(sum_even, sum_odd)
        query_grads = (c0, c1, c2, c3)
        if pack:
            for old, new in zip(rest, query_grads):
                new[0:pack] = old[0:pack]
        for block, e in enumerate(blocks_of(even, odd)):
            parts = [
                unrolled(roll, slot, me, block, rows, half).astype(BF16) for slot in range(3)
            ]
            query_grads[block][pack] = parts[0]
            sums[block][...] = (nt(parts[1], weights[0]) + nt(parts[2], weights[1])).astype(BF16)
            for slot in range(2):
                grad = tn(parts[slot + 1], e[...])
                before = rest[4] if block == 0 else total
                total[slot] = grad if pack == 0 and block == 0 else before[slot] + grad


def silu_parts(hidden):
    gate = 1.0 / (1.0 + jnp.exp(-hidden))
    return hidden * gate, gate


def split_weights(stacked):
    width = stacked.shape[0] - 2 * stacked.shape[1]
    inner = (stacked.shape[0] - width) // 2
    return pl.ds(0, width), pl.ds(width, inner), pl.ds(width + inner, inner)


def ffn_forward(normed, shares, out):
    _, up, down = split_weights(shares[0])
    for k, share in enumerate(shares):
        hidden = nn(normed, share[up, :])
        part = nn(silu_parts(hidden)[0].astype(BF16), share[down, :])
        out[...] = part if k == 0 else out[...] + part


def ffn_backward(normed, grad, shares, kept, grad_kept, out):
    _, up, down = split_weights(shares[0])
    for k, share in enumerate(shares):
        hidden = nn(normed, share[up, :])
        value, gate = silu_parts(hidden)
        kept[k] = value.astype(BF16)
        slope = gate * (1.0 + hidden * (1.0 - gate))
        grad_pre = (nt(grad, share[down, :]) * slope).astype(BF16)
        grad_kept[k] = grad_pre
        part = nt(grad_pre, share[up, :])
        out[...] = part if k == 0 else out[...] + part


def after_self(
    pack, m0, m1, m2, m3, x, w0, w1, w2, w3, gains, biases,
    scaled, inverse, low, encoded, scaled_two, inverse_two, work,
):
    is_dec, _ = place_of()
    shares = (w0, w1, w2, w3)
    rows = split_weights(shares[0])[0]
    total = x[pack].astype(F32)
    for mixed, share in zip((m0, m1, m2, m3), shares):
        total = total + nn(mixed[...], share[rows, :])
    first_scaled, first_inverse = center_rows(total)
    scaled[...] = first_scaled
    inverse[...] = first_inverse
    first = first_scaled * gains[0:1, :] + biases[0:1, :]
    low[...] = first.astype(BF16)

    @pl.when(is_dec == 0)
    def _():
        ffn_forward(low[...], shares, work)
        again = scaled[...] * gains[0:1, :] + biases[0:1, :]
        second_scaled, second_inverse = center_rows(again + work[...])
        scaled_two[...] = second_scaled
        inverse_two[...] = second_inverse
        encoded[...] = (second_scaled * gains[1:2, :] + biases[1:2, :]).astype(BF16)


def cross_queries(packs, *refs):
    lows, (ka, kb, *queries) = refs[:packs], refs[packs:]

    @pl.when(place_of()[0] == 1)
    def _():
        for pack, low in enumerate(lows):
            for query, share in zip(queries, blocks_of(ka, kb)):
                query[pack] = nn(low[...], share[0]).astype(BF16)


def after_cross(
    pack, target, m0, m1, m2, m3, scaled, w0, w1, w2, w3, ka, kb,
    gains, biases, cross_gain, cross_shift, cotangent,
    decoded, low, grad_low, hidden, grad_hidden, out_low, g0, g1, g2, g3, grad_two, norms, work, kept,
):
    is_dec, me = place_of()

    @pl.when(is_dec == 1)
    def _():
        shares, crosses = (w0, w1, w2, w3), blocks_of(ka, kb)
        rows = scaled.shape[0]
        total = scaled[...] * gains[0:1, :] + biases[0:1, :]
        for mixed, share in zip((m0, m1, m2, m3), crosses):
            total = total + nt(mixed[...], share[1])
        second_scaled, second_inverse = center_rows(total)
        kept[...] = second_scaled
        low[...] = (second_scaled * cross_gain[...] + cross_shift[...]).astype(BF16)
        ffn_forward(low[...], shares, work)
        second = kept[...] * cross_gain[...] + cross_shift[...]
        third_scaled, third_inverse = center_rows(second + work[...])
        decoded[...] = (third_scaled * gains[1:2, :] + biases[1:2, :]).astype(BF16)
        at = lax.broadcasted_iota(jnp.int32, (rows, 1), 0) + me * rows
        end = pack_layout(target, pack, target.shape[1])[0][-1]
        grad = jnp.where(at < end, cotangent[pack].astype(F32), 0.0)
        grad_third, gain_two, bias_two = norm_back(grad, third_scaled, third_inverse, gains[1:2, :])
        grad_low[...] = grad_third.astype(BF16)
        grad_two[...] = grad_third
        ffn_backward(low[...], grad_low[...], shares, hidden, grad_hidden, work)
        grad_second, cross_gain_grad, cross_bias_grad = norm_back(
            grad_two[...] + work[...], kept[...], second_inverse, cross_gain[...]
        )
        grad_two[...] = grad_second
        out_low[...] = grad_second.astype(BF16)
        for g, share in zip((g0, g1, g2, g3), crosses):
            g[...] = nn(out_low[...], share[1]).astype(BF16)
        norms[...] = jnp.zeros(norms.shape, F32)
        norms[1:2, :] = gain_two
        norms[3:4, :] = bias_two
        norms[4:5, :] = cross_gain_grad
        norms[5:6, :] = cross_bias_grad


def before_self(
    pack, scaled, inverse, low, gains, w0, w1, w2, w3, ka, kb, grad_encoded, scaled_two, inverse_two,
    c0, c1, c2, c3, grad_two, norms_in, in_low_old, grad_low_old, hidden_old, grad_hidden_old,
    grad_rows, out_low, g0, g1, g2, g3, norms, in_low, grad_low, hidden, grad_hidden, work,
):
    is_dec, _ = place_of()
    shares = (w0, w1, w2, w3)
    rows = split_weights(shares[0])[0]

    @pl.when(is_dec == 0)
    def _():
        grad_sum, gain_two, bias_two = norm_back(
            grad_encoded[...].astype(F32), scaled_two[...], inverse_two[...], gains[1:2, :]
        )
        in_low[...] = low[...]
        grad_low[...] = grad_sum.astype(BF16)
        grad_rows[...] = grad_sum
        ffn_backward(low[...], grad_low[...], shares, hidden, grad_hidden, work)
        work[...] += grad_rows[...]
        norms[...] = jnp.zeros(norms.shape, F32)
        norms[1:2, :] = gain_two
        norms[3:4, :] = bias_two

    @pl.when(is_dec == 1)
    def _():
        total = grad_two[...]
        for grad, share in zip((c0, c1, c2, c3), blocks_of(ka, kb)):
            total = total + nt(grad[pack], share[0])
        work[...] = total
        norms[...] = norms_in[...]
        in_low[...] = in_low_old[...]
        grad_low[...] = grad_low_old[...]
        hidden[...] = hidden_old[...]
        grad_hidden[...] = grad_hidden_old[...]

    grad_first, gain_one, bias_one = norm_back(work[...], scaled[...], inverse[...], gains[0:1, :])
    norms[0:1, :] = gain_one
    norms[2:3, :] = bias_one
    grad_rows[...] = grad_first
    out_low[...] = grad_first.astype(BF16)
    for g, share in zip((g0, g1, g2, g3), shares):
        g[...] = nt(out_low[...], share[rows, :]).astype(BF16)


def ffn_grads(packs, *refs):
    inputs, hiddens, grads, grad_hiddens = [refs[i * packs : (i + 1) * packs] for i in range(4)]
    up_even, up_odd, down_even, down_odd = refs[4 * packs :]
    ups, downs = blocks_of(up_even, up_odd), blocks_of(down_even, down_odd)
    for k in range(4):
        downs[k][...] = sum(tn(h[k], g[...]) for h, g in zip(hiddens, grads)).astype(BF16)
        ups[k][...] = sum(tn(x[...], h[k]) for x, h in zip(inputs, grad_hiddens)).astype(BF16)


def projection_grads(packs, *refs):
    is_dec, _ = place_of()
    take = lambda count: [refs.pop(0) for _ in range(count)]
    refs = list(refs)
    mixes, crosses = [take(4) for _ in range(packs)], [take(4) for _ in range(packs)]
    queries = take(4)
    outs, lows, cross_outs, norms = take(packs), take(packs), take(packs), take(packs)
    (received,) = take(1)
    targets = blocks_of(*take(2))
    width = mixes[0][0].shape[1]
    part = lambda k: pl.ds(k * width, width)
    sums = sum(n[...] for n in norms)
    row = lax.broadcasted_iota(jnp.int32, sums.shape, 0)
    from_cross = (is_dec == 0) & ((row == 4) | (row == 5))
    sums = jnp.where(from_cross, received[pl.ds(2 * width, sums.shape[0]), :].astype(F32), sums).astype(BF16)
    for k in range(4):
        targets[k][part(0), :] = sum(tn(m[k][...], g[...]) for m, g in zip(mixes, outs)).astype(BF16)
        targets[k][pl.ds(3 * width, sums.shape[0]), :] = sums

    @pl.when(is_dec == 1)
    def _():
        for k in range(4):
            targets[k][part(1), :] = sum(
                tn(queries[k][p], x[...]) for p, x in enumerate(lows)
            ).astype(BF16)
            targets[k][part(2), :] = sum(
                tn(c[k][...], g[...]) for g, c in zip(cross_outs, crosses)
            ).astype(BF16)


def call(clock, kernel, scalars, outs, scratch, micros, *operands, aliases=()):
    space = pl.BlockSpec(memory_space=pltpu.VMEM)
    operands = after(operands, *clock)
    operands = [pltpu.with_memory_space_constraint(x, pltpu.VMEM) for x in operands]
    results = pl.pallas_call(
        kernel,
        out_shape=[pltpu.VMEM(shape, kind) for shape, kind in outs],
        in_specs=[pl.BlockSpec(memory_space=pltpu.SMEM)] * len(scalars) + [space] * len(operands),
        out_specs=[space] * len(outs),
        scratch_shapes=[pltpu.VMEM(shape, kind) for shape, kind in scratch],
        input_output_aliases={len(scalars) + len(operands) + a: b for a, b in aliases},
        compiler_params=pltpu.CompilerParams(vmem_limit_bytes=SCOPED),
        cost_estimate=pl.CostEstimate(
            flops=int(micros * COST), bytes_accessed=1, transcendentals=0
        ),
    )(*scalars, *operands)
    clock[:] = [results[0]]
    return results


def body(
    embeddings, src_len, tgt_len, attn_in, attn_out, ffn_in, ffn_out, cross_a, cross_b,
    norm_gain, norm_bias, cross_gain, cross_bias_vec, cotangent,
):
    is_dec = lax.axis_index("section") == 1
    x_all = embeddings[0]
    packs, rows, features = x_all.shape
    total_rows = rows * lax.axis_size("mp")
    half = total_rows // 2
    width = attn_in.shape[3]
    hidden = ffn_in.shape[2]
    gains, biases = norm_gain[0], norm_bias[0]
    cgain, cbias = cross_gain[None, :], cross_bias_vec[None, :]
    lens = (src_len, tgt_len)
    every = range(packs)
    w_self = attn_in[0]
    share = jnp.concatenate([attn_out[0], ffn_in[0], ffn_out[0]], axis=0)
    cross_share = jnp.stack([cross_a[0], cross_b[0]])

    clock = []
    x_far = hop(x_all, 2)
    xs = (x_all, hop(x_all, 1), x_far, hop(x_far, 1))
    cross_share = after(cross_share, x_far)
    memory_weights = section_send(cross_share, 0)
    share_far = hop(after(share, x_far), 2)
    share_near = hop(after(share, xs[3]), 1)

    pair = lambda *tail: [((2,) + tail, BF16)] * 2
    saved_spec = [((total_rows, width), BF16)] * 3 + [((8, total_rows), F32), ((total_rows, width), F32)]
    roll_spec = ((3, 2 * total_rows, width), F32)
    back_spec = [((3, total_rows, width), F32), ((total_rows, width), BF16)]
    full = (rows, features)
    column = ((rows, 1), F32)
    hid_spec = ((4, rows, hidden), BF16)
    self_scratch = [roll_spec, ((half, QC), F32)]
    cross_scratch = [roll_spec, ((total_rows, QC), F32)]
    part = functools.partial

    blocks = [((rows, width), BF16)] * 4
    saved, mixes = [], []
    for p in every:
        if p == 1:
            clock += [share_near, memory_weights]
        else:
            clock += sum(mixes[:1], [])
        out = call(
            clock, part(self_forward, p), lens, blocks + saved_spec, self_scratch, 5.0, *xs, w_self,
        )
        mixes.append(exchange(out[:4]))
        saved.append(out[4:])
    share_far, cross_share = after((share_far, cross_share), saved[-1][0])
    shares = (share, share_near, share_far, hop(share_far, 1))
    cross_far = hop(cross_share, 2)

    firsts, arrived = [], []
    for p in every:
        clock += sum(mixes[p + 1 : p + 2], [])
        out = call(
            clock, part(after_self, p), (),
            [(full, F32), column, (full, BF16), (full, BF16), (full, F32), column],
            [(full, F32)], 3.0,
            *mixes[p], x_all, *shares, gains, biases,
        )
        firsts.append(out)
        arrived.append(section_send(out[3], 0))
    cross_even = jnp.stack([cross_share, after(cross_far, firsts[-2][0])])
    cross_shares = (cross_even, hop(cross_even, 1))
    clock += arrived[:1]
    queries = exchange(call(
        clock, part(cross_queries, packs), (), [((packs, rows, width), BF16)] * 4, [], 2.0,
        *[f[2] for f in firsts], *cross_shares,
    ))
    memory_far = [hop(x, 2) for x in arrived]

    cross_saved, cross_mixes, memories = [], [], []
    clock += arrived[1:]
    for p in every:
        even = jnp.stack([arrived[p], after(memory_far[p], *clock) if p else memory_far[p]])
        memories.append((even, hop(even, 1)))
        out = call(
            clock, part(cross_forward, p), lens, blocks + saved_spec, cross_scratch, 6.0,
            *queries, *memories[p], memory_weights,
        )
        cross_mixes.append(exchange(out[:4]))
        cross_saved.append(out[4:])

    add = lambda a, b: (a.astype(F32) + b.astype(F32)).astype(BF16)
    decs, cross_grads, nears, fars, encoded_grads = [], [], [], [], []

    def run_after(p):
        out = call(
            clock, part(after_cross, p), (tgt_len,),
            [(full, BF16)] * 3 + [hid_spec] * 2 + [(full, BF16)] + blocks + [(full, F32), ((16, features), F32)],
            [(full, F32), (full, F32)], 5.0,
            *cross_mixes[p], firsts[p][0], *shares, *cross_shares, gains, biases, cgain, cbias, cotangent,
        )
        decs.append(out)
        cross_grads.append(exchange(out[6:10]))

    def run_cross(p, carried):
        out = call(
            clock, part(cross_backward, p), lens,
            [((packs, rows, width), BF16)] * 4 + pair(rows, features) + [((2, width, features), F32)],
            cross_scratch + back_spec, 7.0,
            *cross_grads[p], *cross_saved[p], *memories[p], memory_weights, *carried,
            aliases=((-5, 0), (-4, 1), (-3, 2), (-2, 3), (-1, 6)) if p else (),
        )
        nears.append(hop(out[5], 1))
        fars.append(hop(add(out[4][1], nears[-1][1]), 2))
        encoded_grads.append(section_send(add(add(out[4][0], nears[-1][0]), fars[-1]), 1))
        return (*out[:4], out[6])

    carried = ()
    for p in every:
        run_after(p)
        if p == packs - 2:
            carried = run_cross(0, carried)
    for p in range(1 if packs > 1 else 0, packs):
        clock += nears[:1] if p == 1 else fars[:1]
        carried = run_cross(p, carried)
    query_grads = exchange(after(carried[:4], fars[-1]))
    norm_rows = sum(d[11] for d in decs).astype(BF16)
    memory_sent = jnp.concatenate([carried[4].astype(BF16).reshape(2 * width, features), norm_rows])

    encs, self_grads = [], []
    for p in every:
        out = call(
            clock, part(before_self, p), (),
            [(full, F32), (full, BF16)] + blocks + [((16, features), F32)]
            + [(full, BF16), (full, BF16), hid_spec, hid_spec],
            [(full, F32)], 4.0,
            firsts[p][0], firsts[p][1], firsts[p][2], gains, *shares, *cross_shares, encoded_grads[p],
            firsts[p][4], firsts[p][5], *query_grads, decs[p][10], decs[p][11],
            *decs[p][1:5], aliases=((-4, 7), (-3, 8), (-2, 9), (-1, 10)),
        )
        encs.append(out)
        if p == 0:
            memory_sent = section_send(after(memory_sent, out[0]), 1)
        self_grads.append(exchange(out[2:6]))
    clock += self_grads[0] + self_grads[1] + [memory_sent]
    up_even, up_odd, down_even, down_odd = call(
        clock, part(ffn_grads, packs), (), pair(features, hidden) + pair(hidden, features), [], 4.0,
        *[e[7] for e in encs], *[e[9] for e in encs], *[e[8] for e in encs], *[e[10] for e in encs],
    )
    down_near, up_near = hop(down_odd, 1), hop(up_odd, 1)
    down_far = hop(add(down_even[1], down_near[1]), 2)
    down_sum = add(add(down_even[0], down_near[0]), down_far)
    up_far = hop(after(add(up_even[1], up_near[1]), down_far), 2)
    up_sum = add(add(up_even[0], up_near[0]), up_far)
    chained = []
    down_grad = chain_sum(down_sum, chained)
    rest_rows = 3 * width + 16
    out_even, out_odd = call(
        clock, part(projection_grads, packs), (), pair(rest_rows, features), [], 2.0,
        *sum(mixes, []), *sum(cross_mixes, []), *query_grads,
        *[e[1] for e in encs], *[f[2] for f in firsts], *[d[5] for d in decs], *[e[6] for e in encs], memory_sent,
    )
    clock += [down_near, up_near]
    out_near = hop(out_odd, 1)
    out_far = hop(after(add(out_even[1], out_near[1]), up_far), 2)
    carried = ()
    for p in every:
        if p == packs - 1:
            clock += [down_far, up_far]
        carried = call(
            clock, part(self_backward, p), lens,
            [((2, packs, rows, features), BF16)] * 2 + [((3, features, width), F32)], self_scratch + back_spec, 7.0,
            *self_grads[p], *saved[p], *xs, w_self, *carried, aliases=((-3, 0), (-2, 1), (-1, 2)) if p else (),
        )
    row_near = hop(carried[1], 1)
    row_far = hop(add(carried[0][1], row_near[1]), 2)
    input_grads = [
        encs[p][0] + carried[0][0, p].astype(F32) + row_near[0, p].astype(F32) + row_far[p].astype(F32)
        for p in every
    ]
    out_sum = add(add(out_even[0], out_near[0]), out_far)
    norm_at = 3 * width
    cross_sum = jnp.where(is_dec, out_sum[width:norm_at], memory_sent[: 2 * width])
    out_sum = jnp.concatenate([out_sum[:width], cross_sum, out_sum[norm_at:]])
    up_grad = chain_sum(up_sum, chained)
    out_grad = chain_sum(out_sum, chained)
    qkv_grad = chain_sum(carried[2].astype(BF16), chained)
    norms = out_grad[norm_at:].astype(F32)

    picks = after([(decs[p][0], firsts[p][3]) for p in every], *clock)
    layer_rows = jnp.stack([jnp.where(is_dec, a, b) for a, b in picks])
    wide = lambda value: value.astype(F32)[None]
    return (
        layer_rows[None],
        jnp.stack(input_grads)[None],
        wide(qkv_grad),
        wide(out_grad[:width]),
        wide(up_grad),
        wide(down_grad),
        wide(out_grad[width : 2 * width].T),
        wide(out_grad[2 * width : norm_at].T),
        norms[0:2][None],
        norms[2:4][None],
        norms[4],
        norms[5],
    )


def solution(mesh):
    return jax.shard_map(
        body,
        mesh=mesh,
        in_specs=(
            P("section", "dp", "mp", None),
            P("dp", None),
            P("dp", None),
            P("section", None, None, "mp"),
            P("section", "mp", None),
            P("section", None, "mp"),
            P("section", "mp", None),
            P("section", None, "mp"),
            P("section", None, "mp"),
            P("section", None, None),
            P("section", None, None),
            P(),
            P(),
            P("dp", "mp", None),
        ),
        out_specs=(
            P("section", "dp", "mp", None),
            P("section", "dp", "mp", None),
            P("section", None, None, "mp"),
            P("section", "mp", None),
            P("section", None, "mp"),
            P("section", "mp", None),
            P("section", None, "mp"),
            P("section", None, "mp"),
            P("section", None, None),
            P("section", None, None),
            P(),
            P(),
        ),
        check_vma=False,
    )
```

```python
import functools

import jax
import jax.numpy as jnp
from jax import lax
from jax.experimental import pallas as pl
from jax.experimental.pallas import tpu as pltpu
from jax.sharding import PartitionSpec as P

HD = 64
EPS = 1e-05
NEG = -1000000000.0
F32 = jnp.float32
BF16 = jnp.bfloat16
QC = 512
COST = 2e8
SCOPED = 14 * 1024 * 1024


def nn(left, right):
    return lax.dot_general(left, right, (((1,), (0,)), ((), ())), preferred_element_type=F32)


def nt(left, right):
    return lax.dot_general(left, right, (((1,), (1,)), ((), ())), preferred_element_type=F32)


def tn(left, right):
    return lax.dot_general(left, right, (((0,), (0,)), ((), ())), preferred_element_type=F32)


def hop(value, distance):
    count = lax.axis_size("mp")
    return lax.ppermute(value, "mp", [(i, i ^ distance) for i in range(count)])


def gather(own):
    even = jnp.stack([own, hop(own, 2)])
    return even, hop(even, 1)


def exchange(blocks):
    return [blocks[0]] + [hop(blocks[r], r) for r in range(1, 4)]


def after(value, *earlier):
    return lax.optimization_barrier((value, earlier))[0]


def reduce_rows(even, odd):
    near = hop(odd, 1)
    far = hop((even[1].astype(F32) + near[1].astype(F32)).astype(BF16), 2)
    return even[0].astype(F32) + near[0].astype(F32) + far.astype(F32)


def section_send(value, source):
    return lax.ppermute(value, "section", [(source, 1 - source)])


def chain_sum(values, earlier):
    count = lax.axis_size("dp")
    if count == 1:
        return values
    if count % 2:
        return lax.psum(values, "dp")
    index = lax.axis_index("dp")
    middle = count // 2
    pairs = [[(i, i + 1), (count - 1 - i, count - 2 - i)] for i in range(middle - 1)]
    for k, step in enumerate(pairs + [[(middle - 1, middle), (middle, middle - 1)]]):
        moved = lax.ppermute(after(values, *earlier) if k == 0 else values, "dp", step)
        if k == 0:
            earlier[:] = [moved]
        values = (values.astype(F32) + moved.astype(F32)).astype(BF16)
    for i in reversed(range(middle - 1)):
        moved = lax.ppermute(values, "dp", [(b, a) for a, b in pairs[i]])
        values = jnp.where((index == i) | (index == count - 1 - i), moved, values)
    return values


def blocks_of(even, odd):
    return even.at[0], odd.at[0], even.at[1], odd.at[1]


def pack_layout(lengths, pack, sentences):
    ends, start, largest, top, end = [], 0, 0, 0, 0
    for j in range(sentences):
        size = lengths[pack, j]
        better = size > top
        start = jnp.where(better, end, start)
        largest = jnp.where(better, j, largest)
        top = jnp.where(better, size, top)
        end = end + size
        ends.append(end)
    return ends, start, largest


def segment_ids(ends, shift, first, shape, dim, total):
    at = lax.broadcasted_iota(jnp.int32, shape, dim) + (first + shift)
    at = jnp.where(at >= total, at - total, at)
    return sum(jnp.where(at >= end, 1, 0) for end in ends)


def center_rows(total):
    center = jnp.mean(total, axis=-1, keepdims=True)
    centred = total - center
    inverse = lax.rsqrt(jnp.mean(centred * centred, axis=-1, keepdims=True) + EPS)
    return centred * inverse, inverse


def norm_back(grad, scaled, inverse, gain):
    inner = grad * gain
    first = jnp.mean(inner, axis=-1, keepdims=True)
    second = jnp.mean(inner * scaled, axis=-1, keepdims=True)
    return (
        inverse * (inner - first - scaled * second),
        jnp.sum(grad * scaled, axis=0, keepdims=True),
        jnp.sum(grad, axis=0, keepdims=True),
    )


def place(roll, slot, me, block, rows, value):
    count = roll.shape[1] // 2
    start = pl.multiple_of((me ^ block) * rows, rows)
    roll[slot, pl.ds(start, rows), :] = value
    roll[slot, pl.ds(start + count, rows), :] = value


def rolled(roll, slot, shift, half, size):
    return roll[slot, pl.ds(shift + half * size, size), :]


def unroll_into(roll, slot, shift, source, half):
    roll[slot, pl.ds(shift + half, half), :] = source[0:half, :]
    roll[slot, pl.ds(shift + 2 * half, half), :] = source[half : 2 * half, :]
    roll[slot, pl.ds(shift, half), :] = source[half : 2 * half, :]


def unrolled(roll, slot, me, block, rows, half):
    return roll[slot, pl.ds(pl.multiple_of(half + (me ^ block) * rows, rows), rows), :]


def head_masks(width):
    lane = lax.broadcasted_iota(jnp.int32, (1, width), 1)
    return [
        jnp.where((lane >= h * HD) & (lane < (h + 1) * HD), 1.0, 0.0).astype(BF16)
        for h in range(width // HD)
    ]


def attend_chunk(keys, values, query, bias, masks):
    tops, sums, outs = [], [], []
    for h, mask in enumerate(masks):
        scores = nt(keys, query * mask) + bias
        top = jnp.max(scores, axis=0, keepdims=True)
        raised = jnp.exp(scores - top)
        total = jnp.sum(raised, axis=0, keepdims=True)
        mixed = tn(values, raised.astype(BF16))
        outs.append(mixed[h * HD : (h + 1) * HD, :] / total)
        sums.append(top + jnp.log(total))
    return jnp.concatenate(outs, axis=0).T, sums


def attend_back_chunk(keys, values, query, grad, out, lse, bias, masks):
    folded = (grad.astype(F32) * out).T
    grad_query = []
    probs, grads = [], []
    for h, mask in enumerate(masks):
        scores = nt(keys, query * mask) + bias
        prob = jnp.exp(scores - lse[h])
        grad_prob = nt(values, grad * mask)
        inner = jnp.sum(folded[h * HD : (h + 1) * HD, :], axis=0, keepdims=True)
        grad_score = (prob * (grad_prob - inner)).astype(BF16)
        probs.append(prob.astype(BF16))
        grads.append(grad_score)
        grad_query.append(tn(keys, grad_score)[h * HD : (h + 1) * HD, :])
    grad_keys = sum(nn(g, query * m) for g, m in zip(grads, masks))
    grad_values = sum(nn(p, grad * m) for p, m in zip(probs, masks))
    return jnp.concatenate(grad_query, axis=0).T * (HD ** (-0.5)), grad_keys, grad_values


def self_bias(is_dec, ends, shift, bias, h, c, half):
    key = lax.broadcasted_iota(jnp.int32, (half, QC), 0)
    query = lax.broadcasted_iota(jnp.int32, (half, QC), 1) + c * QC
    key_ids = segment_ids(ends, shift, h * half, (half, 1), 0, 2 * half)
    query_ids = segment_ids(ends, shift, h * half + c * QC, (1, QC), 1, 2 * half)
    allowed = ((key <= query) | (is_dec == 0)) & (key_ids == query_ids)
    bias[...] = jnp.where(allowed, 0.0, NEG)


def cross_bias(source, target, first_key, first_query, size, bias, half):
    key_ids = segment_ids(source[0], source[1], first_key, (size, 1), 0, 2 * half)
    query_ids = segment_ids(target[0], target[1], first_query, (1, QC), 1, 2 * half)
    bias[0:size, :] = jnp.where(key_ids == query_ids, 0.0, NEG)


def place_of():
    return lax.axis_index("section"), lax.axis_index("mp")


def own_layout(source, target, is_dec, pack):
    sentences = source.shape[1]
    first, second = pack_layout(source, pack, sentences), pack_layout(target, pack, sentences)
    return [jnp.where(is_dec == 1, b, a) for a, b in zip(first[0], second[0])], jnp.where(
        is_dec == 1, second[1], first[1]
    )


def self_forward(
    pack, source, target, x0, x1, x2, x3, weights,
    o0, o1, o2, o3, query, keys, values, lse, outs, roll, bias,
):
    is_dec, me = place_of()
    ends, shift = own_layout(source, target, is_dec, pack)
    rows = x0.shape[1]
    half = 2 * rows
    for block, x in enumerate((x0, x1, x2, x3)):
        for slot in range(3):
            value = nn(x[pack], weights[slot])
            if slot == 0:
                value = value.astype(BF16).astype(F32) * (HD ** (-0.5))
            place(roll, slot, me, block, rows, value)
    for h in range(2):
        part = slice(h * half, (h + 1) * half)
        query[part, :] = rolled(roll, 0, shift, h, half).astype(BF16)
        keys[part, :] = rolled(roll, 1, shift, h, half).astype(BF16)
        values[part, :] = rolled(roll, 2, shift, h, half).astype(BF16)
    masks = head_masks(query.shape[1])
    chunks = half // QC

    def step(i, carry):
        h, c = i // chunks, i % chunks
        at = pl.multiple_of(i * QC, QC)
        part = pl.ds(pl.multiple_of(h * half, half), half)
        self_bias(is_dec, ends, shift, bias, h, c, half)
        out, sums = attend_chunk(
            keys[part, :],
            values[part, :],
            query[pl.ds(at, QC), :],
            bias[...],
            masks,
        )
        outs[pl.ds(at, QC), :] = out
        for k, row in enumerate(sums):
            lse[k : k + 1, pl.ds(at, QC)] = row
        return carry

    lax.fori_loop(0, 2 * chunks, step, 0)
    unroll_into(roll, 0, shift, outs, half)
    for block, o in enumerate((o0, o1, o2, o3)):
        o[...] = unrolled(roll, 0, me, block, rows, half).astype(BF16)


def self_backward(
    pack, at_grad, source, target, *refs,
):
    given, saved, xs, weights, rest = refs[:4], refs[4:9], refs[9:13], refs[13], refs[14:]
    sum_even, sum_odd, total, roll, bias, grads, grad_out, query, keys, values, lse, outs, x, g, arrived = rest[-15:]
    copies = [
        pltpu.make_async_copy(a, b, arrived.at[k])
        for k, (a, b) in enumerate(
            [(a.at[at_grad], g.at[k]) for k, a in enumerate(given)]
            + [*zip(saved, (query, keys, values, lse, outs))]
            + [(a.at[pack], x.at[k]) for k, a in enumerate(xs)]
        )
    ]
    for copy in copies:
        copy.start()
    is_dec, me = place_of()
    ends, shift = own_layout(source, target, is_dec, pack)
    rows = x.shape[1]
    half = 2 * rows
    for copy in copies[:4]:
        copy.wait()
    for block in range(4):
        place(roll, 0, me, block, rows, g[block].astype(F32))
    for h in range(2):
        grad_out[h * half : (h + 1) * half, :] = rolled(roll, 0, shift, h, half).astype(BF16)
    for copy in copies[4:9]:
        copy.wait()
    masks = head_masks(query.shape[1])
    chunks = half // QC
    grads[1] = jnp.zeros(grads.shape[1:], F32)
    grads[2] = jnp.zeros(grads.shape[1:], F32)

    def step(i, carry):
        h, c = i // chunks, i % chunks
        at = pl.ds(pl.multiple_of(i * QC, QC), QC)
        part = pl.ds(pl.multiple_of(h * half, half), half)
        self_bias(is_dec, ends, shift, bias, h, c, half)
        dq, dk, dv = attend_back_chunk(
            keys[part, :],
            values[part, :],
            query[at, :],
            grad_out[at, :],
            outs[at, :],
            [lse[k : k + 1, at] for k in range(len(masks))],
            bias[...],
            masks,
        )
        grads[0, at, :] = dq
        grads[1, part, :] += dk
        grads[2, part, :] += dv
        return carry

    lax.fori_loop(0, 2 * chunks, step, 0)
    for slot in range(3):
        unroll_into(roll, slot, shift, grads.at[slot], half)
    for copy in copies[9:]:
        copy.wait()
    sums = blocks_of(sum_even, sum_odd)
    for block in range(4):
        parts = [
            unrolled(roll, slot, me, block, rows, half).astype(BF16) for slot in range(3)
        ]
        sums[block][...] = sum(nt(parts[slot], weights[slot]) for slot in range(3)).astype(BF16)
        for slot in range(3):
            grad = tn(x[block], parts[slot])
            before = rest[0] if block == 0 else total
            total[slot] = grad if pack == 0 and block == 0 else before[slot] + grad


def cross_forward(
    pack, source, target, q0, q1, q2, q3, even, odd, weights,
    o0, o1, o2, o3, query, keys, values, lse, outs, roll, bias,
):
    is_dec, me = place_of()

    @pl.when(is_dec == 1)
    def _():
        sentences = source.shape[1]
        source_ends, source_shift, source_big = pack_layout(source, pack, sentences)
        ends, shift, big = pack_layout(target, pack, sentences)
        rows = even.shape[1]
        half = 2 * rows
        own_keys = pl.multiple_of(jnp.where(source_big == big, 0, half), half)
        source_at, target_at = (source_ends, source_shift), (ends, shift)
        for block, (q, e) in enumerate(zip((q0, q1, q2, q3), blocks_of(even, odd))):
            place(roll, 0, me, block, rows, q[pack].astype(F32) * (HD ** (-0.5)))
            place(roll, 1, me, block, rows, nn(e[...], weights[0]))
            place(roll, 2, me, block, rows, nn(e[...], weights[1]))
        for h in range(2):
            part = slice(h * half, (h + 1) * half)
            query[part, :] = rolled(roll, 0, shift, h, half).astype(BF16)
            keys[part, :] = rolled(roll, 1, source_shift, h, half).astype(BF16)
            values[part, :] = rolled(roll, 2, source_shift, h, half).astype(BF16)
        masks = head_masks(query.shape[1])

        def run(i, kind, key_rows):
            at = pl.multiple_of(kind * half + i * QC, QC)
            cross_bias(source_at, target_at, key_rows.start, at, key_rows.size, bias, half)
            out, sums = attend_chunk(
                keys[key_rows, :],
                values[key_rows, :],
                query[pl.ds(at, QC), :],
                bias[0 : key_rows.size, :],
                masks,
            )
            outs[pl.ds(at, QC), :] = out
            for k, row in enumerate(sums):
                lse[k : k + 1, pl.ds(at, QC)] = row

        def step(i, carry):
            run(i, 0, pl.ds(own_keys, half))
            run(i, 1, pl.ds(0, 2 * half))
            return carry

        lax.fori_loop(0, half // QC, step, 0)
        unroll_into(roll, 0, shift, outs, half)
        for block, o in enumerate((o0, o1, o2, o3)):
            o[...] = unrolled(roll, 0, me, block, rows, half).astype(BF16)


def cross_backward(
    pack, source, target, g0, g1, g2, g3, query, keys, values, lse, outs, even, odd, weights, *rest,
):
    c0, c1, c2, c3, sum_even, sum_odd, total, roll, bias, grads, grad_out = rest[-11:]
    is_dec, me = place_of()

    @pl.when(is_dec == 1)
    def _():
        sentences = source.shape[1]
        source_ends, source_shift, source_big = pack_layout(source, pack, sentences)
        ends, shift, big = pack_layout(target, pack, sentences)
        rows = even.shape[1]
        half = 2 * rows
        own_keys = pl.multiple_of(jnp.where(source_big == big, 0, half), half)
        source_at, target_at = (source_ends, source_shift), (ends, shift)
        for block, g in enumerate((g0, g1, g2, g3)):
            place(roll, 0, me, block, rows, g[...].astype(F32))
        for h in range(2):
            grad_out[h * half : (h + 1) * half, :] = rolled(roll, 0, shift, h, half).astype(BF16)
        masks = head_masks(query.shape[1])
        grads[1] = jnp.zeros(grads.shape[1:], F32)
        grads[2] = jnp.zeros(grads.shape[1:], F32)

        def run(i, kind, key_rows):
            at = pl.ds(pl.multiple_of(kind * half + i * QC, QC), QC)
            cross_bias(source_at, target_at, key_rows.start, at.start, key_rows.size, bias, half)
            dq, dk, dv = attend_back_chunk(
                keys[key_rows, :],
                values[key_rows, :],
                query[at, :],
                grad_out[at, :],
                outs[at, :],
                [lse[k : k + 1, at] for k in range(len(masks))],
                bias[0 : key_rows.size, :],
                masks,
            )
            grads[0, at, :] = dq
            grads[1, key_rows, :] += dk
            grads[2, key_rows, :] += dv

        def step(i, carry):
            run(i, 0, pl.ds(own_keys, half))
            run(i, 1, pl.ds(0, 2 * half))
            return carry

        lax.fori_loop(0, half // QC, step, 0)
        unroll_into(roll, 0, shift, grads.at[0], half)
        unroll_into(roll, 1, source_shift, grads.at[1], half)
        unroll_into(roll, 2, source_shift, grads.at[2], half)
        sums = blocks_of(sum_even, sum_odd)
        query_grads = (c0, c1, c2, c3)
        if pack:
            for old, new in zip(rest, query_grads):
                new[0:pack] = old[0:pack]
        for block, e in enumerate(blocks_of(even, odd)):
            parts = [
                unrolled(roll, slot, me, block, rows, half).astype(BF16) for slot in range(3)
            ]
            query_grads[block][pack] = parts[0]
            sums[block][...] = (nt(parts[1], weights[0]) + nt(parts[2], weights[1])).astype(BF16)
            for slot in range(2):
                grad = tn(parts[slot + 1], e[...])
                before = rest[4] if block == 0 else total
                total[slot] = grad if pack == 0 and block == 0 else before[slot] + grad


def silu_parts(hidden):
    gate = 1.0 / (1.0 + jnp.exp(-hidden))
    return hidden * gate, gate


def split_weights(stacked):
    width = stacked.shape[0] - 2 * stacked.shape[1]
    inner = (stacked.shape[0] - width) // 2
    return pl.ds(0, width), pl.ds(width, inner), pl.ds(width + inner, inner)


def silu_slope(hidden, value, gate):
    return gate + value * (1.0 - gate)


def ffn_forward(normed, shares, out, kept=None, slopes=None):
    _, up, down = split_weights(shares[0])
    for k, share in enumerate(shares):
        hidden = nn(normed, share[up, :])
        value, gate = silu_parts(hidden)
        low = value.astype(BF16)
        if kept is not None:
            kept[k] = low
            slopes[k] = silu_slope(hidden, value, gate)
        part = nn(low, share[down, :])
        out[...] = part if k == 0 else out[...] + part


def ffn_backward(normed, grad, shares, kept, grad_kept, out, slopes=None):
    _, up, down = split_weights(shares[0])
    for k, share in enumerate(shares):
        if slopes is None:
            hidden = nn(normed, share[up, :])
            value, gate = silu_parts(hidden)
            kept[k] = value.astype(BF16)
            slope = silu_slope(hidden, value, gate)
        else:
            slope = slopes[k]
        grad_pre = (nt(grad, share[down, :]) * slope).astype(BF16)
        grad_kept[k] = grad_pre
        part = nt(grad_pre, share[up, :])
        out[...] = part if k == 0 else out[...] + part


def after_self(
    packs, m0, m1, m2, m3, x, w0, w1, w2, w3, gains, biases,
    scaled, inverse, low, scaled_two, inverse_two, *rest,
):
    encoded, work = rest[:packs], rest[packs]
    is_dec, _ = place_of()
    shares = (w0, w1, w2, w3)
    rows = split_weights(shares[0])[0]
    flat = lambda ref: jnp.concatenate([ref[p] for p in range(packs)], axis=0)
    total = flat(x).astype(F32)
    for mixed, share in zip((m0, m1, m2, m3), shares):
        total = total + nn(flat(mixed), share[rows, :])
    first_scaled, first_inverse = center_rows(total)
    scaled[...] = first_scaled
    inverse[...] = first_inverse
    low[...] = (first_scaled * gains[0:1, :] + biases[0:1, :]).astype(BF16)

    @pl.when(is_dec == 0)
    def _():
        ffn_forward(low[...], shares, work)
        again = scaled[...] * gains[0:1, :] + biases[0:1, :]
        second_scaled, second_inverse = center_rows(again + work[...])
        scaled_two[...] = second_scaled
        inverse_two[...] = second_inverse
        result = (second_scaled * gains[1:2, :] + biases[1:2, :]).astype(BF16)
        size = result.shape[0] // packs
        for p in range(packs):
            encoded[p][...] = result[p * size : (p + 1) * size, :]


def cross_queries(packs, low, ka, kb, *queries):
    @pl.when(place_of()[0] == 1)
    def _():
        size = low.shape[0] // packs
        for query, share in zip(queries, blocks_of(ka, kb)):
            result = nn(low[...], share[0]).astype(BF16)
            for p in range(packs):
                query[p] = result[p * size : (p + 1) * size, :]


def after_cross(
    pack, target, m0, m1, m2, m3, scaled, w0, w1, w2, w3, ka, kb,
    gains, biases, cross_gain, cross_shift, cotangent,
    decoded, low, grad_low, hidden, grad_hidden, out_low, g0, g1, g2, g3, grad_two, norms, work, kept, slopes,
):
    is_dec, me = place_of()

    @pl.when(is_dec == 1)
    def _():
        shares, crosses = (w0, w1, w2, w3), blocks_of(ka, kb)
        rows = decoded.shape[0]
        total = scaled[pl.ds(pack * rows, rows), :] * gains[0:1, :] + biases[0:1, :]
        for mixed, share in zip((m0, m1, m2, m3), crosses):
            total = total + nt(mixed[...], share[1])
        second_scaled, second_inverse = center_rows(total)
        kept[...] = second_scaled
        low[...] = (second_scaled * cross_gain[...] + cross_shift[...]).astype(BF16)
        ffn_forward(low[...], shares, work, hidden, slopes)
        second = kept[...] * cross_gain[...] + cross_shift[...]
        third_scaled, third_inverse = center_rows(second + work[...])
        decoded[...] = (third_scaled * gains[1:2, :] + biases[1:2, :]).astype(BF16)
        at = lax.broadcasted_iota(jnp.int32, (rows, 1), 0) + me * rows
        end = pack_layout(target, pack, target.shape[1])[0][-1]
        grad = jnp.where(at < end, cotangent[pack].astype(F32), 0.0)
        grad_third, gain_two, bias_two = norm_back(grad, third_scaled, third_inverse, gains[1:2, :])
        grad_low[...] = grad_third.astype(BF16)
        grad_two[...] = grad_third
        ffn_backward(low[...], grad_low[...], shares, hidden, grad_hidden, work, slopes)
        grad_second, cross_gain_grad, cross_bias_grad = norm_back(
            grad_two[...] + work[...], kept[...], second_inverse, cross_gain[...]
        )
        grad_two[...] = grad_second
        out_low[...] = grad_second.astype(BF16)
        for g, share in zip((g0, g1, g2, g3), crosses):
            g[...] = nn(out_low[...], share[1]).astype(BF16)
        norms[...] = jnp.zeros(norms.shape, F32)
        norms[1:2, :] = gain_two
        norms[3:4, :] = bias_two
        norms[4:5, :] = cross_gain_grad
        norms[5:6, :] = cross_bias_grad


def before_self(
    pack, scaled, inverse, low, gains, w0, w1, w2, w3, ka, kb, grad_encoded, scaled_two, inverse_two,
    c0, c1, c2, c3, grad_two, norms_in, in_low_old, grad_low_old, hidden_old, grad_hidden_old,
    grad_rows, out_low, g0, g1, g2, g3, norms, in_low, grad_low, hidden, grad_hidden, work,
):
    is_dec, _ = place_of()
    size = grad_rows.shape[0]
    own = pl.ds(pack * size, size)
    shares = (w0, w1, w2, w3)
    rows = split_weights(shares[0])[0]

    @pl.when(is_dec == 0)
    def _():
        grad_sum, gain_two, bias_two = norm_back(
            grad_encoded[pl.ds(0, size), :].astype(F32), scaled_two[own, :], inverse_two[own, :], gains[1:2, :]
        )
        in_low[...] = low[own, :]
        grad_low[...] = grad_sum.astype(BF16)
        grad_rows[...] = grad_sum
        ffn_backward(low[own, :], grad_low[...], shares, hidden, grad_hidden, work)
        work[...] += grad_rows[...]
        norms[...] = jnp.zeros(norms.shape, F32)
        norms[1:2, :] = gain_two
        norms[3:4, :] = bias_two

    @pl.when(is_dec == 1)
    def _():
        total = grad_two[...]
        for grad, share in zip((c0, c1, c2, c3), blocks_of(ka, kb)):
            total = total + nt(grad[pack], share[0])
        work[...] = total
        norms[...] = norms_in[...]
        in_low[...] = in_low_old[...]
        grad_low[...] = grad_low_old[...]
        hidden[...] = hidden_old[...]
        grad_hidden[...] = grad_hidden_old[...]

    grad_first, gain_one, bias_one = norm_back(work[...], scaled[own, :], inverse[own, :], gains[0:1, :])
    norms[0:1, :] = gain_one
    norms[2:3, :] = bias_one
    grad_rows[...] = grad_first
    out_low[...] = grad_first.astype(BF16)
    for g, share in zip((g0, g1, g2, g3), shares):
        g[...] = nt(out_low[...], share[rows, :]).astype(BF16)


def pair_sums(even, near, keep, send):
    keep[...] = (even[0].astype(F32) + near[0].astype(F32)).astype(BF16)
    send[...] = (even[1].astype(F32) + near[1].astype(F32)).astype(BF16)


def ffn_grads(packs, *refs):
    inputs, hiddens, grads, grad_hiddens = [refs[i * packs : (i + 1) * packs] for i in range(4)]
    up_even, up_odd, down_even, down_odd = refs[4 * packs :]
    ups, downs = blocks_of(up_even, up_odd), blocks_of(down_even, down_odd)
    for k in range(4):
        downs[k][...] = sum(tn(h[k], g[...]) for h, g in zip(hiddens, grads)).astype(BF16)
        ups[k][...] = sum(tn(x[...], h[k]) for x, h in zip(inputs, grad_hiddens)).astype(BF16)


def projection_grads(packs, *refs):
    is_dec, _ = place_of()
    take = lambda count: [refs.pop(0) for _ in range(count)]
    refs = list(refs)
    mixes, crosses = take(4), [take(4) for _ in range(packs)]
    queries = take(4)
    outs, cross_outs, norms = take(packs), take(packs), take(packs)
    low, received = take(2)
    size = outs[0].shape[0]
    targets = blocks_of(*take(2))
    width = mixes[0][0].shape[1]
    part = lambda k: pl.ds(k * width, width)
    sums = sum(n[...] for n in norms)
    row = lax.broadcasted_iota(jnp.int32, sums.shape, 0)
    from_cross = (is_dec == 0) & ((row == 4) | (row == 5))
    sums = jnp.where(from_cross, received[pl.ds(received.shape[0] - sums.shape[0], sums.shape[0]), :].astype(F32), sums).astype(BF16)
    for k in range(4):
        targets[k][part(0), :] = sum(
            tn(mixes[k][p], g[...]) for p, g in enumerate(outs)
        ).astype(BF16)
        targets[k][pl.ds(3 * width, sums.shape[0]), :] = sums

    @pl.when(is_dec == 1)
    def _():
        for k in range(4):
            targets[k][part(1), :] = sum(
                tn(queries[k][p], low[pl.ds(p * size, size), :]) for p in range(packs)
            ).astype(BF16)
            targets[k][part(2), :] = sum(
                tn(c[k][...], g[...]) for g, c in zip(cross_outs, crosses)
            ).astype(BF16)


def call(clock, kernel, scalars, outs, scratch, micros, *operands, aliases=(), far_outs=(), any_ins=()):
    space = pl.BlockSpec(memory_space=pltpu.VMEM)
    operands = after(operands, *clock)
    operands = [
        pltpu.with_memory_space_constraint(x, pltpu.HBM if i in any_ins else pltpu.VMEM)
        for i, x in enumerate(operands)
    ]
    results = pl.pallas_call(
        kernel,
        out_shape=[
            pltpu.HBM(shape, kind) if i in far_outs else pltpu.VMEM(shape, kind)
            for i, (shape, kind) in enumerate(outs)
        ],
        in_specs=[pl.BlockSpec(memory_space=pltpu.SMEM)] * len(scalars) + [pl.BlockSpec(memory_space=pl.ANY) if i in any_ins else space for i in range(len(operands))],
        out_specs=[space] * len(outs),
        scratch_shapes=[pltpu.VMEM(*item) if isinstance(item, tuple) else item for item in scratch],
        input_output_aliases={len(scalars) + len(operands) + a: b for a, b in aliases},
        compiler_params=pltpu.CompilerParams(vmem_limit_bytes=SCOPED),
        cost_estimate=pl.CostEstimate(
            flops=int(micros * COST), bytes_accessed=1, transcendentals=0
        ),
    )(*scalars, *operands)
    clock[:] = [results[0]]
    return results


def body(
    embeddings, src_len, tgt_len, attn_in, attn_out, ffn_in, ffn_out, cross_a, cross_b,
    norm_gain, norm_bias, cross_gain, cross_bias_vec, cotangent,
):
    is_dec = lax.axis_index("section") == 1
    x_all = embeddings[0]
    packs, rows, features = x_all.shape
    total_rows = rows * lax.axis_size("mp")
    half = total_rows // 2
    width = attn_in.shape[3]
    hidden = ffn_in.shape[2]
    gains, biases = norm_gain[0], norm_bias[0]
    cgain, cbias = cross_gain[None, :], cross_bias_vec[None, :]
    lens = (src_len, tgt_len)
    every = range(packs)
    w_self = attn_in[0]
    share = jnp.concatenate([attn_out[0], ffn_in[0], ffn_out[0]], axis=0)
    cross_share = jnp.stack([cross_a[0], cross_b[0]])

    clock = []
    x_far = hop(x_all, 2)
    xs = (x_all, hop(x_all, 1), x_far, hop(x_far, 1))
    cross_share = after(cross_share, x_far)
    memory_weights = section_send(cross_share, 0)
    share_far = hop(after(share, x_far), 2)
    share_near = hop(after(share, xs[3]), 1)

    pair = lambda *tail: [((2,) + tail, BF16)] * 2
    saved_spec = [((total_rows, width), BF16)] * 3 + [((8, total_rows), F32), ((total_rows, width), F32)]
    roll_spec = ((3, 2 * total_rows, width), F32)
    back_spec = [((3, total_rows, width), F32), ((total_rows, width), BF16)]
    full = (rows, features)
    column = ((rows, 1), F32)
    hid_spec = ((4, rows, hidden), BF16)
    self_scratch = [roll_spec, ((half, QC), F32)]
    cross_scratch = [roll_spec, ((total_rows, QC), F32)]
    part = functools.partial

    blocks = [((rows, width), BF16)] * 4
    blocks = [((rows, width), BF16)] * 4
    stacked = lambda outs: [jnp.stack(block) for block in zip(*outs)]
    saved, mixes = [], []
    for p in every:
        if p == 1:
            clock += [share_near, memory_weights]
        out = call(
            clock, part(self_forward, p), lens, blocks + saved_spec, self_scratch, 5.0, *xs, w_self,
            far_outs=range(4, 9),
        )
        mixes.append(out[:4])
        saved.append(out[4:])
    mixes = exchange(stacked(mixes))
    share_far, cross_share = after((share_far, cross_share), clock[0], mixes[1])
    shares = (share, share_near, share_far, hop(share_far, 1))
    cross_far = hop(cross_share, 2)

    tall = (packs * rows, features)
    tall_column = ((packs * rows, 1), F32)
    out = call(
        clock, part(after_self, packs), (),
        [(tall, F32), tall_column, (tall, BF16), (tall, F32), tall_column] + [(full, BF16)] * packs,
        [(tall, F32)], 7.0,
        *mixes, x_all, *shares, gains, biases,
    )
    firsts, encoded = out[:5], out[5:]
    arrived = [section_send(e, 0) for e in encoded]
    cross_even = jnp.stack([cross_share, cross_far])
    cross_shares = (cross_even, hop(cross_even, 1))
    queries = exchange(call(
        clock, part(cross_queries, packs), (), [((packs, rows, width), BF16)] * 4, [], 2.0,
        firsts[2], *cross_shares,
    ))
    memory_far = [hop(x, 2) for x in arrived]

    cross_saved, cross_mixes, memories = [], [], []
    clock += arrived[1:]
    for p in every:
        even = jnp.stack([arrived[p], after(memory_far[p], *clock) if p else memory_far[p]])
        memories.append((even, hop(even, 1)))
        out = call(
            clock, part(cross_forward, p), lens, blocks + saved_spec, cross_scratch, 6.0,
            *queries, *memories[p], memory_weights,
        )
        cross_mixes.append(exchange(out[:4]))
        cross_saved.append(out[4:])

    add = lambda a, b: (a.astype(F32) + b.astype(F32)).astype(BF16)
    decs, cross_grads, nears, fars, encoded_grads = [], [], [], [], []

    def run_after(p):
        out = call(
            clock, part(after_cross, p), (tgt_len,),
            [(full, BF16)] * 3 + [hid_spec] * 2 + [(full, BF16)] + blocks + [(full, F32), ((16, features), F32)],
            [(full, F32), (full, F32), ((4, rows, hidden), F32)], 5.0,
            *cross_mixes[p], firsts[0], *shares, *cross_shares, gains, biases, cgain, cbias, cotangent,
        )
        decs.append(out)
        cross_grads.append(exchange(out[6:10]))

    def run_cross(p, carried):
        out = call(
            clock, part(cross_backward, p), lens,
            [((packs, rows, width), BF16)] * 4 + pair(rows, features) + [((2, width, features), F32)],
            cross_scratch + back_spec, 7.0,
            *cross_grads[p], *cross_saved[p], *memories[p], memory_weights, *carried,
            aliases=((-5, 0), (-4, 1), (-3, 2), (-2, 3), (-1, 6)) if p else (),
        )
        nears.append(hop(out[5], 1))
        fars.append(hop(add(out[4][1], nears[-1][1]), 2))
        sent = add(add(out[4][0], nears[-1][0]), fars[-1])
        if p == packs - 1:
            sent = jnp.concatenate([sent, sum(d[11] for d in decs).astype(BF16)])
        encoded_grads.append(section_send(sent, 1))
        return (*out[:4], out[6])

    carried = ()
    for p in every:
        run_after(p)
        if p == packs - 2:
            carried = run_cross(0, carried)
    for p in range(1 if packs > 1 else 0, packs):
        clock += nears[:1] if p == 1 else fars[:1]
        carried = run_cross(p, carried)
    query_grads = exchange(after(carried[:4], fars[-1]))
    memory_sent = carried[4].astype(BF16).reshape(2 * width, features)

    encs, self_grads = [], []
    for p in every:
        out = call(
            clock, part(before_self, p), (),
            [(full, F32), (full, BF16)] + blocks + [((16, features), F32)]
            + [(full, BF16), (full, BF16), hid_spec, hid_spec],
            [(full, F32)], 4.0,
            firsts[0], firsts[1], firsts[2], gains, *shares, *cross_shares, encoded_grads[p],
            firsts[3], firsts[4], *query_grads, decs[p][10], decs[p][11],
            *decs[p][1:5], aliases=((-4, 7), (-3, 8), (-2, 9), (-1, 10)),
        )
        encs.append(out)
        if p == 0:
            memory_sent = section_send(after(memory_sent, out[0]), 1)
        self_grads.append(out[2:6])
        if p == packs - 2:
            early = exchange(stacked(self_grads))
    clock += early
    self_grads = [early] * (packs - 1) + [exchange(stacked(self_grads[-1:]))]
    up_even, up_odd, down_even, down_odd = call(
        clock, part(ffn_grads, packs), (), pair(features, hidden) + pair(hidden, features), [], 4.0,
        *[e[7] for e in encs], *[e[9] for e in encs], *[e[8] for e in encs], *[e[10] for e in encs],
    )
    down_near, up_near = hop(down_odd, 1), hop(up_odd, 1)

    def merged(even, near):
        return call([], pair_sums, (), [(even.shape[1:], BF16)] * 2, [], 0.5, even, near)

    down_keep, down_send = merged(down_even, down_near)
    up_keep, up_send = merged(up_even, up_near)
    down_far = hop(down_send, 2)
    down_sum = add(down_keep, down_far)
    up_far = hop(after(up_send, down_far), 2)
    up_sum = add(up_keep, up_far)
    chained = []
    down_grad = chain_sum(down_sum, chained)
    clock += [down_near, up_send]
    carried, row_sums = (), []
    for p in every:
        if p == 1:
            rest_rows = 3 * width + 16
            out_even, out_odd = call(
                clock, part(projection_grads, packs), (), pair(rest_rows, features), [], 2.0,
                *mixes, *sum(cross_mixes, []), *query_grads,
                *[e[1] for e in encs], *[d[5] for d in decs], *[e[6] for e in encs], firsts[2], encoded_grads[-1],
            )
            out_near = hop(out_odd, 1)
            out_keep, out_send = merged(out_even, out_near)
            out_far = hop(after(out_send, up_far), 2)
        if p == packs - 1:
            clock += [down_far, up_far]
        out = call(
            clock, part(self_backward, p, p if p < packs - 1 else 0), lens,
            pair(rows, features) + [((3, features, width), F32)],
            self_scratch + back_spec + saved_spec + [((4,) + full, BF16), ((4, rows, width), BF16), pltpu.SemaphoreType.DMA((13,))], 7.0 if p else 20.0,
            *self_grads[p], *saved[p], *xs, w_self, *carried, aliases=((-1, 2),) if p else (), any_ins=range(13),
        )
        carried = out[2:]
        row_sums.append(out[:2])
    row_even, row_odd = stacked(row_sums)
    row_near = hop(row_odd, 1)
    row_far = hop(add(row_even[:, 1], row_near[:, 1]), 2)
    input_grads = [
        encs[p][0] + row_even[p, 0].astype(F32) + row_near[p, 0].astype(F32) + row_far[p].astype(F32)
        for p in every
    ]
    out_sum = add(out_keep, out_far)
    norm_at = 3 * width
    cross_sum = jnp.where(is_dec, out_sum[width:norm_at], memory_sent)
    out_sum = jnp.concatenate([out_sum[:width], cross_sum, out_sum[norm_at:]])
    up_grad = chain_sum(up_sum, chained)
    out_grad = chain_sum(out_sum, chained)
    qkv_grad = chain_sum(carried[0].astype(BF16), chained)
    norms = out_grad[norm_at:].astype(F32)

    picks = after([(decs[p][0], encoded[p]) for p in every], *clock)
    layer_rows = jnp.stack([jnp.where(is_dec, a, b) for a, b in picks])
    wide = lambda value: value.astype(F32)[None]
    input_grads = jnp.stack(input_grads)
    qkv_grad = after(qkv_grad, input_grads)
    return (
        layer_rows[None],
        input_grads[None],
        wide(qkv_grad),
        wide(out_grad[:width]),
        wide(up_grad),
        wide(down_grad),
        wide(out_grad[width : 2 * width].T),
        wide(out_grad[2 * width : norm_at].T),
        norms[0:2][None],
        norms[2:4][None],
        norms[4],
        norms[5],
    )


def solution(mesh):
    return jax.shard_map(
        body,
        mesh=mesh,
        in_specs=(
            P("section", "dp", "mp", None),
            P("dp", None),
            P("dp", None),
            P("section", None, None, "mp"),
            P("section", "mp", None),
            P("section", None, "mp"),
            P("section", "mp", None),
            P("section", None, "mp"),
            P("section", None, "mp"),
            P("section", None, None),
            P("section", None, None),
            P(),
            P(),
            P("dp", "mp", None),
        ),
        out_specs=(
            P("section", "dp", "mp", None),
            P("section", "dp", "mp", None),
            P("section", None, None, "mp"),
            P("section", "mp", None),
            P("section", None, "mp"),
            P("section", "mp", None),
            P("section", None, "mp"),
            P("section", None, "mp"),
            P("section", None, None),
            P("section", None, None),
            P(),
            P(),
        ),
        check_vma=False,
    )
```

```python
import functools

import jax
import jax.numpy as jnp
from jax import lax
from jax.experimental import pallas as pl
from jax.experimental.pallas import tpu as pltpu
from jax.sharding import PartitionSpec as P

HD = 64
EPS = 1e-05
NEG = -1000000000.0
F32 = jnp.float32
BF16 = jnp.bfloat16
QC = 512
COST = 6e8
SCOPED = 14 * 1024 * 1024


def nn(left, right):
    return lax.dot_general(left, right, (((1,), (0,)), ((), ())), preferred_element_type=F32)


def nt(left, right):
    return lax.dot_general(left, right, (((1,), (1,)), ((), ())), preferred_element_type=F32)


def tn(left, right):
    return lax.dot_general(left, right, (((0,), (0,)), ((), ())), preferred_element_type=F32)


def hop(value, distance):
    count = lax.axis_size("mp")
    return lax.ppermute(value, "mp", [(i, i ^ distance) for i in range(count)])


def gather(own):
    even = jnp.stack([own, hop(own, 2)])
    return even, hop(even, 1)


def exchange(blocks):
    return [blocks[0]] + [hop(blocks[r], r) for r in range(1, 4)]


def after(value, *earlier):
    return lax.optimization_barrier((value, earlier))[0]


def reduce_rows(even, odd):
    near = hop(odd, 1)
    far = hop((even[1].astype(F32) + near[1].astype(F32)).astype(BF16), 2)
    return even[0].astype(F32) + near[0].astype(F32) + far.astype(F32)


def section_send(value, source):
    return lax.ppermute(value, "section", [(source, 1 - source)])


def chain_sum(values, earlier):
    count = lax.axis_size("dp")
    if count == 1:
        return values
    if count % 2:
        return lax.psum(values, "dp")
    index = lax.axis_index("dp")
    middle = count // 2
    pairs = [[(i, i + 1), (count - 1 - i, count - 2 - i)] for i in range(middle - 1)]
    for k, step in enumerate(pairs + [[(middle - 1, middle), (middle, middle - 1)]]):
        moved = lax.ppermute(after(values, *earlier) if k == 0 else values, "dp", step)
        if k == 0:
            earlier[:] = [moved]
        values = (values.astype(F32) + moved.astype(F32)).astype(BF16)
    for i in reversed(range(middle - 1)):
        moved = lax.ppermute(values, "dp", [(b, a) for a, b in pairs[i]])
        values = jnp.where((index == i) | (index == count - 1 - i), moved, values)
    return values


def blocks_of(even, odd):
    return even.at[0], odd.at[0], even.at[1], odd.at[1]


def pack_layout(lengths, pack, sentences):
    ends, start, largest, top, end = [], 0, 0, 0, 0
    for j in range(sentences):
        size = lengths[pack, j]
        better = size > top
        start = jnp.where(better, end, start)
        largest = jnp.where(better, j, largest)
        top = jnp.where(better, size, top)
        end = end + size
        ends.append(end)
    return ends, start, largest


def segment_ids(ends, shift, first, shape, dim, total):
    at = lax.broadcasted_iota(jnp.int32, shape, dim) + (first + shift)
    at = jnp.where(at >= total, at - total, at)
    return sum(jnp.where(at >= end, 1, 0) for end in ends)


def center_rows(total):
    center = jnp.mean(total, axis=-1, keepdims=True)
    centred = total - center
    inverse = lax.rsqrt(jnp.mean(centred * centred, axis=-1, keepdims=True) + EPS)
    return centred * inverse, inverse


def norm_back(grad, scaled, inverse, gain):
    inner = grad * gain
    first = jnp.mean(inner, axis=-1, keepdims=True)
    second = jnp.mean(inner * scaled, axis=-1, keepdims=True)
    return (
        inverse * (inner - first - scaled * second),
        jnp.sum(grad * scaled, axis=0, keepdims=True),
        jnp.sum(grad, axis=0, keepdims=True),
    )


def place(roll, slot, me, block, rows, value):
    count = roll.shape[1] // 2
    start = pl.multiple_of((me ^ block) * rows, rows)
    roll[slot, pl.ds(start, rows), :] = value
    roll[slot, pl.ds(start + count, rows), :] = value


def rolled(roll, slot, shift, half, size):
    return roll[slot, pl.ds(shift + half * size, size), :]


def unroll_into(roll, slot, shift, source, half):
    roll[slot, pl.ds(shift + half, half), :] = source[0:half, :]
    roll[slot, pl.ds(shift + 2 * half, half), :] = source[half : 2 * half, :]
    roll[slot, pl.ds(shift, half), :] = source[half : 2 * half, :]


def unrolled(roll, slot, me, block, rows, half):
    return roll[slot, pl.ds(pl.multiple_of(half + (me ^ block) * rows, rows), rows), :]


def head_masks(width):
    lane = lax.broadcasted_iota(jnp.int32, (1, width), 1)
    return [
        jnp.where((lane >= h * HD) & (lane < (h + 1) * HD), 1.0, 0.0).astype(BF16)
        for h in range(width // HD)
    ]


def attend_chunk(keys, values, query, bias, masks):
    tops, sums, outs = [], [], []
    for h, mask in enumerate(masks):
        scores = nt(keys, query * mask) + bias
        top = jnp.max(scores, axis=0, keepdims=True)
        raised = jnp.exp(scores - top)
        total = jnp.sum(raised, axis=0, keepdims=True)
        mixed = tn(values, raised.astype(BF16))
        outs.append(mixed[h * HD : (h + 1) * HD, :] / total)
        sums.append(top + jnp.log(total))
    return jnp.concatenate(outs, axis=0).T, sums


def attend_back_chunk(keys, values, query, grad, out, lse, bias, masks):
    folded = (grad.astype(F32) * out).T
    grad_query = []
    probs, grads = [], []
    for h, mask in enumerate(masks):
        scores = nt(keys, query * mask) + bias
        prob = jnp.exp(scores - lse[h])
        grad_prob = nt(values, grad * mask)
        inner = jnp.sum(folded[h * HD : (h + 1) * HD, :], axis=0, keepdims=True)
        grad_score = (prob * (grad_prob - inner)).astype(BF16)
        probs.append(prob.astype(BF16))
        grads.append(grad_score)
        grad_query.append(tn(keys, grad_score)[h * HD : (h + 1) * HD, :])
    grad_keys = sum(nn(g, query * m) for g, m in zip(grads, masks))
    grad_values = sum(nn(p, grad * m) for p, m in zip(probs, masks))
    return jnp.concatenate(grad_query, axis=0).T * (HD ** (-0.5)), grad_keys, grad_values


def self_bias(is_dec, ends, shift, bias, h, c, half):
    key = lax.broadcasted_iota(jnp.int32, (half, QC), 0)
    query = lax.broadcasted_iota(jnp.int32, (half, QC), 1) + c * QC
    key_ids = segment_ids(ends, shift, h * half, (half, 1), 0, 2 * half)
    query_ids = segment_ids(ends, shift, h * half + c * QC, (1, QC), 1, 2 * half)
    allowed = ((key <= query) | (is_dec == 0)) & (key_ids == query_ids)
    bias[...] = jnp.where(allowed, 0.0, NEG)


def cross_bias(source, target, first_key, first_query, size, bias, half):
    key_ids = segment_ids(source[0], source[1], first_key, (size, 1), 0, 2 * half)
    query_ids = segment_ids(target[0], target[1], first_query, (1, QC), 1, 2 * half)
    bias[0:size, :] = jnp.where(key_ids == query_ids, 0.0, NEG)


def place_of():
    return lax.axis_index("section"), lax.axis_index("mp")


def own_layout(source, target, is_dec, pack):
    sentences = source.shape[1]
    first, second = pack_layout(source, pack, sentences), pack_layout(target, pack, sentences)
    return [jnp.where(is_dec == 1, b, a) for a, b in zip(first[0], second[0])], jnp.where(
        is_dec == 1, second[1], first[1]
    )


def self_forward(
    pack, source, target, x0, x1, x2, x3, weights,
    o0, o1, o2, o3, query, keys, values, lse, outs, roll, bias,
):
    is_dec, me = place_of()
    ends, shift = own_layout(source, target, is_dec, pack)
    rows = x0.shape[1]
    half = 2 * rows
    for block, x in enumerate((x0, x1, x2, x3)):
        for slot in range(3):
            value = nn(x[pack], weights[slot])
            if slot == 0:
                value = value.astype(BF16).astype(F32) * (HD ** (-0.5))
            place(roll, slot, me, block, rows, value)
    for h in range(2):
        part = slice(h * half, (h + 1) * half)
        query[part, :] = rolled(roll, 0, shift, h, half).astype(BF16)
        keys[part, :] = rolled(roll, 1, shift, h, half).astype(BF16)
        values[part, :] = rolled(roll, 2, shift, h, half).astype(BF16)
    masks = head_masks(query.shape[1])
    chunks = half // QC

    def step(i, carry):
        h, c = i // chunks, i % chunks
        at = pl.multiple_of(i * QC, QC)
        part = pl.ds(pl.multiple_of(h * half, half), half)
        self_bias(is_dec, ends, shift, bias, h, c, half)
        out, sums = attend_chunk(
            keys[part, :],
            values[part, :],
            query[pl.ds(at, QC), :],
            bias[...],
            masks,
        )
        outs[pl.ds(at, QC), :] = out
        for k, row in enumerate(sums):
            lse[k : k + 1, pl.ds(at, QC)] = row
        return carry

    lax.fori_loop(0, 2 * chunks, step, 0)
    unroll_into(roll, 0, shift, outs, half)
    for block, o in enumerate((o0, o1, o2, o3)):
        o[...] = unrolled(roll, 0, me, block, rows, half).astype(BF16)


def self_backward(
    pack, at_grad, source, target, *refs,
):
    given, saved, xs, weights, rest = refs[:4], refs[4:9], refs[9:13], refs[13], refs[14:]
    sum_even, sum_odd, total, roll, bias, grads, grad_out, query, keys, values, lse, outs, x, g, arrived = rest[-15:]
    copies = [
        pltpu.make_async_copy(a, b, arrived.at[k])
        for k, (a, b) in enumerate(
            [(a.at[at_grad], g.at[k]) for k, a in enumerate(given)]
            + [*zip(saved, (query, keys, values, lse, outs))]
            + [(a.at[pack], x.at[k]) for k, a in enumerate(xs)]
        )
    ]
    for copy in copies:
        copy.start()
    is_dec, me = place_of()
    ends, shift = own_layout(source, target, is_dec, pack)
    rows = x.shape[1]
    half = 2 * rows
    for copy in copies[:4]:
        copy.wait()
    for block in range(4):
        place(roll, 0, me, block, rows, g[block].astype(F32))
    for h in range(2):
        grad_out[h * half : (h + 1) * half, :] = rolled(roll, 0, shift, h, half).astype(BF16)
    for copy in copies[4:9]:
        copy.wait()
    masks = head_masks(query.shape[1])
    chunks = half // QC
    grads[1] = jnp.zeros(grads.shape[1:], F32)
    grads[2] = jnp.zeros(grads.shape[1:], F32)

    def step(i, carry):
        h, c = i // chunks, i % chunks
        at = pl.ds(pl.multiple_of(i * QC, QC), QC)
        part = pl.ds(pl.multiple_of(h * half, half), half)
        self_bias(is_dec, ends, shift, bias, h, c, half)
        dq, dk, dv = attend_back_chunk(
            keys[part, :],
            values[part, :],
            query[at, :],
            grad_out[at, :],
            outs[at, :],
            [lse[k : k + 1, at] for k in range(len(masks))],
            bias[...],
            masks,
        )
        grads[0, at, :] = dq
        grads[1, part, :] += dk
        grads[2, part, :] += dv
        return carry

    lax.fori_loop(0, 2 * chunks, step, 0)
    for slot in range(3):
        unroll_into(roll, slot, shift, grads.at[slot], half)
    for copy in copies[9:]:
        copy.wait()
    sums = blocks_of(sum_even, sum_odd)
    for block in range(4):
        parts = [
            unrolled(roll, slot, me, block, rows, half).astype(BF16) for slot in range(3)
        ]
        sums[block][...] = sum(nt(parts[slot], weights[slot]) for slot in range(3)).astype(BF16)
        for slot in range(3):
            grad = tn(x[block], parts[slot])
            before = rest[0] if block == 0 else total
            total[slot] = grad if pack == 0 and block == 0 else before[slot] + grad


def cross_forward(
    pack, source, target, q0, q1, q2, q3, even, odd, weights,
    o0, o1, o2, o3, query, keys, values, lse, outs, roll, bias,
):
    is_dec, me = place_of()

    @pl.when(is_dec == 1)
    def _():
        sentences = source.shape[1]
        source_ends, source_shift, source_big = pack_layout(source, pack, sentences)
        ends, shift, big = pack_layout(target, pack, sentences)
        rows = even.shape[1]
        half = 2 * rows
        own_keys = pl.multiple_of(jnp.where(source_big == big, 0, half), half)
        source_at, target_at = (source_ends, source_shift), (ends, shift)
        for block, (q, e) in enumerate(zip((q0, q1, q2, q3), blocks_of(even, odd))):
            place(roll, 0, me, block, rows, q[pack].astype(F32) * (HD ** (-0.5)))
            place(roll, 1, me, block, rows, nn(e[...], weights[0]))
            place(roll, 2, me, block, rows, nn(e[...], weights[1]))
        for h in range(2):
            part = slice(h * half, (h + 1) * half)
            query[part, :] = rolled(roll, 0, shift, h, half).astype(BF16)
            keys[part, :] = rolled(roll, 1, source_shift, h, half).astype(BF16)
            values[part, :] = rolled(roll, 2, source_shift, h, half).astype(BF16)
        masks = head_masks(query.shape[1])

        def run(i, kind, key_rows):
            at = pl.multiple_of(kind * half + i * QC, QC)
            cross_bias(source_at, target_at, key_rows.start, at, key_rows.size, bias, half)
            out, sums = attend_chunk(
                keys[key_rows, :],
                values[key_rows, :],
                query[pl.ds(at, QC), :],
                bias[0 : key_rows.size, :],
                masks,
            )
            outs[pl.ds(at, QC), :] = out
            for k, row in enumerate(sums):
                lse[k : k + 1, pl.ds(at, QC)] = row

        def step(i, carry):
            run(i, 0, pl.ds(own_keys, half))
            run(i, 1, pl.ds(0, 2 * half))
            return carry

        lax.fori_loop(0, half // QC, step, 0)
        unroll_into(roll, 0, shift, outs, half)
        for block, o in enumerate((o0, o1, o2, o3)):
            o[...] = unrolled(roll, 0, me, block, rows, half).astype(BF16)


def cross_backward(
    pack, source, target, g0, g1, g2, g3, query, keys, values, lse, outs, even, odd, weights, *rest,
):
    c0, c1, c2, c3, sum_even, sum_odd, total, roll, bias, grads, grad_out = rest[-11:]
    is_dec, me = place_of()

    @pl.when(is_dec == 1)
    def _():
        sentences = source.shape[1]
        source_ends, source_shift, source_big = pack_layout(source, pack, sentences)
        ends, shift, big = pack_layout(target, pack, sentences)
        rows = even.shape[1]
        half = 2 * rows
        own_keys = pl.multiple_of(jnp.where(source_big == big, 0, half), half)
        source_at, target_at = (source_ends, source_shift), (ends, shift)
        for block, g in enumerate((g0, g1, g2, g3)):
            place(roll, 0, me, block, rows, g[...].astype(F32))
        for h in range(2):
            grad_out[h * half : (h + 1) * half, :] = rolled(roll, 0, shift, h, half).astype(BF16)
        masks = head_masks(query.shape[1])
        grads[1] = jnp.zeros(grads.shape[1:], F32)
        grads[2] = jnp.zeros(grads.shape[1:], F32)

        def run(i, kind, key_rows):
            at = pl.ds(pl.multiple_of(kind * half + i * QC, QC), QC)
            cross_bias(source_at, target_at, key_rows.start, at.start, key_rows.size, bias, half)
            dq, dk, dv = attend_back_chunk(
                keys[key_rows, :],
                values[key_rows, :],
                query[at, :],
                grad_out[at, :],
                outs[at, :],
                [lse[k : k + 1, at] for k in range(len(masks))],
                bias[0 : key_rows.size, :],
                masks,
            )
            grads[0, at, :] = dq
            grads[1, key_rows, :] += dk
            grads[2, key_rows, :] += dv

        def step(i, carry):
            run(i, 0, pl.ds(own_keys, half))
            run(i, 1, pl.ds(0, 2 * half))
            return carry

        lax.fori_loop(0, half // QC, step, 0)
        unroll_into(roll, 0, shift, grads.at[0], half)
        unroll_into(roll, 1, source_shift, grads.at[1], half)
        unroll_into(roll, 2, source_shift, grads.at[2], half)
        sums = blocks_of(sum_even, sum_odd)
        query_grads = (c0, c1, c2, c3)
        if pack:
            for old, new in zip(rest, query_grads):
                new[0:pack] = old[0:pack]
        for block, e in enumerate(blocks_of(even, odd)):
            parts = [
                unrolled(roll, slot, me, block, rows, half).astype(BF16) for slot in range(3)
            ]
            query_grads[block][pack] = parts[0]
            sums[block][...] = (nt(parts[1], weights[0]) + nt(parts[2], weights[1])).astype(BF16)
            for slot in range(2):
                grad = tn(parts[slot + 1], e[...])
                before = rest[4] if block == 0 else total
                total[slot] = grad if pack == 0 and block == 0 else before[slot] + grad


def silu_parts(hidden):
    gate = 1.0 / (1.0 + jnp.exp(-hidden))
    return hidden * gate, gate


def split_weights(stacked):
    width = stacked.shape[0] - 2 * stacked.shape[1]
    inner = (stacked.shape[0] - width) // 2
    return pl.ds(0, width), pl.ds(width, inner), pl.ds(width + inner, inner)


def silu_slope(hidden, value, gate):
    return gate + value * (1.0 - gate)


def ffn_forward(normed, shares, out, kept=None, slopes=None):
    _, up, down = split_weights(shares[0])
    for k, share in enumerate(shares):
        hidden = nn(normed, share[up, :])
        value, gate = silu_parts(hidden)
        low = value.astype(BF16)
        if kept is not None:
            kept[k] = low
            slopes[k] = silu_slope(hidden, value, gate)
        part = nn(low, share[down, :])
        out[...] = part if k == 0 else out[...] + part


def ffn_backward(normed, grad, shares, kept, grad_kept, out, slopes=None):
    _, up, down = split_weights(shares[0])
    for k, share in enumerate(shares):
        if slopes is None:
            hidden = nn(normed, share[up, :])
            value, gate = silu_parts(hidden)
            kept[k] = value.astype(BF16)
            slope = silu_slope(hidden, value, gate)
        else:
            slope = slopes[k]
        grad_pre = (nt(grad, share[down, :]) * slope).astype(BF16)
        grad_kept[k] = grad_pre
        part = nt(grad_pre, share[up, :])
        out[...] = part if k == 0 else out[...] + part


def after_self(
    packs, m0, m1, m2, m3, x, w0, w1, w2, w3, gains, biases,
    scaled, inverse, low, scaled_two, inverse_two, *rest,
):
    encoded, work = rest[:packs], rest[packs]
    is_dec, _ = place_of()
    shares = (w0, w1, w2, w3)
    rows = split_weights(shares[0])[0]
    flat = lambda ref: jnp.concatenate([ref[p] for p in range(packs)], axis=0)
    total = flat(x).astype(F32)
    for mixed, share in zip((m0, m1, m2, m3), shares):
        total = total + nn(flat(mixed), share[rows, :])
    first_scaled, first_inverse = center_rows(total)
    scaled[...] = first_scaled
    inverse[...] = first_inverse
    low[...] = (first_scaled * gains[0:1, :] + biases[0:1, :]).astype(BF16)

    @pl.when(is_dec == 0)
    def _():
        ffn_forward(low[...], shares, work)
        again = scaled[...] * gains[0:1, :] + biases[0:1, :]
        second_scaled, second_inverse = center_rows(again + work[...])
        scaled_two[...] = second_scaled
        inverse_two[...] = second_inverse
        result = (second_scaled * gains[1:2, :] + biases[1:2, :]).astype(BF16)
        size = result.shape[0] // packs
        for p in range(packs):
            encoded[p][...] = result[p * size : (p + 1) * size, :]


def cross_queries(packs, low, ka, kb, *queries):
    @pl.when(place_of()[0] == 1)
    def _():
        size = low.shape[0] // packs
        for query, share in zip(queries, blocks_of(ka, kb)):
            result = nn(low[...], share[0]).astype(BF16)
            for p in range(packs):
                query[p] = result[p * size : (p + 1) * size, :]


def after_cross(
    pack, target, m0, m1, m2, m3, scaled, w0, w1, w2, w3, ka, kb,
    gains, biases, cross_gain, cross_shift, cotangent,
    decoded, low, grad_low, hidden, grad_hidden, out_low, g0, g1, g2, g3, grad_two, norms, work, kept, slopes,
):
    is_dec, me = place_of()

    @pl.when(is_dec == 1)
    def _():
        shares, crosses = (w0, w1, w2, w3), blocks_of(ka, kb)
        rows = decoded.shape[0]
        total = scaled[pl.ds(pack * rows, rows), :] * gains[0:1, :] + biases[0:1, :]
        for mixed, share in zip((m0, m1, m2, m3), crosses):
            total = total + nt(mixed[...], share[1])
        second_scaled, second_inverse = center_rows(total)
        kept[...] = second_scaled
        low[...] = (second_scaled * cross_gain[...] + cross_shift[...]).astype(BF16)
        ffn_forward(low[...], shares, work, hidden, slopes)
        second = kept[...] * cross_gain[...] + cross_shift[...]
        third_scaled, third_inverse = center_rows(second + work[...])
        decoded[...] = (third_scaled * gains[1:2, :] + biases[1:2, :]).astype(BF16)
        at = lax.broadcasted_iota(jnp.int32, (rows, 1), 0) + me * rows
        end = pack_layout(target, pack, target.shape[1])[0][-1]
        grad = jnp.where(at < end, cotangent[pack].astype(F32), 0.0)
        grad_third, gain_two, bias_two = norm_back(grad, third_scaled, third_inverse, gains[1:2, :])
        grad_low[...] = grad_third.astype(BF16)
        grad_two[...] = grad_third
        ffn_backward(low[...], grad_low[...], shares, hidden, grad_hidden, work, slopes)
        grad_second, cross_gain_grad, cross_bias_grad = norm_back(
            grad_two[...] + work[...], kept[...], second_inverse, cross_gain[...]
        )
        grad_two[...] = grad_second
        out_low[...] = grad_second.astype(BF16)
        for g, share in zip((g0, g1, g2, g3), crosses):
            g[...] = nn(out_low[...], share[1]).astype(BF16)
        norms[...] = jnp.zeros(norms.shape, F32)
        norms[1:2, :] = gain_two
        norms[3:4, :] = bias_two
        norms[4:5, :] = cross_gain_grad
        norms[5:6, :] = cross_bias_grad


def before_self(
    pack, scaled, inverse, low, gains, w0, w1, w2, w3, ka, kb, grad_encoded, scaled_two, inverse_two,
    c0, c1, c2, c3, grad_two, norms_in, in_low_old, grad_low_old, hidden_old, grad_hidden_old,
    grad_rows, out_low, g0, g1, g2, g3, norms, in_low, grad_low, hidden, grad_hidden, work,
):
    is_dec, _ = place_of()
    size = grad_rows.shape[0]
    own = pl.ds(pack * size, size)
    shares = (w0, w1, w2, w3)
    rows = split_weights(shares[0])[0]

    @pl.when(is_dec == 0)
    def _():
        grad_sum, gain_two, bias_two = norm_back(
            grad_encoded[pl.ds(0, size), :].astype(F32), scaled_two[own, :], inverse_two[own, :], gains[1:2, :]
        )
        in_low[...] = low[own, :]
        grad_low[...] = grad_sum.astype(BF16)
        grad_rows[...] = grad_sum
        ffn_backward(low[own, :], grad_low[...], shares, hidden, grad_hidden, work)
        work[...] += grad_rows[...]
        norms[...] = jnp.zeros(norms.shape, F32)
        norms[1:2, :] = gain_two
        norms[3:4, :] = bias_two

    @pl.when(is_dec == 1)
    def _():
        total = grad_two[...]
        for grad, share in zip((c0, c1, c2, c3), blocks_of(ka, kb)):
            total = total + nt(grad[pack], share[0])
        work[...] = total
        norms[...] = norms_in[...]
        in_low[...] = in_low_old[...]
        grad_low[...] = grad_low_old[...]
        hidden[...] = hidden_old[...]
        grad_hidden[...] = grad_hidden_old[...]

    grad_first, gain_one, bias_one = norm_back(work[...], scaled[own, :], inverse[own, :], gains[0:1, :])
    norms[0:1, :] = gain_one
    norms[2:3, :] = bias_one
    grad_rows[...] = grad_first
    out_low[...] = grad_first.astype(BF16)
    for g, share in zip((g0, g1, g2, g3), shares):
        g[...] = nt(out_low[...], share[rows, :]).astype(BF16)


def pair_sums(even, near, keep, send):
    keep[...] = (even[0].astype(F32) + near[0].astype(F32)).astype(BF16)
    send[...] = (even[1].astype(F32) + near[1].astype(F32)).astype(BF16)


def ffn_grads(packs, *refs):
    inputs, hiddens, grads, grad_hiddens = [refs[i * packs : (i + 1) * packs] for i in range(4)]
    up_even, up_odd, down_even, down_odd = refs[4 * packs :]
    ups, downs = blocks_of(up_even, up_odd), blocks_of(down_even, down_odd)
    for k in range(4):
        downs[k][...] = sum(tn(h[k], g[...]) for h, g in zip(hiddens, grads)).astype(BF16)
        ups[k][...] = sum(tn(x[...], h[k]) for x, h in zip(inputs, grad_hiddens)).astype(BF16)


def projection_grads(packs, *refs):
    is_dec, _ = place_of()
    take = lambda count: [refs.pop(0) for _ in range(count)]
    refs = list(refs)
    mixes, crosses = take(4), [take(4) for _ in range(packs)]
    queries = take(4)
    outs, cross_outs, norms = take(packs), take(packs), take(packs)
    low, received = take(2)
    size = outs[0].shape[0]
    targets = blocks_of(*take(2))
    width = mixes[0][0].shape[1]
    part = lambda k: pl.ds(k * width, width)
    sums = sum(n[...] for n in norms)
    row = lax.broadcasted_iota(jnp.int32, sums.shape, 0)
    from_cross = (is_dec == 0) & ((row == 4) | (row == 5))
    sums = jnp.where(from_cross, received[pl.ds(received.shape[0] - sums.shape[0], sums.shape[0]), :].astype(F32), sums).astype(BF16)
    for k in range(4):
        targets[k][part(0), :] = sum(
            tn(mixes[k][p], g[...]) for p, g in enumerate(outs)
        ).astype(BF16)
        targets[k][pl.ds(3 * width, sums.shape[0]), :] = sums

    @pl.when(is_dec == 1)
    def _():
        for k in range(4):
            targets[k][part(1), :] = sum(
                tn(queries[k][p], low[pl.ds(p * size, size), :]) for p in range(packs)
            ).astype(BF16)
            targets[k][part(2), :] = sum(
                tn(c[k][...], g[...]) for g, c in zip(cross_outs, crosses)
            ).astype(BF16)


def call(clock, kernel, scalars, outs, scratch, micros, *operands, aliases=(), far_outs=(), any_ins=()):
    space = pl.BlockSpec(memory_space=pltpu.VMEM)
    operands = after(operands, *clock)
    operands = [
        pltpu.with_memory_space_constraint(x, pltpu.HBM if i in any_ins else pltpu.VMEM)
        for i, x in enumerate(operands)
    ]
    results = pl.pallas_call(
        kernel,
        out_shape=[
            pltpu.HBM(shape, kind) if i in far_outs else pltpu.VMEM(shape, kind)
            for i, (shape, kind) in enumerate(outs)
        ],
        in_specs=[pl.BlockSpec(memory_space=pltpu.SMEM)] * len(scalars) + [pl.BlockSpec(memory_space=pl.ANY) if i in any_ins else space for i in range(len(operands))],
        out_specs=[space] * len(outs),
        scratch_shapes=[pltpu.VMEM(*item) if isinstance(item, tuple) else item for item in scratch],
        input_output_aliases={len(scalars) + len(operands) + a: b for a, b in aliases},
        compiler_params=pltpu.CompilerParams(vmem_limit_bytes=SCOPED),
        cost_estimate=pl.CostEstimate(
            flops=int(micros * COST), bytes_accessed=1, transcendentals=0
        ),
    )(*scalars, *operands)
    clock[:] = [results[0]]
    return results


def body(
    embeddings, src_len, tgt_len, attn_in, attn_out, ffn_in, ffn_out, cross_a, cross_b,
    norm_gain, norm_bias, cross_gain, cross_bias_vec, cotangent,
):
    is_dec = lax.axis_index("section") == 1
    x_all = embeddings[0]
    packs, rows, features = x_all.shape
    total_rows = rows * lax.axis_size("mp")
    half = total_rows // 2
    width = attn_in.shape[3]
    hidden = ffn_in.shape[2]
    gains, biases = norm_gain[0], norm_bias[0]
    cgain, cbias = cross_gain[None, :], cross_bias_vec[None, :]
    lens = (src_len, tgt_len)
    every = range(packs)
    w_self = attn_in[0]
    share = jnp.concatenate([attn_out[0], ffn_in[0], ffn_out[0]], axis=0)
    cross_share = jnp.stack([cross_a[0], cross_b[0]])

    clock = []
    x_far = hop(x_all, 2)
    xs = (x_all, hop(x_all, 1), x_far, hop(x_far, 1))
    cross_share = after(cross_share, x_far)
    memory_weights = section_send(cross_share, 0)
    share_far = hop(after(share, x_far), 2)
    share_near = hop(after(share, xs[3]), 1)

    pair = lambda *tail: [((2,) + tail, BF16)] * 2
    saved_spec = [((total_rows, width), BF16)] * 3 + [((8, total_rows), F32), ((total_rows, width), F32)]
    roll_spec = ((3, 2 * total_rows, width), F32)
    back_spec = [((3, total_rows, width), F32), ((total_rows, width), BF16)]
    full = (rows, features)
    column = ((rows, 1), F32)
    hid_spec = ((4, rows, hidden), BF16)
    self_scratch = [roll_spec, ((half, QC), F32)]
    cross_scratch = [roll_spec, ((total_rows, QC), F32)]
    part = functools.partial

    blocks = [((rows, width), BF16)] * 4
    blocks = [((rows, width), BF16)] * 4
    stacked = lambda outs: [jnp.stack(block) for block in zip(*outs)]
    saved, mixes = [], []
    for p in every:
        if p == 1:
            clock += [share_near, memory_weights]
        out = call(
            clock, part(self_forward, p), lens, blocks + saved_spec, self_scratch, 5.0, *xs, w_self,
            far_outs=range(4, 9),
        )
        mixes.append(out[:4])
        saved.append(out[4:])
    mixes = exchange(stacked(mixes))
    share_far, cross_share = after((share_far, cross_share), clock[0], mixes[1])
    shares = (share, share_near, share_far, hop(share_far, 1))
    cross_far = hop(cross_share, 2)

    tall = (packs * rows, features)
    tall_column = ((packs * rows, 1), F32)
    out = call(
        clock, part(after_self, packs), (),
        [(tall, F32), tall_column, (tall, BF16), (tall, F32), tall_column] + [(full, BF16)] * packs,
        [(tall, F32)], 7.0,
        *mixes, x_all, *shares, gains, biases,
    )
    firsts, encoded = out[:5], out[5:]
    arrived = [section_send(e, 0) for e in encoded]
    cross_even = jnp.stack([cross_share, cross_far])
    cross_shares = (cross_even, hop(cross_even, 1))
    queries = exchange(call(
        clock, part(cross_queries, packs), (), [((packs, rows, width), BF16)] * 4, [], 2.0,
        firsts[2], *cross_shares,
    ))
    memory_far = [hop(x, 2) for x in arrived]

    cross_saved, cross_mixes, memories = [], [], []
    clock += arrived[1:]
    for p in every:
        even = jnp.stack([arrived[p], after(memory_far[p], *clock) if p else memory_far[p]])
        memories.append((even, hop(even, 1)))
        out = call(
            clock, part(cross_forward, p), lens, blocks + saved_spec, cross_scratch, 6.0,
            *queries, *memories[p], memory_weights,
        )
        cross_mixes.append(exchange(out[:4]))
        cross_saved.append(out[4:])

    add = lambda a, b: (a.astype(F32) + b.astype(F32)).astype(BF16)
    decs, cross_grads, nears, fars, encoded_grads = [], [], [], [], []

    def run_after(p):
        out = call(
            clock, part(after_cross, p), (tgt_len,),
            [(full, BF16)] * 3 + [hid_spec] * 2 + [(full, BF16)] + blocks + [(full, F32), ((16, features), F32)],
            [(full, F32), (full, F32), ((4, rows, hidden), F32)], 14.0,
            *cross_mixes[p], firsts[0], *shares, *cross_shares, gains, biases, cgain, cbias, cotangent,
        )
        decs.append(out)
        cross_grads.append(exchange(out[6:10]))

    def run_cross(p, carried):
        out = call(
            clock, part(cross_backward, p), lens,
            [((packs, rows, width), BF16)] * 4 + pair(rows, features) + [((2, width, features), F32)],
            cross_scratch + back_spec, 14.0,
            *cross_grads[p], *cross_saved[p], *memories[p], memory_weights, *carried,
            aliases=((-5, 0), (-4, 1), (-3, 2), (-2, 3), (-1, 6)) if p else (),
        )
        nears.append(hop(out[5], 1))
        fars.append(hop(add(out[4][1], nears[-1][1]), 2))
        sent = add(add(out[4][0], nears[-1][0]), fars[-1])
        if p == packs - 1:
            sent = jnp.concatenate([sent, sum(d[11] for d in decs).astype(BF16)])
        encoded_grads.append(section_send(sent, 1))
        return (*out[:4], out[6])

    carried = ()
    for p in every:
        run_after(p)
        if p == packs - 2:
            carried = run_cross(0, carried)
    for p in range(1 if packs > 1 else 0, packs):
        clock += nears[:1] if p == 1 else fars[:1]
        carried = run_cross(p, carried)
    query_grads = exchange(after(carried[:4], fars[-1]))
    memory_sent = carried[4].astype(BF16).reshape(2 * width, features)

    encs, self_grads = [], []
    for p in every:
        out = call(
            clock, part(before_self, p), (),
            [(full, F32), (full, BF16)] + blocks + [((16, features), F32)]
            + [(full, BF16), (full, BF16), hid_spec, hid_spec],
            [(full, F32)], 4.0,
            firsts[0], firsts[1], firsts[2], gains, *shares, *cross_shares, encoded_grads[p],
            firsts[3], firsts[4], *query_grads, decs[p][10], decs[p][11],
            *decs[p][1:5], aliases=((-4, 7), (-3, 8), (-2, 9), (-1, 10)),
        )
        encs.append(out)
        if p == 0:
            memory_sent = section_send(after(memory_sent, out[0]), 1)
        self_grads.append(out[2:6])
        if p == packs - 2:
            early = exchange(stacked(self_grads))
    clock += early
    self_grads = [early] * (packs - 1) + [exchange(stacked(self_grads[-1:]))]
    up_even, up_odd, down_even, down_odd = call(
        clock, part(ffn_grads, packs), (), pair(features, hidden) + pair(hidden, features), [], 4.0,
        *[e[7] for e in encs], *[e[9] for e in encs], *[e[8] for e in encs], *[e[10] for e in encs],
    )
    down_near, up_near = hop(down_odd, 1), hop(up_odd, 1)

    def merged(even, near):
        return call([], pair_sums, (), [(even.shape[1:], BF16)] * 2, [], 0.5, even, near)

    down_keep, down_send = merged(down_even, down_near)
    up_keep, up_send = merged(up_even, up_near)
    down_far = hop(down_send, 2)
    down_sum = add(down_keep, down_far)
    up_far = hop(after(up_send, down_far), 2)
    up_sum = add(up_keep, up_far)
    chained = []
    down_grad = chain_sum(down_sum, chained)
    clock += [down_near, up_send]
    carried, row_sums = (), []
    for p in every:
        if p == 1:
            rest_rows = 3 * width + 16
            out_even, out_odd = call(
                clock, part(projection_grads, packs), (), pair(rest_rows, features), [], 2.0,
                *mixes, *sum(cross_mixes, []), *query_grads,
                *[e[1] for e in encs], *[d[5] for d in decs], *[e[6] for e in encs], firsts[2], encoded_grads[-1],
            )
            out_near = hop(out_odd, 1)
            out_keep, out_send = merged(out_even, out_near)
            out_far = hop(after(out_send, up_far), 2)
        if p == packs - 1:
            clock += [down_far, up_far, memory_sent]
        out = call(
            clock, part(self_backward, p, p if p < packs - 1 else 0), lens,
            pair(rows, features) + [((3, features, width), F32)],
            self_scratch + back_spec + saved_spec + [((4,) + full, BF16), ((4, rows, width), BF16), pltpu.SemaphoreType.DMA((13,))], 7.0,
            *self_grads[p], *saved[p], *xs, w_self, *carried, aliases=((-1, 2),) if p else (), any_ins=range(13),
        )
        carried = out[2:]
        row_sums.append(out[:2])
    row_even, row_odd = stacked(row_sums)
    row_near = hop(row_odd, 1)
    row_far = hop(add(row_even[:, 1], row_near[:, 1]), 2)
    input_grads = [
        encs[p][0] + row_even[p, 0].astype(F32) + row_near[p, 0].astype(F32) + row_far[p].astype(F32)
        for p in every
    ]
    out_sum = add(out_keep, out_far)
    norm_at = 3 * width
    cross_sum = jnp.where(is_dec, out_sum[width:norm_at], memory_sent)
    out_sum = jnp.concatenate([out_sum[:width], cross_sum, out_sum[norm_at:]])
    up_grad = chain_sum(up_sum, chained)
    out_grad = chain_sum(out_sum, chained)
    qkv_grad = chain_sum(carried[0].astype(BF16), chained)
    norms = out_grad[norm_at:].astype(F32)

    picks = after([(decs[p][0], encoded[p]) for p in every], *clock)
    layer_rows = jnp.stack([jnp.where(is_dec, a, b) for a, b in picks])
    wide = lambda value: value.astype(F32)[None]
    input_grads = jnp.stack(input_grads)
    qkv_grad = after(qkv_grad, input_grads)
    return (
        layer_rows[None],
        input_grads[None],
        wide(qkv_grad),
        wide(out_grad[:width]),
        wide(up_grad),
        wide(down_grad),
        wide(out_grad[width : 2 * width].T),
        wide(out_grad[2 * width : norm_at].T),
        norms[0:2][None],
        norms[2:4][None],
        norms[4],
        norms[5],
    )


def solution(mesh):
    return jax.shard_map(
        body,
        mesh=mesh,
        in_specs=(
            P("section", "dp", "mp", None),
            P("dp", None),
            P("dp", None),
            P("section", None, None, "mp"),
            P("section", "mp", None),
            P("section", None, "mp"),
            P("section", "mp", None),
            P("section", None, "mp"),
            P("section", None, "mp"),
            P("section", None, None),
            P("section", None, None),
            P(),
            P(),
            P("dp", "mp", None),
        ),
        out_specs=(
            P("section", "dp", "mp", None),
            P("section", "dp", "mp", None),
            P("section", None, None, "mp"),
            P("section", "mp", None),
            P("section", None, "mp"),
            P("section", "mp", None),
            P("section", None, "mp"),
            P("section", None, "mp"),
            P("section", None, None),
            P("section", None, None),
            P(),
            P(),
        ),
        check_vma=False,
    )
```

```python
import functools

import jax
import jax.numpy as jnp
from jax import lax
from jax.experimental import pallas as pl
from jax.experimental.pallas import tpu as pltpu
from jax.sharding import PartitionSpec as P

HD = 64
EPS = 1e-05
NEG = -1000000000.0
F32 = jnp.float32
BF16 = jnp.bfloat16
QC = 512
COST = 6e8
SCOPED = 14 * 1024 * 1024


def nn(left, right):
    return lax.dot_general(left, right, (((1,), (0,)), ((), ())), preferred_element_type=F32)


def nt(left, right):
    return lax.dot_general(left, right, (((1,), (1,)), ((), ())), preferred_element_type=F32)


def tn(left, right):
    return lax.dot_general(left, right, (((0,), (0,)), ((), ())), preferred_element_type=F32)


def hop(value, distance):
    count = lax.axis_size("mp")
    return lax.ppermute(value, "mp", [(i, i ^ distance) for i in range(count)])


def gather(own):
    even = jnp.stack([own, hop(own, 2)])
    return even, hop(even, 1)


def exchange(blocks):
    return [blocks[0]] + [hop(blocks[r], r) for r in range(1, 4)]


def after(value, *earlier):
    return lax.optimization_barrier((value, earlier))[0]


def reduce_rows(even, odd):
    near = hop(odd, 1)
    far = hop((even[1].astype(F32) + near[1].astype(F32)).astype(BF16), 2)
    return even[0].astype(F32) + near[0].astype(F32) + far.astype(F32)


def section_send(value, source):
    return lax.ppermute(value, "section", [(source, 1 - source)])


def chain_sum(values, earlier):
    count = lax.axis_size("dp")
    if count == 1:
        return values
    if count % 2:
        return lax.psum(values, "dp")
    index = lax.axis_index("dp")
    middle = count // 2
    pairs = [[(i, i + 1), (count - 1 - i, count - 2 - i)] for i in range(middle - 1)]
    for k, step in enumerate(pairs + [[(middle - 1, middle), (middle, middle - 1)]]):
        moved = lax.ppermute(after(values, *earlier) if k == 0 else values, "dp", step)
        if k == 0:
            earlier[:] = [moved]
        values = (values.astype(F32) + moved.astype(F32)).astype(BF16)
    for i in reversed(range(middle - 1)):
        moved = lax.ppermute(values, "dp", [(b, a) for a, b in pairs[i]])
        values = jnp.where((index == i) | (index == count - 1 - i), moved, values)
    return values


def blocks_of(even, odd):
    return even.at[0], odd.at[0], even.at[1], odd.at[1]


def pack_layout(lengths, pack, sentences):
    ends, start, largest, top, end = [], 0, 0, 0, 0
    for j in range(sentences):
        size = lengths[pack, j]
        better = size > top
        start = jnp.where(better, end, start)
        largest = jnp.where(better, j, largest)
        top = jnp.where(better, size, top)
        end = end + size
        ends.append(end)
    return ends, start, largest


def segment_ids(ends, shift, first, shape, dim, total):
    at = lax.broadcasted_iota(jnp.int32, shape, dim) + (first + shift)
    at = jnp.where(at >= total, at - total, at)
    return sum(jnp.where(at >= end, 1, 0) for end in ends)


def center_rows(total):
    center = jnp.mean(total, axis=-1, keepdims=True)
    centred = total - center
    inverse = lax.rsqrt(jnp.mean(centred * centred, axis=-1, keepdims=True) + EPS)
    return centred * inverse, inverse


def norm_back(grad, scaled, inverse, gain):
    inner = grad * gain
    first = jnp.mean(inner, axis=-1, keepdims=True)
    second = jnp.mean(inner * scaled, axis=-1, keepdims=True)
    return (
        inverse * (inner - first - scaled * second),
        jnp.sum(grad * scaled, axis=0, keepdims=True),
        jnp.sum(grad, axis=0, keepdims=True),
    )


def place(roll, slot, me, block, rows, value):
    count = roll.shape[1] // 2
    start = pl.multiple_of((me ^ block) * rows, rows)
    roll[slot, pl.ds(start, rows), :] = value
    roll[slot, pl.ds(start + count, rows), :] = value


def rolled(roll, slot, shift, half, size):
    return roll[slot, pl.ds(shift + half * size, size), :]


def unroll_into(roll, slot, shift, source, half):
    roll[slot, pl.ds(shift + half, half), :] = source[0:half, :]
    roll[slot, pl.ds(shift + 2 * half, half), :] = source[half : 2 * half, :]
    roll[slot, pl.ds(shift, half), :] = source[half : 2 * half, :]


def unrolled(roll, slot, me, block, rows, half):
    return roll[slot, pl.ds(pl.multiple_of(half + (me ^ block) * rows, rows), rows), :]


def head_masks(width):
    lane = lax.broadcasted_iota(jnp.int32, (1, width), 1)
    return [
        jnp.where((lane >= h * HD) & (lane < (h + 1) * HD), 1.0, 0.0).astype(BF16)
        for h in range(width // HD)
    ]


def attend_chunk(keys, values, query, bias, masks):
    tops, sums, outs = [], [], []
    for h, mask in enumerate(masks):
        scores = nt(keys, query * mask) + bias
        top = jnp.max(scores, axis=0, keepdims=True)
        raised = jnp.exp(scores - top)
        total = jnp.sum(raised, axis=0, keepdims=True)
        mixed = tn(values, raised.astype(BF16))
        outs.append(mixed[h * HD : (h + 1) * HD, :] / total)
        sums.append(top + jnp.log(total))
    return jnp.concatenate(outs, axis=0).T, sums


def attend_back_chunk(keys, values, query, grad, out, lse, bias, masks):
    folded = (grad.astype(F32) * out).T
    grad_query = []
    probs, grads = [], []
    for h, mask in enumerate(masks):
        scores = nt(keys, query * mask) + bias
        prob = jnp.exp(scores - lse[h])
        grad_prob = nt(values, grad * mask)
        inner = jnp.sum(folded[h * HD : (h + 1) * HD, :], axis=0, keepdims=True)
        grad_score = (prob * (grad_prob - inner)).astype(BF16)
        probs.append(prob.astype(BF16))
        grads.append(grad_score)
        grad_query.append(tn(keys, grad_score)[h * HD : (h + 1) * HD, :])
    grad_keys = sum(nn(g, query * m) for g, m in zip(grads, masks))
    grad_values = sum(nn(p, grad * m) for p, m in zip(probs, masks))
    return jnp.concatenate(grad_query, axis=0).T * (HD ** (-0.5)), grad_keys, grad_values


def self_bias(is_dec, ends, shift, bias, h, c, half):
    key = lax.broadcasted_iota(jnp.int32, (half, QC), 0)
    query = lax.broadcasted_iota(jnp.int32, (half, QC), 1) + c * QC
    key_ids = segment_ids(ends, shift, h * half, (half, 1), 0, 2 * half)
    query_ids = segment_ids(ends, shift, h * half + c * QC, (1, QC), 1, 2 * half)
    allowed = ((key <= query) | (is_dec == 0)) & (key_ids == query_ids)
    bias[...] = jnp.where(allowed, 0.0, NEG)


def cross_bias(source, target, first_key, first_query, size, bias, half):
    key_ids = segment_ids(source[0], source[1], first_key, (size, 1), 0, 2 * half)
    query_ids = segment_ids(target[0], target[1], first_query, (1, QC), 1, 2 * half)
    bias[0:size, :] = jnp.where(key_ids == query_ids, 0.0, NEG)


def place_of():
    return lax.axis_index("section"), lax.axis_index("mp")


def own_layout(source, target, is_dec, pack):
    sentences = source.shape[1]
    first, second = pack_layout(source, pack, sentences), pack_layout(target, pack, sentences)
    return [jnp.where(is_dec == 1, b, a) for a, b in zip(first[0], second[0])], jnp.where(
        is_dec == 1, second[1], first[1]
    )


def self_forward(
    pack, source, target, x0, x1, x2, x3, weights,
    o0, o1, o2, o3, query, keys, values, lse, outs, roll, bias,
):
    is_dec, me = place_of()
    ends, shift = own_layout(source, target, is_dec, pack)
    rows = x0.shape[1]
    half = 2 * rows
    for block, x in enumerate((x0, x1, x2, x3)):
        for slot in range(3):
            value = nn(x[pack], weights[slot])
            if slot == 0:
                value = value.astype(BF16).astype(F32) * (HD ** (-0.5))
            place(roll, slot, me, block, rows, value)
    for h in range(2):
        part = slice(h * half, (h + 1) * half)
        query[part, :] = rolled(roll, 0, shift, h, half).astype(BF16)
        keys[part, :] = rolled(roll, 1, shift, h, half).astype(BF16)
        values[part, :] = rolled(roll, 2, shift, h, half).astype(BF16)
    masks = head_masks(query.shape[1])
    chunks = half // QC

    def step(i, carry):
        h, c = i // chunks, i % chunks
        at = pl.multiple_of(i * QC, QC)
        part = pl.ds(pl.multiple_of(h * half, half), half)
        self_bias(is_dec, ends, shift, bias, h, c, half)
        out, sums = attend_chunk(
            keys[part, :],
            values[part, :],
            query[pl.ds(at, QC), :],
            bias[...],
            masks,
        )
        outs[pl.ds(at, QC), :] = out
        for k, row in enumerate(sums):
            lse[k : k + 1, pl.ds(at, QC)] = row
        return carry

    lax.fori_loop(0, 2 * chunks, step, 0)
    unroll_into(roll, 0, shift, outs, half)
    for block, o in enumerate((o0, o1, o2, o3)):
        o[...] = unrolled(roll, 0, me, block, rows, half).astype(BF16)


def self_backward(
    pack, at_grad, source, target, *refs,
):
    given, saved, xs, weights, rest = refs[:4], refs[4:9], refs[9:13], refs[13], refs[14:]
    sum_even, sum_odd, total, roll, bias, grads, grad_out, query, keys, values, lse, outs, x, g, arrived = rest[-15:]
    copies = [
        pltpu.make_async_copy(a, b, arrived.at[k])
        for k, (a, b) in enumerate(
            [(a.at[at_grad], g.at[k]) for k, a in enumerate(given)]
            + [*zip(saved, (query, keys, values, lse, outs))]
            + [(a.at[pack], x.at[k]) for k, a in enumerate(xs)]
        )
    ]
    for copy in copies:
        copy.start()
    is_dec, me = place_of()
    ends, shift = own_layout(source, target, is_dec, pack)
    rows = x.shape[1]
    half = 2 * rows
    for copy in copies[:4]:
        copy.wait()
    for block in range(4):
        place(roll, 0, me, block, rows, g[block].astype(F32))
    for h in range(2):
        grad_out[h * half : (h + 1) * half, :] = rolled(roll, 0, shift, h, half).astype(BF16)
    for copy in copies[4:9]:
        copy.wait()
    masks = head_masks(query.shape[1])
    chunks = half // QC
    grads[1] = jnp.zeros(grads.shape[1:], F32)
    grads[2] = jnp.zeros(grads.shape[1:], F32)

    def step(i, carry):
        h, c = i // chunks, i % chunks
        at = pl.ds(pl.multiple_of(i * QC, QC), QC)
        part = pl.ds(pl.multiple_of(h * half, half), half)
        self_bias(is_dec, ends, shift, bias, h, c, half)
        dq, dk, dv = attend_back_chunk(
            keys[part, :],
            values[part, :],
            query[at, :],
            grad_out[at, :],
            outs[at, :],
            [lse[k : k + 1, at] for k in range(len(masks))],
            bias[...],
            masks,
        )
        grads[0, at, :] = dq
        grads[1, part, :] += dk
        grads[2, part, :] += dv
        return carry

    lax.fori_loop(0, 2 * chunks, step, 0)
    for slot in range(3):
        unroll_into(roll, slot, shift, grads.at[slot], half)
    for copy in copies[9:]:
        copy.wait()
    sums = blocks_of(sum_even, sum_odd)
    for block in range(4):
        parts = [
            unrolled(roll, slot, me, block, rows, half).astype(BF16) for slot in range(3)
        ]
        sums[block][...] = sum(nt(parts[slot], weights[slot]) for slot in range(3)).astype(BF16)
        for slot in range(3):
            grad = tn(x[block], parts[slot])
            before = rest[0] if block == 0 else total
            total[slot] = grad if pack == 0 and block == 0 else before[slot] + grad


def cross_forward(
    pack, source, target, q0, q1, q2, q3, even, odd, weights,
    o0, o1, o2, o3, query, keys, values, lse, outs, roll, bias,
):
    is_dec, me = place_of()

    @pl.when(is_dec == 1)
    def _():
        sentences = source.shape[1]
        source_ends, source_shift, source_big = pack_layout(source, pack, sentences)
        ends, shift, big = pack_layout(target, pack, sentences)
        rows = even.shape[1]
        half = 2 * rows
        own_keys = pl.multiple_of(jnp.where(source_big == big, 0, half), half)
        source_at, target_at = (source_ends, source_shift), (ends, shift)
        for block, (q, e) in enumerate(zip((q0, q1, q2, q3), blocks_of(even, odd))):
            place(roll, 0, me, block, rows, q[pack].astype(F32) * (HD ** (-0.5)))
            place(roll, 1, me, block, rows, nn(e[...], weights[0]))
            place(roll, 2, me, block, rows, nn(e[...], weights[1]))
        for h in range(2):
            part = slice(h * half, (h + 1) * half)
            query[part, :] = rolled(roll, 0, shift, h, half).astype(BF16)
            keys[part, :] = rolled(roll, 1, source_shift, h, half).astype(BF16)
            values[part, :] = rolled(roll, 2, source_shift, h, half).astype(BF16)
        masks = head_masks(query.shape[1])

        def run(i, kind, key_rows):
            at = pl.multiple_of(kind * half + i * QC, QC)
            cross_bias(source_at, target_at, key_rows.start, at, key_rows.size, bias, half)
            out, sums = attend_chunk(
                keys[key_rows, :],
                values[key_rows, :],
                query[pl.ds(at, QC), :],
                bias[0 : key_rows.size, :],
                masks,
            )
            outs[pl.ds(at, QC), :] = out
            for k, row in enumerate(sums):
                lse[k : k + 1, pl.ds(at, QC)] = row

        def step(i, carry):
            run(i, 0, pl.ds(own_keys, half))
            run(i, 1, pl.ds(0, 2 * half))
            return carry

        lax.fori_loop(0, half // QC, step, 0)
        unroll_into(roll, 0, shift, outs, half)
        for block, o in enumerate((o0, o1, o2, o3)):
            o[...] = unrolled(roll, 0, me, block, rows, half).astype(BF16)


def cross_backward(
    pack, source, target, g0, g1, g2, g3, query, keys, values, lse, outs, even, odd, weights, *rest,
):
    c0, c1, c2, c3, sum_even, sum_odd, total, roll, bias, grads, grad_out = rest[-11:]
    is_dec, me = place_of()

    @pl.when(is_dec == 1)
    def _():
        sentences = source.shape[1]
        source_ends, source_shift, source_big = pack_layout(source, pack, sentences)
        ends, shift, big = pack_layout(target, pack, sentences)
        rows = even.shape[1]
        half = 2 * rows
        own_keys = pl.multiple_of(jnp.where(source_big == big, 0, half), half)
        source_at, target_at = (source_ends, source_shift), (ends, shift)
        for block, g in enumerate((g0, g1, g2, g3)):
            place(roll, 0, me, block, rows, g[...].astype(F32))
        for h in range(2):
            grad_out[h * half : (h + 1) * half, :] = rolled(roll, 0, shift, h, half).astype(BF16)
        masks = head_masks(query.shape[1])
        grads[1] = jnp.zeros(grads.shape[1:], F32)
        grads[2] = jnp.zeros(grads.shape[1:], F32)

        def run(i, kind, key_rows):
            at = pl.ds(pl.multiple_of(kind * half + i * QC, QC), QC)
            cross_bias(source_at, target_at, key_rows.start, at.start, key_rows.size, bias, half)
            dq, dk, dv = attend_back_chunk(
                keys[key_rows, :],
                values[key_rows, :],
                query[at, :],
                grad_out[at, :],
                outs[at, :],
                [lse[k : k + 1, at] for k in range(len(masks))],
                bias[0 : key_rows.size, :],
                masks,
            )
            grads[0, at, :] = dq
            grads[1, key_rows, :] += dk
            grads[2, key_rows, :] += dv

        def step(i, carry):
            run(i, 0, pl.ds(own_keys, half))
            run(i, 1, pl.ds(0, 2 * half))
            return carry

        lax.fori_loop(0, half // QC, step, 0)
        unroll_into(roll, 0, shift, grads.at[0], half)
        unroll_into(roll, 1, source_shift, grads.at[1], half)
        unroll_into(roll, 2, source_shift, grads.at[2], half)
        sums = blocks_of(sum_even, sum_odd)
        query_grads = (c0, c1, c2, c3)
        if pack:
            for old, new in zip(rest, query_grads):
                new[0:pack] = old[0:pack]
        for block, e in enumerate(blocks_of(even, odd)):
            parts = [
                unrolled(roll, slot, me, block, rows, half).astype(BF16) for slot in range(3)
            ]
            query_grads[block][pack] = parts[0]
            sums[block][...] = (nt(parts[1], weights[0]) + nt(parts[2], weights[1])).astype(BF16)
            for slot in range(2):
                grad = tn(parts[slot + 1], e[...])
                before = rest[4] if block == 0 else total
                total[slot] = grad if pack == 0 and block == 0 else before[slot] + grad


def silu_parts(hidden):
    gate = 1.0 / (1.0 + jnp.exp(-hidden))
    return hidden * gate, gate


def split_weights(stacked):
    width = stacked.shape[0] - 2 * stacked.shape[1]
    inner = (stacked.shape[0] - width) // 2
    return pl.ds(0, width), pl.ds(width, inner), pl.ds(width + inner, inner)


def silu_slope(hidden, value, gate):
    return gate + value * (1.0 - gate)


def ffn_forward(normed, shares, out, kept=None, slopes=None):
    _, up, down = split_weights(shares[0])
    for k, share in enumerate(shares):
        hidden = nn(normed, share[up, :])
        value, gate = silu_parts(hidden)
        low = value.astype(BF16)
        if kept is not None:
            kept[k] = low
            slopes[k] = silu_slope(hidden, value, gate)
        part = nn(low, share[down, :])
        out[...] = part if k == 0 else out[...] + part


def ffn_backward(normed, grad, shares, kept, grad_kept, out, slopes=None):
    _, up, down = split_weights(shares[0])
    for k, share in enumerate(shares):
        if slopes is None:
            hidden = nn(normed, share[up, :])
            value, gate = silu_parts(hidden)
            kept[k] = value.astype(BF16)
            slope = silu_slope(hidden, value, gate)
        else:
            slope = slopes[k]
        grad_pre = (nt(grad, share[down, :]) * slope).astype(BF16)
        grad_kept[k] = grad_pre
        part = nt(grad_pre, share[up, :])
        out[...] = part if k == 0 else out[...] + part


def after_self(
    packs, m0, m1, m2, m3, x, w0, w1, w2, w3, gains, biases,
    scaled, inverse, low, scaled_two, inverse_two, *rest,
):
    encoded, work = rest[:packs], rest[packs]
    is_dec, _ = place_of()
    shares = (w0, w1, w2, w3)
    rows = split_weights(shares[0])[0]
    flat = lambda ref: jnp.concatenate([ref[p] for p in range(packs)], axis=0)
    total = flat(x).astype(F32)
    for mixed, share in zip((m0, m1, m2, m3), shares):
        total = total + nn(flat(mixed), share[rows, :])
    first_scaled, first_inverse = center_rows(total)
    scaled[...] = first_scaled
    inverse[...] = first_inverse
    low[...] = (first_scaled * gains[0:1, :] + biases[0:1, :]).astype(BF16)

    @pl.when(is_dec == 0)
    def _():
        ffn_forward(low[...], shares, work)
        again = scaled[...] * gains[0:1, :] + biases[0:1, :]
        second_scaled, second_inverse = center_rows(again + work[...])
        scaled_two[...] = second_scaled
        inverse_two[...] = second_inverse
        result = (second_scaled * gains[1:2, :] + biases[1:2, :]).astype(BF16)
        size = result.shape[0] // packs
        for p in range(packs):
            encoded[p][...] = result[p * size : (p + 1) * size, :]


def cross_queries(packs, low, ka, kb, *queries):
    @pl.when(place_of()[0] == 1)
    def _():
        size = low.shape[0] // packs
        for query, share in zip(queries, blocks_of(ka, kb)):
            result = nn(low[...], share[0]).astype(BF16)
            for p in range(packs):
                query[p] = result[p * size : (p + 1) * size, :]


def after_cross(
    pack, target, m0, m1, m2, m3, scaled, w0, w1, w2, w3, ka, kb,
    gains, biases, cross_gain, cross_shift, cotangent,
    decoded, low, grad_low, hidden, grad_hidden, out_low, g0, g1, g2, g3, grad_two, norms, work, kept, slopes,
):
    is_dec, me = place_of()

    @pl.when(is_dec == 1)
    def _():
        shares, crosses = (w0, w1, w2, w3), blocks_of(ka, kb)
        rows = decoded.shape[0]
        total = scaled[pl.ds(pack * rows, rows), :] * gains[0:1, :] + biases[0:1, :]
        for mixed, share in zip((m0, m1, m2, m3), crosses):
            total = total + nt(mixed[...], share[1])
        second_scaled, second_inverse = center_rows(total)
        kept[...] = second_scaled
        low[...] = (second_scaled * cross_gain[...] + cross_shift[...]).astype(BF16)
        ffn_forward(low[...], shares, work, hidden, slopes)
        second = kept[...] * cross_gain[...] + cross_shift[...]
        third_scaled, third_inverse = center_rows(second + work[...])
        decoded[...] = (third_scaled * gains[1:2, :] + biases[1:2, :]).astype(BF16)
        at = lax.broadcasted_iota(jnp.int32, (rows, 1), 0) + me * rows
        end = pack_layout(target, pack, target.shape[1])[0][-1]
        grad = jnp.where(at < end, cotangent[pack].astype(F32), 0.0)
        grad_third, gain_two, bias_two = norm_back(grad, third_scaled, third_inverse, gains[1:2, :])
        grad_low[...] = grad_third.astype(BF16)
        grad_two[...] = grad_third
        ffn_backward(low[...], grad_low[...], shares, hidden, grad_hidden, work, slopes)
        grad_second, cross_gain_grad, cross_bias_grad = norm_back(
            grad_two[...] + work[...], kept[...], second_inverse, cross_gain[...]
        )
        grad_two[...] = grad_second
        out_low[...] = grad_second.astype(BF16)
        for g, share in zip((g0, g1, g2, g3), crosses):
            g[...] = nn(out_low[...], share[1]).astype(BF16)
        norms[...] = jnp.zeros(norms.shape, F32)
        norms[1:2, :] = gain_two
        norms[3:4, :] = bias_two
        norms[4:5, :] = cross_gain_grad
        norms[5:6, :] = cross_bias_grad


def before_self(
    pack, scaled, inverse, low, gains, w0, w1, w2, w3, ka, kb, grad_encoded, scaled_two, inverse_two,
    c0, c1, c2, c3, grad_two, norms_in, in_low_old, grad_low_old, hidden_old, grad_hidden_old,
    grad_rows, out_low, g0, g1, g2, g3, norms, in_low, grad_low, hidden, grad_hidden, work,
):
    is_dec, _ = place_of()
    size = grad_rows.shape[0]
    own = pl.ds(pack * size, size)
    shares = (w0, w1, w2, w3)
    rows = split_weights(shares[0])[0]

    @pl.when(is_dec == 0)
    def _():
        grad_sum, gain_two, bias_two = norm_back(
            grad_encoded[pl.ds(0, size), :].astype(F32), scaled_two[own, :], inverse_two[own, :], gains[1:2, :]
        )
        in_low[...] = low[own, :]
        grad_low[...] = grad_sum.astype(BF16)
        grad_rows[...] = grad_sum
        ffn_backward(low[own, :], grad_low[...], shares, hidden, grad_hidden, work)
        work[...] += grad_rows[...]
        norms[...] = jnp.zeros(norms.shape, F32)
        norms[1:2, :] = gain_two
        norms[3:4, :] = bias_two

    @pl.when(is_dec == 1)
    def _():
        total = grad_two[...]
        for grad, share in zip((c0, c1, c2, c3), blocks_of(ka, kb)):
            total = total + nt(grad[pack], share[0])
        work[...] = total
        norms[...] = norms_in[...]
        in_low[...] = in_low_old[...]
        grad_low[...] = grad_low_old[...]
        hidden[...] = hidden_old[...]
        grad_hidden[...] = grad_hidden_old[...]

    grad_first, gain_one, bias_one = norm_back(work[...], scaled[own, :], inverse[own, :], gains[0:1, :])
    norms[0:1, :] = gain_one
    norms[2:3, :] = bias_one
    grad_rows[...] = grad_first
    out_low[...] = grad_first.astype(BF16)
    for g, share in zip((g0, g1, g2, g3), shares):
        g[...] = nt(out_low[...], share[rows, :]).astype(BF16)


def pair_sums(even, near, keep, send):
    keep[...] = (even[0].astype(F32) + near[0].astype(F32)).astype(BF16)
    send[...] = (even[1].astype(F32) + near[1].astype(F32)).astype(BF16)


def ffn_grads(packs, *refs):
    inputs, hiddens, grads, grad_hiddens = [refs[i * packs : (i + 1) * packs] for i in range(4)]
    up_even, up_odd, down_even, down_odd = refs[4 * packs :]
    ups, downs = blocks_of(up_even, up_odd), blocks_of(down_even, down_odd)
    for k in range(4):
        downs[k][...] = sum(tn(h[k], g[...]) for h, g in zip(hiddens, grads)).astype(BF16)
        ups[k][...] = sum(tn(x[...], h[k]) for x, h in zip(inputs, grad_hiddens)).astype(BF16)


def projection_grads(packs, *refs):
    is_dec, _ = place_of()
    take = lambda count: [refs.pop(0) for _ in range(count)]
    refs = list(refs)
    mixes, crosses = take(4), [take(4) for _ in range(packs)]
    queries = take(4)
    outs, cross_outs, norms = take(packs), take(packs), take(packs)
    low, received = take(2)
    size = outs[0].shape[0]
    targets = blocks_of(*take(2))
    width = mixes[0][0].shape[1]
    part = lambda k: pl.ds(k * width, width)
    sums = sum(n[...] for n in norms)
    row = lax.broadcasted_iota(jnp.int32, sums.shape, 0)
    from_cross = (is_dec == 0) & ((row == 4) | (row == 5))
    sums = jnp.where(from_cross, received[pl.ds(received.shape[0] - sums.shape[0], sums.shape[0]), :].astype(F32), sums).astype(BF16)
    for k in range(4):
        targets[k][part(0), :] = sum(
            tn(mixes[k][p], g[...]) for p, g in enumerate(outs)
        ).astype(BF16)
        targets[k][pl.ds(3 * width, sums.shape[0]), :] = sums

    @pl.when(is_dec == 1)
    def _():
        for k in range(4):
            targets[k][part(1), :] = sum(
                tn(queries[k][p], low[pl.ds(p * size, size), :]) for p in range(packs)
            ).astype(BF16)
            targets[k][part(2), :] = sum(
                tn(c[k][...], g[...]) for g, c in zip(cross_outs, crosses)
            ).astype(BF16)


def call(clock, kernel, scalars, outs, scratch, micros, *operands, aliases=(), far_outs=(), any_ins=()):
    space = pl.BlockSpec(memory_space=pltpu.VMEM)
    operands = after(operands, *clock)
    operands = [
        pltpu.with_memory_space_constraint(x, pltpu.HBM if i in any_ins else pltpu.VMEM)
        for i, x in enumerate(operands)
    ]
    results = pl.pallas_call(
        kernel,
        out_shape=[
            pltpu.HBM(shape, kind) if i in far_outs else pltpu.VMEM(shape, kind)
            for i, (shape, kind) in enumerate(outs)
        ],
        in_specs=[pl.BlockSpec(memory_space=pltpu.SMEM)] * len(scalars) + [pl.BlockSpec(memory_space=pl.ANY) if i in any_ins else space for i in range(len(operands))],
        out_specs=[space] * len(outs),
        scratch_shapes=[pltpu.VMEM(*item) if isinstance(item, tuple) else item for item in scratch],
        input_output_aliases={len(scalars) + len(operands) + a: b for a, b in aliases},
        compiler_params=pltpu.CompilerParams(vmem_limit_bytes=SCOPED),
        cost_estimate=pl.CostEstimate(
            flops=int(micros * COST), bytes_accessed=1, transcendentals=0
        ),
    )(*scalars, *operands)
    clock[:] = [results[0]]
    return results


def body(
    embeddings, src_len, tgt_len, attn_in, attn_out, ffn_in, ffn_out, cross_a, cross_b,
    norm_gain, norm_bias, cross_gain, cross_bias_vec, cotangent,
):
    is_dec = lax.axis_index("section") == 1
    x_all = embeddings[0]
    packs, rows, features = x_all.shape
    total_rows = rows * lax.axis_size("mp")
    half = total_rows // 2
    width = attn_in.shape[3]
    hidden = ffn_in.shape[2]
    gains, biases = norm_gain[0], norm_bias[0]
    cgain, cbias = cross_gain[None, :], cross_bias_vec[None, :]
    lens = (src_len, tgt_len)
    every = range(packs)
    w_self = attn_in[0]
    share = jnp.concatenate([attn_out[0], ffn_in[0], ffn_out[0]], axis=0)
    cross_share = jnp.stack([cross_a[0], cross_b[0]])

    clock = []
    x_far = hop(x_all, 2)
    xs = (x_all, hop(x_all, 1), x_far, hop(x_far, 1))
    cross_share = after(cross_share, x_far)
    memory_weights = section_send(cross_share, 0)
    share_far = hop(after(share, x_far), 2)
    share_near = hop(after(share, xs[3]), 1)

    pair = lambda *tail: [((2,) + tail, BF16)] * 2
    saved_spec = [((total_rows, width), BF16)] * 3 + [((8, total_rows), F32), ((total_rows, width), F32)]
    roll_spec = ((3, 2 * total_rows, width), F32)
    back_spec = [((3, total_rows, width), F32), ((total_rows, width), BF16)]
    full = (rows, features)
    column = ((rows, 1), F32)
    hid_spec = ((4, rows, hidden), BF16)
    self_scratch = [roll_spec, ((half, QC), F32)]
    cross_scratch = [roll_spec, ((total_rows, QC), F32)]
    part = functools.partial

    blocks = [((rows, width), BF16)] * 4
    blocks = [((rows, width), BF16)] * 4
    stacked = lambda outs: [jnp.stack(block) for block in zip(*outs)]
    saved, mixes = [], []
    for p in every:
        if p == 1:
            clock += [share_near, memory_weights]
        out = call(
            clock, part(self_forward, p), lens, blocks + saved_spec, self_scratch, 5.0, *xs, w_self,
            far_outs=range(4, 9),
        )
        mixes.append(out[:4])
        saved.append(out[4:])
    mixes = exchange(stacked(mixes))
    share_far, cross_share = after((share_far, cross_share), clock[0], mixes[1])
    shares = (share, share_near, share_far, hop(share_far, 1))
    cross_far = hop(cross_share, 2)

    tall = (packs * rows, features)
    tall_column = ((packs * rows, 1), F32)
    out = call(
        clock, part(after_self, packs), (),
        [(tall, F32), tall_column, (tall, BF16), (tall, F32), tall_column] + [(full, BF16)] * packs,
        [(tall, F32)], 7.0,
        *mixes, x_all, *shares, gains, biases,
    )
    firsts, encoded = out[:5], out[5:]
    arrived = [section_send(e, 0) for e in encoded]
    cross_even = jnp.stack([cross_share, cross_far])
    cross_shares = (cross_even, hop(cross_even, 1))
    queries = exchange(call(
        clock, part(cross_queries, packs), (), [((packs, rows, width), BF16)] * 4, [], 2.0,
        firsts[2], *cross_shares,
    ))
    memory_far = [hop(x, 2) for x in arrived]

    cross_saved, cross_mixes, memories = [], [], []
    clock += arrived[1:]
    for p in every:
        even = jnp.stack([arrived[p], after(memory_far[p], *clock) if p else memory_far[p]])
        memories.append((even, hop(even, 1)))
        out = call(
            clock, part(cross_forward, p), lens, blocks + saved_spec, cross_scratch, 6.0,
            *queries, *memories[p], memory_weights,
        )
        cross_mixes.append(exchange(out[:4]))
        cross_saved.append(out[4:])

    add = lambda a, b: (a.astype(F32) + b.astype(F32)).astype(BF16)
    decs, cross_grads, nears, fars, encoded_grads = [], [], [], [], []

    def run_after(p):
        out = call(
            clock, part(after_cross, p), (tgt_len,),
            [(full, BF16)] * 3 + [hid_spec] * 2 + [(full, BF16)] + blocks + [(full, F32), ((16, features), F32)],
            [(full, F32), (full, F32), ((4, rows, hidden), F32)], 14.0,
            *cross_mixes[p], firsts[0], *shares, *cross_shares, gains, biases, cgain, cbias, cotangent,
        )
        decs.append(out)
        cross_grads.append(exchange(out[6:10]))

    def run_cross(p, carried):
        out = call(
            clock, part(cross_backward, p), lens,
            [((packs, rows, width), BF16)] * 4 + pair(rows, features) + [((2, width, features), F32)],
            cross_scratch + back_spec, 14.0,
            *cross_grads[p], *cross_saved[p], *memories[p], memory_weights, *carried,
            aliases=((-5, 0), (-4, 1), (-3, 2), (-2, 3), (-1, 6)) if p else (),
        )
        nears.append(hop(out[5], 1))
        fars.append(hop(add(out[4][1], nears[-1][1]), 2))
        sent = add(add(out[4][0], nears[-1][0]), fars[-1])
        if p == packs - 1:
            sent = jnp.concatenate([sent, sum(d[11] for d in decs).astype(BF16)])
        encoded_grads.append(section_send(sent, 1))
        return (*out[:4], out[6])

    carried = ()
    for p in every:
        run_after(p)
        if p == packs - 2:
            carried = run_cross(0, carried)
    for p in range(1 if packs > 1 else 0, packs):
        clock += nears[:1] if p == 1 else fars[:1]
        carried = run_cross(p, carried)
    query_grads = exchange(after(carried[:4], fars[-1]))
    memory_sent = carried[4].astype(BF16).reshape(2 * width, features)

    encs, self_grads = [], []
    for p in every:
        out = call(
            clock, part(before_self, p), (),
            [(full, F32), (full, BF16)] + blocks + [((16, features), F32)]
            + [(full, BF16), (full, BF16), hid_spec, hid_spec],
            [(full, F32)], 4.0,
            firsts[0], firsts[1], firsts[2], gains, *shares, *cross_shares, encoded_grads[p],
            firsts[3], firsts[4], *query_grads, decs[p][10], decs[p][11],
            *decs[p][1:5], aliases=((-4, 7), (-3, 8), (-2, 9), (-1, 10)),
        )
        encs.append(out)
        if p == 0:
            memory_sent = section_send(after(memory_sent, out[0]), 1)
        self_grads.append(out[2:6])
        if p == packs - 2:
            early = exchange(stacked(self_grads))
    clock += early
    self_grads = [early] * (packs - 1) + [exchange(stacked(self_grads[-1:]))]
    up_even, up_odd, down_even, down_odd = call(
        clock, part(ffn_grads, packs), (), pair(features, hidden) + pair(hidden, features), [], 4.0,
        *[e[7] for e in encs], *[e[9] for e in encs], *[e[8] for e in encs], *[e[10] for e in encs],
    )
    down_near, up_near = hop(down_odd, 1), hop(up_odd, 1)

    def merged(even, near):
        return call([], pair_sums, (), [(even.shape[1:], BF16)] * 2, [], 0.5, even, near)

    down_keep, down_send = merged(down_even, down_near)
    up_keep, up_send = merged(up_even, up_near)
    down_far = hop(down_send, 2)
    down_sum = add(down_keep, down_far)
    up_far = hop(after(up_send, down_far), 2)
    up_sum = add(up_keep, up_far)
    chained = []
    down_grad = chain_sum(down_sum, chained)
    clock += [down_near, up_send]
    carried, row_sums = (), []
    for p in every:
        if p == 1:
            rest_rows = 3 * width + 16
            out_even, out_odd = call(
                clock, part(projection_grads, packs), (), pair(rest_rows, features), [], 2.0,
                *mixes, *sum(cross_mixes, []), *query_grads,
                *[e[1] for e in encs], *[d[5] for d in decs], *[e[6] for e in encs], firsts[2], encoded_grads[-1],
            )
            out_near = hop(out_odd, 1)
            out_keep, out_send = merged(out_even, out_near)
            out_far = hop(after(out_send, up_far), 2)
        if p == packs - 1:
            clock += [down_far, up_far, memory_sent]
        out = call(
            clock, part(self_backward, p, p if p < packs - 1 else 0), lens,
            pair(rows, features) + [((3, features, width), F32)],
            self_scratch + back_spec + saved_spec + [((4,) + full, BF16), ((4, rows, width), BF16), pltpu.SemaphoreType.DMA((13,))], 7.0,
            *self_grads[p], *saved[p], *xs, w_self, *carried, aliases=((-1, 2),) if p else (), any_ins=range(13),
        )
        carried = out[2:]
        row_sums.append(out[:2])
    row_even, row_odd = stacked(row_sums)
    row_near = hop(row_odd, 1)
    row_far = hop(add(row_even[:, 1], row_near[:, 1]), 2)
    partial = jnp.stack([e[0] for e in encs]) + row_even[:, 0].astype(F32) + row_near[:, 0].astype(F32)
    input_grads = lax.optimization_barrier(partial) + row_far.astype(F32)
    out_sum = add(out_keep, out_far)
    norm_at = 3 * width
    cross_sum = jnp.where(is_dec, out_sum[width:norm_at], memory_sent)
    out_sum = jnp.concatenate([out_sum[:width], cross_sum, out_sum[norm_at:]])
    up_grad = chain_sum(up_sum, chained)
    out_grad = chain_sum(out_sum, chained)
    qkv_grad = chain_sum(carried[0].astype(BF16), chained)
    norms = out_grad[norm_at:].astype(F32)

    picks = after([(decs[p][0], encoded[p]) for p in every], *clock)
    layer_rows = jnp.stack([jnp.where(is_dec, a, b) for a, b in picks])
    wide = lambda value: value.astype(F32)[None]
    qkv_grad = after(qkv_grad, input_grads)
    return (
        layer_rows[None],
        input_grads[None],
        wide(qkv_grad),
        wide(out_grad[:width]),
        wide(up_grad),
        wide(down_grad),
        wide(out_grad[width : 2 * width].T),
        wide(out_grad[2 * width : norm_at].T),
        norms[0:2][None],
        norms[2:4][None],
        norms[4],
        norms[5],
    )


def solution(mesh):
    return jax.shard_map(
        body,
        mesh=mesh,
        in_specs=(
            P("section", "dp", "mp", None),
            P("dp", None),
            P("dp", None),
            P("section", None, None, "mp"),
            P("section", "mp", None),
            P("section", None, "mp"),
            P("section", "mp", None),
            P("section", None, "mp"),
            P("section", None, "mp"),
            P("section", None, None),
            P("section", None, None),
            P(),
            P(),
            P("dp", "mp", None),
        ),
        out_specs=(
            P("section", "dp", "mp", None),
            P("section", "dp", "mp", None),
            P("section", None, None, "mp"),
            P("section", "mp", None),
            P("section", None, "mp"),
            P("section", "mp", None),
            P("section", None, "mp"),
            P("section", None, "mp"),
            P("section", None, None),
            P("section", None, None),
            P(),
            P(),
        ),
        check_vma=False,
    )
```
